32 devices in a mesh: grp: 8 (over z, core), tp: 4 (over y, x).
Axes of the slice: x: 2, y: 2, z: 4, core: 2. Of those that a mesh axis runs over, the one named last changes fastest.
Arguments:
- query: bfloat16 [64, 128, 576], P(('grp', 'tp')), parts along dimension 0, may hold values from -50 to 50
- cache: bfloat16 [64, 1536, 576], P(('grp', 'tp')), parts along dimension 0, may hold values from -6 to 6
- scales: float32 [576], replicated, may hold values from 0.5 to 2
- lengths: int32 [64], P(('grp', 'tp')), parts along dimension 0, may hold values from 2 to 1536, as said below
- value_up: bfloat16 [128, 512, 128], P('tp'), may hold values from -0.25 to 0.25
Outputs:
- head_values: bfloat16 [64, 16384], P(('grp', 'tp')), parts along dimension 0
The draws below stay inside these ranges and needn't reach their ends.
There are 8 independent parts, one for each index of `grp`. The reference program is written for one: setup_inputs(seed, part) draws one part's arguments, and reference() takes and returns one part's arrays. A program takes and returns all parts, laid end to end along the dimension named above; an argument that names none is the same for every part. Nothing has to cross between parts.
Inputs may be any that keep to these rules, and one draw needn't show every extreme that they name: `lengths`: each request's number of cached positions, counted from position 0; in every draw some request has exactly 1536.
All inputs are finite; a program needn't handle non-finite values.
Results may differ from the reference program's by a relative error of at most 0.0085.
Values may be sent and summed in bfloat16 or wider, within the bound.
No kernel may reach another device: no remote copies, remote signals or barrier semaphores. Data moves between devices by JAX's collectives and lax.ppermute only.
A program may use at most 64 MiB of HBM per device.

```python
import math
import jax
import jax.numpy as jnp
from jax import lax

HEADS = 128
KV_RANK = 512
V_DIM = 128
MAXLEN = 1536
LATENT = 576
REQS = 8


def draw_cache(key, part):
    keys = jax.random.split(jax.random.fold_in(key, 1), 1)
    base = jnp.clip(jax.random.normal(keys[0], (REQS, MAXLEN, LATENT), jnp.float32), -6.0, 6.0)
    return base.astype(jnp.bfloat16)


def draw_query(key, part):
    keys = jax.random.split(jax.random.fold_in(key, 2), 1)
    base = jnp.clip(jax.random.normal(keys[0], (REQS, HEADS, LATENT), jnp.float32), -6.0, 6.0)
    return base.astype(jnp.bfloat16)


def draw_lengths(key, part):
    keys = jax.random.split(jax.random.fold_in(key, 3), 3)
    first_draw = jax.random.randint(keys[0], (REQS,), 2, MAXLEN + 1)
    second_draw = jax.random.randint(keys[1], (REQS,), 1, MAXLEN + 1)
    drawn = jnp.maximum(first_draw * second_draw // MAXLEN, 2)
    forced = jax.random.randint(keys[2], (), 0, REQS)
    return jnp.where(jnp.arange(REQS) == forced, MAXLEN, drawn).astype(jnp.int32)


def levels(key, shape, cuts, low, high):
    def one(axis_at, parts):
        steps = jax.random.uniform(jax.random.fold_in(jax.random.fold_in(key, 6), axis_at), (parts,), jnp.float32, low / len(cuts), high / len(cuts))
        return jnp.repeat(jnp.exp(steps), shape[axis_at] // parts).reshape((-1,) + (1,) * (len(shape) - axis_at - 1))

    gain = one(*cuts[0])
    for cut in cuts[1:]:
        gain = gain * one(*cut)
    return gain


def bell_draw(own_key, dims, scale, bound, cuts=(), kind=jnp.bfloat16):
    values = scale * jax.random.normal(own_key, dims, jnp.float32)
    if cuts:
        values = values * levels(own_key, dims, cuts, -0.22, 0.18)
    return jnp.clip(values, -bound, bound).astype(kind)


def setup_inputs(seed: int = 0, part: int = 0) -> dict:
    arg_keys = jax.random.split(jax.random.key(seed), 6)
    own_keys = jax.random.split(jax.random.fold_in(arg_keys[5], part), 6)
    return {
        "query": draw_query(jax.random.fold_in(jax.random.fold_in(arg_keys[5], part), 71), part),
        "cache": draw_cache(jax.random.fold_in(jax.random.fold_in(arg_keys[5], part), 71), part),
        "scales": jnp.clip(jnp.exp(jax.random.uniform(arg_keys[2], (LATENT,), jnp.float32, math.log(0.5), math.log(2.0))), 0.5, 2.0),
        "lengths": draw_lengths(jax.random.fold_in(jax.random.fold_in(arg_keys[5], part), 71), part),
        "value_up": bell_draw(arg_keys[4], (HEADS, KV_RANK, V_DIM), KV_RANK ** -0.5, 0.25, ((0, 4),)),
    }


SOFTMAX_SCALE = (1.0 + 0.1 * math.log(40.0)) ** 2 / math.sqrt(192.0)

def reference(query, cache, scales, lengths, value_up):
    scaled = (query.astype(jnp.float32) * scales).astype(jnp.bfloat16)
    positions = jnp.arange(MAXLEN, dtype=jnp.int32)

    def one_request(items):
        query_rows, cache_rows, length = items
        scores = jnp.dot(query_rows, cache_rows.T, preferred_element_type=jnp.float32) * SOFTMAX_SCALE
        visible = positions[None, :] < length
        scores = jnp.where(visible, scores, -jnp.inf)
        highest = lax.optimization_barrier(jnp.max(scores, axis=1, keepdims=True))
        weights = jnp.exp(scores - highest)
        summed = lax.optimization_barrier(jnp.sum(weights, axis=1, keepdims=True))
        probabilities = weights.astype(jnp.bfloat16)
        mixture = jnp.dot(probabilities, cache_rows[:, :KV_RANK], preferred_element_type=jnp.float32)
        return (mixture / summed * scales[:KV_RANK]).astype(jnp.bfloat16)
    latent = lax.map(one_request, (scaled, cache, lengths))
    projected = jnp.einsum('bhc,hcv->bhv', latent.astype(jnp.float32), value_up.astype(jnp.float32), precision=lax.Precision.HIGHEST)
    return projected.astype(jnp.bfloat16).reshape(REQS, HEADS * V_DIM)
```

```python
import math

import jax
import jax.numpy as jnp
from jax import lax
from jax.experimental import pallas as pl
from jax.experimental.pallas import tpu as pltpu
from jax.sharding import PartitionSpec as P

ROPE_DIM = 64
SOFTMAX_SCALE = (1.0 + 0.1 * math.log(40.0)) ** 2 / math.sqrt(192.0)
BLOCK = 512
LANES = 128


def attend_kernel(lengths, query, scales, cache, out, keys, sems):
    requests, channels, heads = query.shape
    rank = out.shape[3]
    owners, local_heads = out.shape[0], out.shape[2]
    cache_len = cache.shape[2]
    block = min(BLOCK, cache_len)
    blocks = cache_len // block

    def fetch(r, b):
        span = pl.ds(b * block, block)
        return pltpu.make_async_copy(cache.at[r, :, span], keys.at[r, :, span], sems.at[r, b])

    for r in range(requests):
        for b in range(blocks):
            @pl.when(b * block < lengths[r])
            def _():
                fetch(r, b).start()

    scale_row = scales[...]

    def request(r, live):
        scaled = (query[r].astype(jnp.float32).T * scale_row).astype(jnp.bfloat16)
        parts = []
        for b in range(live):
            fetch(r, b).wait()
            part = jnp.dot(
                scaled, keys[r, :, b * block:(b + 1) * block],
                preferred_element_type=jnp.float32,
            )
            if b == live - 1:
                place = b * block + lax.broadcasted_iota(jnp.int32, part.shape, 1)
                part = jnp.where(place < lengths[r], part, -jnp.inf)
            parts.append(part)
        top = jnp.max(parts[0], axis=1, keepdims=True)
        for part in parts[1:]:
            top = jnp.maximum(top, jnp.max(part, axis=1, keepdims=True))
        total = jnp.zeros_like(top)
        mixture = jnp.zeros((heads, rank), jnp.float32)
        for b, part in enumerate(parts):
            weights = jnp.exp((part - top) * SOFTMAX_SCALE)
            total += jnp.sum(weights, axis=1, keepdims=True)
            mixture += lax.dot_general(
                weights.astype(jnp.bfloat16), keys[r, :rank, b * block:(b + 1) * block],
                (((1,), (1,)), ((), ())), preferred_element_type=jnp.float32,
            )
        latent = (mixture / total * scale_row[:, :rank]).astype(jnp.bfloat16)
        for d in range(owners):
            out[d, r] = latent[d * local_heads:(d + 1) * local_heads]

    for r in range(requests):
        for live in range(1, blocks + 1):
            @pl.when((lengths[r] > (live - 1) * block) & (lengths[r] <= live * block))
            def _():
                request(r, live)


def attend(query, cache, scales, lengths, owners):
    requests, heads, channels = query.shape
    cache_len = cache.shape[1]
    rank = channels - ROPE_DIM
    return pl.pallas_call(
        attend_kernel,
        out_shape=jax.ShapeDtypeStruct((owners, requests, heads // owners, rank), jnp.bfloat16),
        in_specs=[
            pl.BlockSpec(memory_space=pltpu.SMEM),
            pl.BlockSpec(memory_space=pltpu.VMEM),
            pl.BlockSpec(memory_space=pltpu.VMEM),
            pl.BlockSpec(memory_space=pltpu.HBM),
        ],
        out_specs=pl.BlockSpec(memory_space=pltpu.VMEM),
        scratch_shapes=[
            pltpu.VMEM((requests, channels, cache_len), jnp.bfloat16),
            pltpu.SemaphoreType.DMA((requests, cache_len // min(BLOCK, cache_len))),
        ],
        compiler_params=pltpu.CompilerParams(vmem_limit_bytes=24 * 2**20),
        cost_estimate=pl.CostEstimate(
            flops=4 * requests * heads * channels * cache_len,
            bytes_accessed=2 * requests * channels * cache_len,
            transcendentals=requests * heads * cache_len,
        ),
        name="attend",
    )(lengths, jnp.swapaxes(query, 1, 2), scales.reshape(1, channels), jnp.swapaxes(cache, 1, 2))


def project_kernel(latent, maps, out, rows):
    owners, requests, local_heads, rank = latent.shape
    width = maps.shape[2]
    batch = owners * requests
    for b in range(batch):
        for k in range(rank // LANES):
            rows[k, b * local_heads:(b + 1) * local_heads] = latent[
                b // requests, b % requests, :, k * LANES:(k + 1) * LANES
            ].astype(jnp.float32)
    for h in range(0, local_heads, 2):
        pair = jnp.concatenate(
            [
                jnp.concatenate(
                    [rows[k, pl.ds(h + i, batch, stride=local_heads), :] for i in range(2)], axis=0
                ).astype(jnp.bfloat16)
                for k in range(rank // LANES)
            ],
            axis=1,
        )
        both = jnp.concatenate([maps[h], maps[h + 1]], axis=1)
        values = jnp.dot(pair, both, preferred_element_type=jnp.float32)
        for i in range(2):
            mine = values[i * batch:(i + 1) * batch, i * width:(i + 1) * width]
            for d in range(owners):
                out[d, h + i] = mine[d * requests:(d + 1) * requests].astype(jnp.bfloat16)


def project(latent, maps):
    owners, requests, local_heads, rank = latent.shape
    width = maps.shape[2]
    return pl.pallas_call(
        project_kernel,
        out_shape=jax.ShapeDtypeStruct((owners, local_heads, requests, width), jnp.bfloat16),
        in_specs=[pl.BlockSpec(memory_space=pltpu.VMEM)] * 2,
        out_specs=pl.BlockSpec(memory_space=pltpu.VMEM),
        scratch_shapes=[pltpu.VMEM((rank // LANES, owners * requests * local_heads, LANES), jnp.float32)],
        compiler_params=pltpu.CompilerParams(vmem_limit_bytes=24 * 2**20),
        cost_estimate=pl.CostEstimate(
            flops=2 * owners * requests * local_heads * rank * width,
            bytes_accessed=2 * local_heads * rank * width,
            transcendentals=0,
        ),
        name="project",
    )(latent, maps)


def on_device(query, cache, scales, lengths, value_up):
    owners = lax.axis_size("tp")
    latent = attend(query, cache, scales, lengths, owners)
    owned = lax.all_to_all(latent, "tp", split_axis=0, concat_axis=0, tiled=True)
    projected = project(owned, value_up)
    returned = lax.all_to_all(projected, "tp", split_axis=0, concat_axis=0, tiled=True)
    _, local_heads, requests, width = returned.shape
    returned = returned.reshape(owners * local_heads, requests, width)
    return jnp.swapaxes(returned, 0, 1).reshape(requests, owners * local_heads * width)


def solution(mesh):
    in_specs = (
        P(("grp", "tp"), None, None),
        P(("grp", "tp"), None, None),
        P(),
        P(("grp", "tp")),
        P("tp", None, None),
    )
    out_specs = P(("grp", "tp"), None)
    return jax.shard_map(
        on_device, mesh=mesh, in_specs=in_specs, out_specs=out_specs, check_vma=False
    )
```

```python
import math

import jax
import jax.numpy as jnp
from jax import lax
from jax.experimental import pallas as pl
from jax.experimental.pallas import tpu as pltpu
from jax.sharding import PartitionSpec as P

ROPE_DIM = 64
SOFTMAX_SCALE = (1.0 + 0.1 * math.log(40.0)) ** 2 / math.sqrt(192.0)
BLOCK = 512
LANES = 128


def attend_kernel(lengths_hbm, query_hbm, scales_hbm, cache, out, lengths, query, scales, keys, sems, small_sems):
    requests, channels, heads = query.shape
    rank = out.shape[3]
    owners, local_heads = out.shape[0], out.shape[2]
    cache_len = cache.shape[2]
    block = min(BLOCK, cache_len)
    blocks = cache_len // block

    def fetch(r, b):
        span = pl.ds(b * block, block)
        return pltpu.make_async_copy(cache.at[r, :, span], keys.at[r, :, span], sems.at[r, b])

    small = [
        pltpu.make_async_copy(source, target, small_sems.at[i])
        for i, (source, target) in enumerate(
            [(lengths_hbm, lengths), (query_hbm, query), (scales_hbm, scales)]
        )
    ]
    for copy in small:
        copy.start()
    fetch(0, 0).start()
    small[0].wait()
    for r in range(requests):
        for b in range(blocks):
            if (r, b) != (0, 0):
                @pl.when(b * block < lengths[r])
                def _():
                    fetch(r, b).start()
    small[1].wait()
    small[2].wait()

    scale_row = scales[...].reshape(1, channels)

    def request(r, live):
        scaled = (query[r].astype(jnp.float32).T * scale_row).astype(jnp.bfloat16)
        parts = []
        for b in range(live):
            fetch(r, b).wait()
            part = jnp.dot(
                scaled, keys[r, :, b * block:(b + 1) * block],
                preferred_element_type=jnp.float32,
            )
            if b == live - 1:
                place = b * block + lax.broadcasted_iota(jnp.int32, part.shape, 1)
                part = jnp.where(place < lengths[r], part, -jnp.inf)
            parts.append(part)
        top = jnp.max(parts[0], axis=1, keepdims=True)
        for part in parts[1:]:
            top = jnp.maximum(top, jnp.max(part, axis=1, keepdims=True))
        total = jnp.zeros_like(top)
        mixture = jnp.zeros((heads, rank), jnp.float32)
        for b, part in enumerate(parts):
            weights = jnp.exp((part - top) * SOFTMAX_SCALE)
            total += jnp.sum(weights, axis=1, keepdims=True)
            mixture += lax.dot_general(
                weights.astype(jnp.bfloat16), keys[r, :rank, b * block:(b + 1) * block],
                (((1,), (1,)), ((), ())), preferred_element_type=jnp.float32,
            )
        latent = (mixture / total * scale_row[:, :rank]).astype(jnp.bfloat16)
        for d in range(owners):
            out[d, r] = latent[d * local_heads:(d + 1) * local_heads]

    for r in range(requests):
        for live in range(1, blocks + 1):
            @pl.when((lengths[r] > (live - 1) * block) & (lengths[r] <= live * block))
            def _():
                request(r, live)


def attend(query, cache, scales, lengths, owners):
    requests, heads, channels = query.shape
    cache_len = cache.shape[1]
    rank = channels - ROPE_DIM
    return pl.pallas_call(
        attend_kernel,
        out_shape=jax.ShapeDtypeStruct((owners, requests, heads // owners, rank), jnp.bfloat16),
        in_specs=[pl.BlockSpec(memory_space=pl.ANY)] * 4,
        out_specs=pl.BlockSpec(memory_space=pltpu.VMEM),
        scratch_shapes=[
            pltpu.SMEM((requests,), jnp.int32),
            pltpu.VMEM((requests, channels, heads), jnp.bfloat16),
            pltpu.VMEM((channels,), jnp.float32),
            pltpu.VMEM((requests, channels, cache_len), jnp.bfloat16),
            pltpu.SemaphoreType.DMA((requests, cache_len // min(BLOCK, cache_len))),
            pltpu.SemaphoreType.DMA((3,)),
        ],
        compiler_params=pltpu.CompilerParams(vmem_limit_bytes=24 * 2**20),
        cost_estimate=pl.CostEstimate(
            flops=4 * requests * heads * channels * cache_len,
            bytes_accessed=2 * requests * channels * cache_len,
            transcendentals=requests * heads * cache_len,
        ),
        name="attend",
    )(*(pltpu.with_memory_space_constraint(x, pltpu.HBM) for x in (lengths, jnp.swapaxes(query, 1, 2), scales, jnp.swapaxes(cache, 1, 2))))


def project_kernel(latent, maps, out, rows):
    owners, requests, local_heads, rank = latent.shape
    width = maps.shape[2]
    batch = owners * requests
    for b in range(batch):
        for k in range(rank // LANES):
            rows[k, b * local_heads:(b + 1) * local_heads] = latent[
                b // requests, b % requests, :, k * LANES:(k + 1) * LANES
            ].astype(jnp.float32)
    for h in range(0, local_heads, 2):
        pair = jnp.concatenate(
            [
                jnp.concatenate(
                    [rows[k, pl.ds(h + i, batch, stride=local_heads), :] for i in range(2)], axis=0
                ).astype(jnp.bfloat16)
                for k in range(rank // LANES)
            ],
            axis=1,
        )
        both = jnp.concatenate([maps[h], maps[h + 1]], axis=1)
        values = jnp.dot(pair, both, preferred_element_type=jnp.float32)
        for i in range(2):
            mine = values[i * batch:(i + 1) * batch, i * width:(i + 1) * width]
            for d in range(owners):
                out[d, h + i] = mine[d * requests:(d + 1) * requests].astype(jnp.bfloat16)


def project(latent, maps):
    owners, requests, local_heads, rank = latent.shape
    width = maps.shape[2]
    return pl.pallas_call(
        project_kernel,
        out_shape=jax.ShapeDtypeStruct((owners, local_heads, requests, width), jnp.bfloat16),
        in_specs=[pl.BlockSpec(memory_space=pltpu.VMEM)] * 2,
        out_specs=pl.BlockSpec(memory_space=pltpu.VMEM),
        scratch_shapes=[pltpu.VMEM((rank // LANES, owners * requests * local_heads, LANES), jnp.float32)],
        compiler_params=pltpu.CompilerParams(vmem_limit_bytes=24 * 2**20),
        cost_estimate=pl.CostEstimate(
            flops=2 * owners * requests * local_heads * rank * width,
            bytes_accessed=2 * local_heads * rank * width,
            transcendentals=0,
        ),
        name="project",
    )(latent, maps)


def on_device(query, cache, scales, lengths, value_up):
    owners = lax.axis_size("tp")
    latent = attend(query, cache, scales, lengths, owners)
    owned = lax.all_to_all(latent, "tp", split_axis=0, concat_axis=0, tiled=True)
    projected = project(owned, value_up)
    returned = lax.all_to_all(projected, "tp", split_axis=0, concat_axis=0, tiled=True)
    _, local_heads, requests, width = returned.shape
    returned = returned.reshape(owners * local_heads, requests, width)
    return jnp.swapaxes(returned, 0, 1).reshape(requests, owners * local_heads * width)


def solution(mesh):
    in_specs = (
        P(("grp", "tp"), None, None),
        P(("grp", "tp"), None, None),
        P(),
        P(("grp", "tp")),
        P("tp", None, None),
    )
    out_specs = P(("grp", "tp"), None)
    return jax.shard_map(
        on_device, mesh=mesh, in_specs=in_specs, out_specs=out_specs, check_vma=False
    )
```

```python
import functools
import math

import jax
import jax.numpy as jnp
from jax import lax
from jax.experimental import pallas as pl
from jax.experimental.pallas import tpu as pltpu
from jax.sharding import PartitionSpec as P

ROPE_DIM = 64
SOFTMAX_SCALE = (1.0 + 0.1 * math.log(40.0)) ** 2 / math.sqrt(192.0)
BLOCK = 512
LANES = 128


def attend_kernel(owners, lengths_hbm, query_hbm, scales_hbm, cache, *refs):
    outs, (latents, lengths, query, scales, keys, sems, small_sems) = refs[:owners], refs[owners:]
    requests, channels, heads = query.shape
    local_heads, rank = latents.shape[2:]
    me = lax.axis_index("tp")
    cache_len = cache.shape[2]
    block = min(BLOCK, cache_len)
    blocks = cache_len // block

    def fetch(r, b):
        span = pl.ds(b * block, block)
        return pltpu.make_async_copy(cache.at[r, :, span], keys.at[r, :, span], sems.at[r, b])

    small = [
        pltpu.make_async_copy(source, target, small_sems.at[i])
        for i, (source, target) in enumerate(
            [(lengths_hbm, lengths), (query_hbm, query), (scales_hbm, scales)]
        )
    ]
    for copy in small:
        copy.start()
    fetch(0, 0).start()
    small[0].wait()
    for r in range(requests):
        for b in range(blocks):
            if (r, b) != (0, 0):
                @pl.when(b * block < lengths[r])
                def _():
                    fetch(r, b).start()
    small[1].wait()
    small[2].wait()

    scale_row = scales[...].reshape(1, channels)

    def request(r, live):
        scaled = (query[r].astype(jnp.float32).T * scale_row).astype(jnp.bfloat16)
        parts = []
        for b in range(live):
            fetch(r, b).wait()
            part = jnp.dot(
                scaled, keys[r, :, b * block:(b + 1) * block],
                preferred_element_type=jnp.float32,
            )
            if b == live - 1:
                place = b * block + lax.broadcasted_iota(jnp.int32, part.shape, 1)
                part = jnp.where(place < lengths[r], part, -jnp.inf)
            parts.append(part)
        top = jnp.max(parts[0], axis=1, keepdims=True)
        for part in parts[1:]:
            top = jnp.maximum(top, jnp.max(part, axis=1, keepdims=True))
        total = jnp.zeros_like(top)
        mixture = jnp.zeros((heads, rank), jnp.float32)
        for b, part in enumerate(parts):
            weights = jnp.exp((part - top) * SOFTMAX_SCALE)
            total += jnp.sum(weights, axis=1, keepdims=True)
            mixture += lax.dot_general(
                weights.astype(jnp.bfloat16), keys[r, :rank, b * block:(b + 1) * block],
                (((1,), (1,)), ((), ())), preferred_element_type=jnp.float32,
            )
        latent = (mixture / total * scale_row[:, :rank]).astype(jnp.bfloat16)
        for d in range(owners):
            latents[d, r] = latent[d * local_heads:(d + 1) * local_heads]

    for r in range(requests):
        for live in range(1, blocks + 1):
            @pl.when((lengths[r] > (live - 1) * block) & (lengths[r] <= live * block))
            def _():
                request(r, live)

    for k, out in enumerate(outs):
        out[...] = latents[me ^ k]


def attend(query, cache, scales, lengths, owners):
    requests, heads, channels = query.shape
    cache_len = cache.shape[1]
    rank = channels - ROPE_DIM
    return pl.pallas_call(
        functools.partial(attend_kernel, owners),
        out_shape=[jax.ShapeDtypeStruct((requests, heads // owners, rank), jnp.bfloat16)] * owners,
        in_specs=[pl.BlockSpec(memory_space=pl.ANY)] * 4,
        out_specs=[pl.BlockSpec(memory_space=pltpu.VMEM)] * owners,
        scratch_shapes=[
            pltpu.VMEM((owners, requests, heads // owners, rank), jnp.bfloat16),
            pltpu.SMEM((requests,), jnp.int32),
            pltpu.VMEM((requests, channels, heads), jnp.bfloat16),
            pltpu.VMEM((channels,), jnp.float32),
            pltpu.VMEM((requests, channels, cache_len), jnp.bfloat16),
            pltpu.SemaphoreType.DMA((requests, cache_len // min(BLOCK, cache_len))),
            pltpu.SemaphoreType.DMA((3,)),
        ],
        compiler_params=pltpu.CompilerParams(vmem_limit_bytes=24 * 2**20),
        cost_estimate=pl.CostEstimate(
            flops=4 * requests * heads * channels * cache_len,
            bytes_accessed=2 * requests * channels * cache_len,
            transcendentals=requests * heads * cache_len,
        ),
        name="attend",
    )(*(pltpu.with_memory_space_constraint(x, pltpu.HBM) for x in (lengths, jnp.swapaxes(query, 1, 2), scales, jnp.swapaxes(cache, 1, 2))))


def project_kernel(owners, *refs):
    parts, maps, outs, rows = refs[:owners], refs[owners], refs[owners + 1:-1], refs[-1]
    requests, local_heads, rank = parts[0].shape
    width = maps.shape[2]
    batch = owners * requests
    for b in range(batch):
        for k in range(rank // LANES):
            rows[k, b * local_heads:(b + 1) * local_heads] = parts[b // requests][
                b % requests, :, k * LANES:(k + 1) * LANES
            ].astype(jnp.float32)
    for h in range(0, local_heads, 2):
        pair = jnp.concatenate(
            [
                jnp.concatenate(
                    [rows[k, pl.ds(h + i, batch, stride=local_heads), :] for i in range(2)], axis=0
                ).astype(jnp.bfloat16)
                for k in range(rank // LANES)
            ],
            axis=1,
        )
        both = jnp.concatenate([maps[h], maps[h + 1]], axis=1)
        values = jnp.dot(pair, both, preferred_element_type=jnp.float32)
        for i in range(2):
            mine = values[i * batch:(i + 1) * batch, i * width:(i + 1) * width]
            for d, out in enumerate(outs):
                out[h + i] = mine[d * requests:(d + 1) * requests].astype(jnp.bfloat16)


def project(latents, maps):
    owners = len(latents)
    requests, local_heads, rank = latents[0].shape
    width = maps.shape[2]
    return pl.pallas_call(
        functools.partial(project_kernel, owners),
        out_shape=[jax.ShapeDtypeStruct((local_heads, requests, width), jnp.bfloat16)] * owners,
        in_specs=[pl.BlockSpec(memory_space=pltpu.VMEM)] * (owners + 1),
        out_specs=[pl.BlockSpec(memory_space=pltpu.VMEM)] * owners,
        scratch_shapes=[pltpu.VMEM((rank // LANES, owners * requests * local_heads, LANES), jnp.float32)],
        compiler_params=pltpu.CompilerParams(vmem_limit_bytes=24 * 2**20),
        cost_estimate=pl.CostEstimate(
            flops=2 * owners * requests * local_heads * rank * width,
            bytes_accessed=2 * local_heads * rank * width,
            transcendentals=0,
        ),
        name="project",
    )(*latents, maps)


def assemble_kernel(owners, *refs):
    parts, out, sems = refs[:owners], refs[owners], refs[owners + 1]
    me = lax.axis_index("tp")
    copies = [
        pltpu.make_async_copy(part, out.at[me ^ k], sems.at[k]) for k, part in enumerate(parts)
    ]
    for copy in copies:
        copy.start()
    for copy in copies:
        copy.wait()


def assemble(parts):
    owners = len(parts)
    return pl.pallas_call(
        functools.partial(assemble_kernel, owners),
        out_shape=pltpu.HBM((owners,) + parts[0].shape, parts[0].dtype),
        in_specs=[pl.BlockSpec(memory_space=pl.ANY)] * owners,
        out_specs=pl.BlockSpec(memory_space=pltpu.HBM),
        scratch_shapes=[pltpu.SemaphoreType.DMA((owners,))],
        name="assemble",
    )(*parts)


def exchange(parts):
    owners = len(parts)
    return [parts[0]] + [
        lax.ppermute(part, "tp", [(i, i ^ k) for i in range(owners)])
        for k, part in enumerate(parts) if k
    ]


def on_device(query, cache, scales, lengths, value_up):
    owners = lax.axis_size("tp")
    latents = exchange(attend(query, cache, scales, lengths, owners))
    values = exchange(project(latents, value_up))
    returned = assemble(values)
    _, local_heads, requests, width = returned.shape
    returned = returned.reshape(owners * local_heads, requests, width)
    return jnp.swapaxes(returned, 0, 1).reshape(requests, owners * local_heads * width)


def solution(mesh):
    in_specs = (
        P(("grp", "tp"), None, None),
        P(("grp", "tp"), None, None),
        P(),
        P(("grp", "tp")),
        P("tp", None, None),
    )
    out_specs = P(("grp", "tp"), None)
    return jax.shard_map(
        on_device, mesh=mesh, in_specs=in_specs, out_specs=out_specs, check_vma=False
    )
```

```python
import functools
import math

import jax
import jax.numpy as jnp
from jax import lax
from jax.experimental import pallas as pl
from jax.experimental.pallas import tpu as pltpu
from jax.sharding import PartitionSpec as P

ROPE_DIM = 64
SOFTMAX_SCALE = (1.0 + 0.1 * math.log(40.0)) ** 2 / math.sqrt(192.0)
BLOCK = 512
LANES = 128


def attend_kernel(owners, lengths_hbm, query_hbm, scales_hbm, cache, maps_hbm, *refs):
    outs, maps = refs[:owners], refs[owners]
    latents, lengths, query, scales, keys, sems, small_sems = refs[owners + 1:]
    requests, channels, heads = query.shape
    local_heads, rank = latents.shape[2:]
    me = lax.axis_index("tp")
    cache_len = cache.shape[2]
    block = min(BLOCK, cache_len)
    blocks = cache_len // block

    def fetch(r, b):
        span = pl.ds(b * block, block)
        return pltpu.make_async_copy(cache.at[r, :, span], keys.at[r, :, span], sems.at[r, b])

    small = [
        pltpu.make_async_copy(source, target, small_sems.at[i])
        for i, (source, target) in enumerate(
            [(lengths_hbm, lengths), (query_hbm, query), (scales_hbm, scales)]
        )
    ]
    for copy in small:
        copy.start()
    fetch(0, 0).start()
    small[0].wait()
    for r in range(requests):
        for b in range(blocks):
            if (r, b) != (0, 0):
                @pl.when(b * block < lengths[r])
                def _():
                    fetch(r, b).start()
    maps_copy = pltpu.make_async_copy(maps_hbm, maps, small_sems.at[3])
    maps_copy.start()
    small[1].wait()
    small[2].wait()

    scale_row = scales[...].reshape(1, channels)

    def request(r, live):
        scaled = (query[r].astype(jnp.float32).T * scale_row).astype(jnp.bfloat16)
        parts = []
        for b in range(live):
            fetch(r, b).wait()
            part = jnp.dot(
                scaled, keys[r, :, b * block:(b + 1) * block],
                preferred_element_type=jnp.float32,
            )
            if b == live - 1:
                place = b * block + lax.broadcasted_iota(jnp.int32, part.shape, 1)
                part = jnp.where(place < lengths[r], part, -jnp.inf)
            parts.append(part)
        top = jnp.max(parts[0], axis=1, keepdims=True)
        for part in parts[1:]:
            top = jnp.maximum(top, jnp.max(part, axis=1, keepdims=True))
        total = jnp.zeros_like(top)
        mixture = jnp.zeros((heads, rank), jnp.float32)
        for b, part in enumerate(parts):
            weights = jnp.exp((part - top) * SOFTMAX_SCALE)
            total += jnp.sum(weights, axis=1, keepdims=True)
            mixture += lax.dot_general(
                weights.astype(jnp.bfloat16), keys[r, :rank, b * block:(b + 1) * block],
                (((1,), (1,)), ((), ())), preferred_element_type=jnp.float32,
            )
        latent = (mixture / total * scale_row[:, :rank]).astype(jnp.bfloat16)
        for d in range(owners):
            latents[d, r] = latent[d * local_heads:(d + 1) * local_heads]

    for r in range(requests):
        for live in range(1, blocks + 1):
            @pl.when((lengths[r] > (live - 1) * block) & (lengths[r] <= live * block))
            def _():
                request(r, live)

    for k, out in enumerate(outs):
        out[...] = latents[me ^ k]
    maps_copy.wait()


def attend(query, cache, scales, lengths, maps, owners):
    requests, heads, channels = query.shape
    cache_len = cache.shape[1]
    rank = channels - ROPE_DIM
    return pl.pallas_call(
        functools.partial(attend_kernel, owners),
        out_shape=[jax.ShapeDtypeStruct((requests, heads // owners, rank), jnp.bfloat16)] * owners
        + [jax.ShapeDtypeStruct(maps.shape, maps.dtype)],
        in_specs=[pl.BlockSpec(memory_space=pl.ANY)] * 5,
        out_specs=[pl.BlockSpec(memory_space=pltpu.VMEM)] * (owners + 1),
        scratch_shapes=[
            pltpu.VMEM((owners, requests, heads // owners, rank), jnp.bfloat16),
            pltpu.SMEM((requests,), jnp.int32),
            pltpu.VMEM((requests, channels, heads), jnp.bfloat16),
            pltpu.VMEM((channels,), jnp.float32),
            pltpu.VMEM((requests, channels, cache_len), jnp.bfloat16),
            pltpu.SemaphoreType.DMA((requests, cache_len // min(BLOCK, cache_len))),
            pltpu.SemaphoreType.DMA((4,)),
        ],
        compiler_params=pltpu.CompilerParams(vmem_limit_bytes=24 * 2**20),
        cost_estimate=pl.CostEstimate(
            flops=4 * requests * heads * channels * cache_len,
            bytes_accessed=2 * requests * channels * cache_len,
            transcendentals=requests * heads * cache_len,
        ),
        name="attend",
    )(*(
        pltpu.with_memory_space_constraint(x, pltpu.HBM)
        for x in (lengths, jnp.swapaxes(query, 1, 2), scales, jnp.swapaxes(cache, 1, 2), maps)
    ))


def project_kernel(owners, *refs):
    parts, maps, outs, rows = refs[:owners], refs[owners], refs[owners + 1:-1], refs[-1]
    requests, local_heads, rank = parts[0].shape
    width = maps.shape[2]
    batch = owners * requests
    for b in range(batch):
        for k in range(rank // LANES):
            rows[k, b * local_heads:(b + 1) * local_heads] = parts[b // requests][
                b % requests, :, k * LANES:(k + 1) * LANES
            ].astype(jnp.float32)
    for h in range(0, local_heads, 2):
        pair = jnp.concatenate(
            [
                jnp.concatenate(
                    [rows[k, pl.ds(h + i, batch, stride=local_heads), :] for i in range(2)], axis=0
                ).astype(jnp.bfloat16)
                for k in range(rank // LANES)
            ],
            axis=1,
        )
        both = jnp.concatenate([maps[h], maps[h + 1]], axis=1)
        values = jnp.dot(pair, both, preferred_element_type=jnp.float32)
        for i in range(2):
            mine = values[i * batch:(i + 1) * batch, i * width:(i + 1) * width]
            for d, out in enumerate(outs):
                out[h + i] = mine[d * requests:(d + 1) * requests].astype(jnp.bfloat16)


def project(latents, maps):
    owners = len(latents)
    requests, local_heads, rank = latents[0].shape
    width = maps.shape[2]
    return pl.pallas_call(
        functools.partial(project_kernel, owners),
        out_shape=[jax.ShapeDtypeStruct((local_heads, requests, width), jnp.bfloat16)] * owners,
        in_specs=[pl.BlockSpec(memory_space=pltpu.VMEM)] * (owners + 1),
        out_specs=[pl.BlockSpec(memory_space=pltpu.VMEM)] * owners,
        scratch_shapes=[pltpu.VMEM((rank // LANES, owners * requests * local_heads, LANES), jnp.float32)],
        compiler_params=pltpu.CompilerParams(vmem_limit_bytes=24 * 2**20),
        cost_estimate=pl.CostEstimate(
            flops=2 * owners * requests * local_heads * rank * width,
            bytes_accessed=2 * local_heads * rank * width,
            transcendentals=0,
        ),
        name="project",
    )(*latents, maps)


def assemble_kernel(owners, *refs):
    parts, out, sems = refs[:owners], refs[owners], refs[owners + 1]
    me = lax.axis_index("tp")
    copies = [
        pltpu.make_async_copy(part, out.at[me ^ k], sems.at[k]) for k, part in enumerate(parts)
    ]
    for copy in copies:
        copy.start()
    for copy in copies:
        copy.wait()


def assemble(parts):
    owners = len(parts)
    return pl.pallas_call(
        functools.partial(assemble_kernel, owners),
        out_shape=pltpu.HBM((owners,) + parts[0].shape, parts[0].dtype),
        in_specs=[pl.BlockSpec(memory_space=pltpu.VMEM)] * owners,
        out_specs=pl.BlockSpec(memory_space=pltpu.HBM),
        scratch_shapes=[pltpu.SemaphoreType.DMA((owners,))],
        name="assemble",
    )(*parts)


def exchange(parts):
    owners = len(parts)
    return [parts[0]] + [
        lax.ppermute(part, "tp", [(i, i ^ k) for i in range(owners)])
        for k, part in enumerate(parts) if k
    ]


def on_device(query, cache, scales, lengths, value_up):
    owners = lax.axis_size("tp")
    *latents, maps = attend(query, cache, scales, lengths, value_up, owners)
    values = exchange(project(exchange(latents), maps))
    returned = assemble(values)
    _, local_heads, requests, width = returned.shape
    returned = returned.reshape(owners * local_heads, requests, width)
    return jnp.swapaxes(returned, 0, 1).reshape(requests, owners * local_heads * width)


def solution(mesh):
    in_specs = (
        P(("grp", "tp"), None, None),
        P(("grp", "tp"), None, None),
        P(),
        P(("grp", "tp")),
        P("tp", None, None),
    )
    out_specs = P(("grp", "tp"), None)
    return jax.shard_map(
        on_device, mesh=mesh, in_specs=in_specs, out_specs=out_specs, check_vma=False
    )
```

```python
import functools
import math

import jax
import jax.numpy as jnp
from jax import lax
from jax.experimental import pallas as pl
from jax.experimental.pallas import tpu as pltpu
from jax.sharding import PartitionSpec as P

ROPE_DIM = 64
SOFTMAX_SCALE = (1.0 + 0.1 * math.log(40.0)) ** 2 / math.sqrt(192.0)
BLOCK = 512
LANES = 128


def attend_kernel(owners, lengths_hbm, query_hbm, scales_hbm, cache, maps_hbm, *refs):
    outs, maps = refs[:owners], refs[owners]
    latents, lengths, query, scales, keys, sems, small_sems = refs[owners + 1:]
    requests, channels, heads = query.shape
    local_heads, rank = latents.shape[2:]
    me = lax.axis_index("tp")
    cache_len = cache.shape[2]
    block = min(BLOCK, cache_len)
    blocks = cache_len // block

    def fetch(r, b):
        span = pl.ds(b * block, block)
        return pltpu.make_async_copy(cache.at[r, :, span], keys.at[r, :, span], sems.at[r, b])

    small = [
        pltpu.make_async_copy(source, target, small_sems.at[i])
        for i, (source, target) in enumerate(
            [(lengths_hbm, lengths), (query_hbm, query), (scales_hbm, scales)]
        )
    ]
    for copy in small:
        copy.start()
    fetch(0, 0).start()
    small[0].wait()
    for r in range(requests):
        for b in range(blocks):
            if (r, b) != (0, 0):
                @pl.when(b * block < lengths[r])
                def _():
                    fetch(r, b).start()
    maps_copy = pltpu.make_async_copy(maps_hbm, maps, small_sems.at[3])
    maps_copy.start()
    small[1].wait()
    small[2].wait()

    scale_row = scales[...].reshape(1, channels)

    def request(r, live):
        scaled = (query[r].astype(jnp.float32).T * scale_row).astype(jnp.bfloat16)
        parts = []
        for b in range(live):
            fetch(r, b).wait()
            part = jnp.dot(
                scaled, keys[r, :, b * block:(b + 1) * block],
                preferred_element_type=jnp.float32,
            )
            if b == live - 1:
                place = b * block + lax.broadcasted_iota(jnp.int32, part.shape, 1)
                part = jnp.where(place < lengths[r], part, -jnp.inf)
            parts.append(part)
        top = jnp.max(parts[0], axis=1, keepdims=True)
        for part in parts[1:]:
            top = jnp.maximum(top, jnp.max(part, axis=1, keepdims=True))
        total = jnp.zeros_like(top)
        mixture = jnp.zeros((heads, rank), jnp.float32)
        for b, part in enumerate(parts):
            weights = jnp.exp((part - top) * SOFTMAX_SCALE)
            total += jnp.sum(weights, axis=1, keepdims=True)
            mixture += lax.dot_general(
                weights.astype(jnp.bfloat16), keys[r, :rank, b * block:(b + 1) * block],
                (((1,), (1,)), ((), ())), preferred_element_type=jnp.float32,
            )
        latent = (mixture / total * scale_row[:, :rank]).astype(jnp.bfloat16)
        for d in range(owners):
            latents[d, r] = latent[d * local_heads:(d + 1) * local_heads]

    for r in range(requests):
        for live in range(1, blocks + 1):
            @pl.when((lengths[r] > (live - 1) * block) & (lengths[r] <= live * block))
            def _():
                request(r, live)

    for k, out in enumerate(outs):
        out[...] = latents[me ^ k]
    maps_copy.wait()


def attend(query, cache, scales, lengths, maps, owners):
    requests, heads, channels = query.shape
    cache_len = cache.shape[1]
    rank = channels - ROPE_DIM
    return pl.pallas_call(
        functools.partial(attend_kernel, owners),
        out_shape=[jax.ShapeDtypeStruct((requests, heads // owners, rank), jnp.bfloat16)] * owners
        + [jax.ShapeDtypeStruct(maps.shape, maps.dtype)],
        in_specs=[pl.BlockSpec(memory_space=pl.ANY)] * 5,
        out_specs=[pl.BlockSpec(memory_space=pltpu.VMEM)] * (owners + 1),
        scratch_shapes=[
            pltpu.VMEM((owners, requests, heads // owners, rank), jnp.bfloat16),
            pltpu.SMEM((requests,), jnp.int32),
            pltpu.VMEM((requests, channels, heads), jnp.bfloat16),
            pltpu.VMEM((channels,), jnp.float32),
            pltpu.VMEM((requests, channels, cache_len), jnp.bfloat16),
            pltpu.SemaphoreType.DMA((requests, cache_len // min(BLOCK, cache_len))),
            pltpu.SemaphoreType.DMA((4,)),
        ],
        compiler_params=pltpu.CompilerParams(vmem_limit_bytes=24 * 2**20),
        cost_estimate=pl.CostEstimate(
            flops=4 * requests * heads * channels * cache_len,
            bytes_accessed=2 * requests * channels * cache_len,
            transcendentals=requests * heads * cache_len,
        ),
        name="attend",
    )(*(
        pltpu.with_memory_space_constraint(x, pltpu.HBM)
        for x in (lengths, jnp.swapaxes(query, 1, 2), scales, jnp.swapaxes(cache, 1, 2), maps)
    ))


def project_kernel(owners, *refs):
    parts, maps, outs, rows = refs[:owners], refs[owners], refs[owners + 1:-1], refs[-1]
    requests, local_heads, rank = parts[0].shape
    width = maps.shape[2]
    batch = owners * requests
    for b in range(batch):
        for k in range(rank // LANES):
            rows[k, b * local_heads:(b + 1) * local_heads] = parts[b // requests][
                b % requests, :, k * LANES:(k + 1) * LANES
            ].astype(jnp.float32)
    for h in range(0, local_heads, 2):
        pair = jnp.concatenate(
            [
                jnp.concatenate(
                    [rows[k, pl.ds(h + i, batch, stride=local_heads), :] for i in range(2)], axis=0
                ).astype(jnp.bfloat16)
                for k in range(rank // LANES)
            ],
            axis=1,
        )
        both = jnp.concatenate([maps[h], maps[h + 1]], axis=1)
        values = jnp.dot(pair, both, preferred_element_type=jnp.float32)
        for i in range(2):
            mine = values[i * batch:(i + 1) * batch, i * width:(i + 1) * width]
            for d, out in enumerate(outs):
                out[h + i] = mine[d * requests:(d + 1) * requests].astype(jnp.bfloat16)


def project(latents, maps):
    owners = len(latents)
    requests, local_heads, rank = latents[0].shape
    width = maps.shape[2]
    return pl.pallas_call(
        functools.partial(project_kernel, owners),
        out_shape=[jax.ShapeDtypeStruct((local_heads, requests, width), jnp.bfloat16)] * owners,
        in_specs=[pl.BlockSpec(memory_space=pltpu.VMEM)] * (owners + 1),
        out_specs=[pl.BlockSpec(memory_space=pltpu.VMEM)] * owners,
        scratch_shapes=[pltpu.VMEM((rank // LANES, owners * requests * local_heads, LANES), jnp.float32)],
        compiler_params=pltpu.CompilerParams(vmem_limit_bytes=24 * 2**20),
        cost_estimate=pl.CostEstimate(
            flops=2 * owners * requests * local_heads * rank * width,
            bytes_accessed=2 * local_heads * rank * width,
            transcendentals=0,
        ),
        name="project",
    )(*latents, maps)


def assemble_kernel(owners, *refs):
    parts, out, sems = refs[:owners], refs[owners], refs[owners + 1]
    me = lax.axis_index("tp")
    copies = [
        pltpu.make_async_copy(part, out.at[me ^ k], sems.at[k]) for k, part in enumerate(parts)
    ]
    for copy in copies:
        copy.start()
    for copy in copies:
        copy.wait()


def assemble(parts):
    owners = len(parts)
    return pl.pallas_call(
        functools.partial(assemble_kernel, owners),
        out_shape=pltpu.HBM((owners,) + parts[0].shape, parts[0].dtype),
        in_specs=[pl.BlockSpec(memory_space=pltpu.VMEM)] * owners,
        out_specs=pl.BlockSpec(memory_space=pltpu.HBM),
        scratch_shapes=[pltpu.SemaphoreType.DMA((owners,))],
        compiler_params=pltpu.CompilerParams(vmem_limit_bytes=2 * 2**20),
        name="assemble",
    )(*parts)


def exchange(parts):
    owners = len(parts)
    moved = {
        k: lax.ppermute(parts[k], "tp", [(i, i ^ k) for i in range(owners)])
        for k in range(owners - 1, 0, -1)
    }
    return [parts[0]] + [moved[k] for k in range(1, owners)]


def on_device(query, cache, scales, lengths, value_up):
    owners = lax.axis_size("tp")
    *latents, maps = attend(query, cache, scales, lengths, value_up, owners)
    values = exchange(project(exchange(latents), maps))
    returned = assemble(values)
    _, local_heads, requests, width = returned.shape
    returned = returned.reshape(owners * local_heads, requests, width)
    return jnp.swapaxes(returned, 0, 1).reshape(requests, owners * local_heads * width)


def solution(mesh):
    in_specs = (
        P(("grp", "tp"), None, None),
        P(("grp", "tp"), None, None),
        P(),
        P(("grp", "tp")),
        P("tp", None, None),
    )
    out_specs = P(("grp", "tp"), None)
    return jax.shard_map(
        on_device, mesh=mesh, in_specs=in_specs, out_specs=out_specs, check_vma=False
    )
```

```python
import functools
import math

import jax
import jax.numpy as jnp
from jax import lax
from jax.experimental import pallas as pl
from jax.experimental.pallas import tpu as pltpu
from jax.sharding import PartitionSpec as P

ROPE_DIM = 64
SOFTMAX_SCALE = (1.0 + 0.1 * math.log(40.0)) ** 2 / math.sqrt(192.0)
BLOCK = 512
LANES = 128


def plan(owners):
    if owners != 4:
        return [(k, [(i, i ^ k) for i in range(owners)]) for k in range(1, owners)]
    return [
        (3, [(0, 3), (3, 0)]),
        (1, [(0, 1), (3, 2)]),
        (2, [(0, 2), (3, 1)]),
        (3, [(1, 2), (2, 1)]),
        (1, [(1, 0), (2, 3)]),
        (2, [(1, 3), (2, 0)]),
    ]


def partners(owners):
    return [0] + [k for k, _ in plan(owners)]


def attend_kernel(owners, lengths_hbm, query_hbm, scales_hbm, cache, maps_hbm, *refs):
    *outs, maps = refs[:-7]
    latents, lengths, query, scales, keys, sems, small_sems = refs[-7:]
    requests, channels, heads = query.shape
    local_heads, rank = latents.shape[2:]
    me = lax.axis_index("tp")
    cache_len = cache.shape[2]
    block = min(BLOCK, cache_len)
    blocks = cache_len // block

    def fetch(r, b):
        span = pl.ds(b * block, block)
        return pltpu.make_async_copy(cache.at[r, :, span], keys.at[r, :, span], sems.at[r, b])

    small = [
        pltpu.make_async_copy(source, target, small_sems.at[i])
        for i, (source, target) in enumerate(
            [(lengths_hbm, lengths), (query_hbm, query), (scales_hbm, scales)]
        )
    ]
    for copy in small:
        copy.start()
    fetch(0, 0).start()
    small[0].wait()
    for r in range(requests):
        for b in range(blocks):
            if (r, b) != (0, 0):
                @pl.when(b * block < lengths[r])
                def _():
                    fetch(r, b).start()
    maps_copy = pltpu.make_async_copy(maps_hbm, maps, small_sems.at[3])
    maps_copy.start()
    small[1].wait()
    small[2].wait()

    scale_row = scales[...].reshape(1, channels)

    def request(r, live):
        scaled = (query[r].astype(jnp.float32).T * scale_row).astype(jnp.bfloat16)
        parts = []
        for b in range(live):
            fetch(r, b).wait()
            part = jnp.dot(
                scaled, keys[r, :, b * block:(b + 1) * block],
                preferred_element_type=jnp.float32,
            )
            if b == live - 1:
                place = b * block + lax.broadcasted_iota(jnp.int32, part.shape, 1)
                part = jnp.where(place < lengths[r], part, -jnp.inf)
            parts.append(part)
        top = jnp.max(parts[0], axis=1, keepdims=True)
        for part in parts[1:]:
            top = jnp.maximum(top, jnp.max(part, axis=1, keepdims=True))
        total = jnp.zeros_like(top)
        mixture = jnp.zeros((heads, rank), jnp.float32)
        for b, part in enumerate(parts):
            weights = jnp.exp((part - top) * SOFTMAX_SCALE)
            total += jnp.sum(weights, axis=1, keepdims=True)
            mixture += lax.dot_general(
                weights.astype(jnp.bfloat16), keys[r, :rank, b * block:(b + 1) * block],
                (((1,), (1,)), ((), ())), preferred_element_type=jnp.float32,
            )
        latent = (mixture / total * scale_row[:, :rank]).astype(jnp.bfloat16)
        for d in range(owners):
            latents[d, r] = latent[d * local_heads:(d + 1) * local_heads]

    for r in range(requests):
        for live in range(1, blocks + 1):
            @pl.when((lengths[r] > (live - 1) * block) & (lengths[r] <= live * block))
            def _():
                request(r, live)

    for out, k in zip(outs, partners(owners)):
        out[...] = latents[me ^ k]
    maps_copy.wait()


def attend(query, cache, scales, lengths, maps, owners):
    requests, heads, channels = query.shape
    cache_len = cache.shape[1]
    rank = channels - ROPE_DIM
    return pl.pallas_call(
        functools.partial(attend_kernel, owners),
        out_shape=[jax.ShapeDtypeStruct((requests, heads // owners, rank), jnp.bfloat16)]
        * len(partners(owners))
        + [jax.ShapeDtypeStruct(maps.shape, maps.dtype)],
        in_specs=[pl.BlockSpec(memory_space=pl.ANY)] * 5,
        out_specs=[pl.BlockSpec(memory_space=pltpu.VMEM)] * (len(partners(owners)) + 1),
        scratch_shapes=[
            pltpu.VMEM((owners, requests, heads // owners, rank), jnp.bfloat16),
            pltpu.SMEM((requests,), jnp.int32),
            pltpu.VMEM((requests, channels, heads), jnp.bfloat16),
            pltpu.VMEM((channels,), jnp.float32),
            pltpu.VMEM((requests, channels, cache_len), jnp.bfloat16),
            pltpu.SemaphoreType.DMA((requests, cache_len // min(BLOCK, cache_len))),
            pltpu.SemaphoreType.DMA((4,)),
        ],
        compiler_params=pltpu.CompilerParams(vmem_limit_bytes=24 * 2**20),
        cost_estimate=pl.CostEstimate(
            flops=4 * requests * heads * channels * cache_len,
            bytes_accessed=2 * requests * channels * cache_len,
            transcendentals=requests * heads * cache_len,
        ),
        name="attend",
    )(*(
        pltpu.with_memory_space_constraint(x, pltpu.HBM)
        for x in (lengths, jnp.swapaxes(query, 1, 2), scales, jnp.swapaxes(cache, 1, 2), maps)
    ))


def project_kernel(owners, count, *refs):
    parts, maps, outs, rows = refs[:count], refs[count], refs[count + 1:-1], refs[-1]
    requests, local_heads, rank = parts[0].shape
    width = maps.shape[2]
    batch = owners * requests

    def lay(received):
        for b in range(batch):
            for k in range(rank // LANES):
                rows[k, b * local_heads:(b + 1) * local_heads] = received[b // requests][
                    b % requests, :, k * LANES:(k + 1) * LANES
                ].astype(jnp.float32)

    by_role(owners, parts, lay)
    for h in range(0, local_heads, 2):
        pair = jnp.concatenate(
            [
                jnp.concatenate(
                    [rows[k, pl.ds(h + i, batch, stride=local_heads), :] for i in range(2)], axis=0
                ).astype(jnp.bfloat16)
                for k in range(rank // LANES)
            ],
            axis=1,
        )
        both = jnp.concatenate([maps[h], maps[h + 1]], axis=1)
        values = jnp.dot(pair, both, preferred_element_type=jnp.float32)
        for i in range(2):
            mine = values[i * batch:(i + 1) * batch, i * width:(i + 1) * width]
            for out, k in zip(outs, partners(owners)):
                out[h + i] = mine[k * requests:(k + 1) * requests].astype(jnp.bfloat16)


def project(parts, maps, owners):
    requests, local_heads, rank = parts[0].shape
    width = maps.shape[2]
    return pl.pallas_call(
        functools.partial(project_kernel, owners, len(parts)),
        out_shape=[jax.ShapeDtypeStruct((local_heads, requests, width), jnp.bfloat16)]
        * len(partners(owners)),
        in_specs=[pl.BlockSpec(memory_space=pltpu.VMEM)] * (len(parts) + 1),
        out_specs=[pl.BlockSpec(memory_space=pltpu.VMEM)] * len(partners(owners)),
        scratch_shapes=[pltpu.VMEM((rank // LANES, owners * requests * local_heads, LANES), jnp.float32)],
        compiler_params=pltpu.CompilerParams(vmem_limit_bytes=24 * 2**20),
        cost_estimate=pl.CostEstimate(
            flops=2 * owners * requests * local_heads * rank * width,
            bytes_accessed=2 * local_heads * rank * width,
            transcendentals=0,
        ),
        name="project",
    )(*parts, maps)


def assemble_kernel(owners, count, *refs):
    parts, out, sems = refs[:count], refs[count], refs[count + 1]
    me = lax.axis_index("tp")

    def place(received):
        copies = [
            pltpu.make_async_copy(part, out.at[me ^ k], sems.at[k])
            for k, part in enumerate(received)
        ]
        for copy in copies:
            copy.start()
        for copy in copies:
            copy.wait()

    by_role(owners, parts, place)


def assemble(parts, owners):
    return pl.pallas_call(
        functools.partial(assemble_kernel, owners, len(parts)),
        out_shape=pltpu.HBM((owners,) + parts[0].shape, parts[0].dtype),
        in_specs=[pl.BlockSpec(memory_space=pltpu.VMEM)] * len(parts),
        out_specs=pl.BlockSpec(memory_space=pltpu.HBM),
        scratch_shapes=[pltpu.SemaphoreType.DMA((owners,))],
        compiler_params=pltpu.CompilerParams(vmem_limit_bytes=2 * 2**20),
        name="assemble",
    )(*parts)


def exchange(parts, owners):
    mine, *sent = parts
    return [mine] + [
        lax.ppermute(part, "tp", pairs) for part, (_, pairs) in zip(sent, plan(owners))
    ]


def by_role(owners, parts, act):
    if len(parts) == owners:
        act(parts)
        return
    mine, opposite, one, two, across, back_one, back_two = parts
    me = lax.axis_index("tp")
    outer = (me == 0) | (me == owners - 1)

    @pl.when(outer)
    def _():
        act([mine, back_one, back_two, opposite])

    @pl.when(jnp.logical_not(outer))
    def _():
        act([mine, one, two, across])


def on_device(query, cache, scales, lengths, value_up):
    owners = lax.axis_size("tp")
    *latents, maps = attend(query, cache, scales, lengths, value_up, owners)
    values = project(exchange(latents, owners), maps, owners)
    returned = assemble(exchange(values, owners), owners)
    _, local_heads, requests, width = returned.shape
    returned = returned.reshape(owners * local_heads, requests, width)
    return jnp.swapaxes(returned, 0, 1).reshape(requests, owners * local_heads * width)


def solution(mesh):
    in_specs = (
        P(("grp", "tp"), None, None),
        P(("grp", "tp"), None, None),
        P(),
        P(("grp", "tp")),
        P("tp", None, None),
    )
    out_specs = P(("grp", "tp"), None)
    return jax.shard_map(
        on_device, mesh=mesh, in_specs=in_specs, out_specs=out_specs, check_vma=False
    )
```

```python
import functools
import math

import jax
import jax.numpy as jnp
from jax import lax
from jax.experimental import pallas as pl
from jax.experimental.pallas import tpu as pltpu
from jax.sharding import PartitionSpec as P

ROPE_DIM = 64
SOFTMAX_SCALE = (1.0 + 0.1 * math.log(40.0)) ** 2 / math.sqrt(192.0)
EXP2_SCALE = SOFTMAX_SCALE * math.log2(math.e)
BLOCK = 512
LANES = 128


def order(owners):
    return [0] + list(range(owners - 1, 0, -1))


def attend_kernel(owners, lengths_hbm, query_hbm, scales_hbm, cache, *refs):
    outs, refs = refs[:owners], refs[owners:]
    latents, lengths, query, scales, keys, scaled, scores, weights, sems, small_sems = refs
    requests, channels, heads = query.shape
    local_heads, rank = latents.shape[2:]
    cache_len = cache.shape[2]
    block = min(BLOCK, cache_len)
    blocks = cache_len // block
    me = lax.axis_index("tp")

    def fetch(r, b):
        span = pl.ds(b * block, block)
        return pltpu.make_async_copy(cache.at[r, :, span], keys.at[r, :, span], sems.at[r, b])

    small = [
        pltpu.make_async_copy(source, target, small_sems.at[i])
        for i, (source, target) in enumerate(
            [(lengths_hbm, lengths), (query_hbm, query), (scales_hbm, scales)]
        )
    ]
    for copy in small:
        copy.start()
    for b in range(blocks):
        for r in range(requests):
            fetch(r, b).start()
    small[1].wait()
    small[2].wait()
    scale_row = scales[...].reshape(1, channels)
    for r in range(requests):
        scaled[r] = (query[r].astype(jnp.float32).T * scale_row).astype(jnp.bfloat16)
    small[0].wait()

    def score(slot, r, live):
        top = None
        for b in range(live):
            fetch(r, b).wait()
            span = slice(b * block, (b + 1) * block)
            part = jnp.dot(scaled[r], keys[r, :, span], preferred_element_type=jnp.float32)
            if b == live - 1:
                place = b * block + lax.broadcasted_iota(jnp.int32, part.shape, 1)
                part = jnp.where(place < lengths[r], part, -jnp.inf)
            scores[slot, :, span] = part
            high = jnp.max(part, axis=1, keepdims=True)
            top = high if top is None else jnp.maximum(top, high)
        return top

    def weigh(slot, live, top):
        total = jnp.zeros_like(top)
        for b in range(live):
            span = slice(b * block, (b + 1) * block)
            weight = jnp.exp2((scores[slot, :, span] - top) * EXP2_SCALE)
            total += jnp.sum(weight, axis=1, keepdims=True)
            weights[slot, :, span] = weight.astype(jnp.bfloat16)
        return total

    def mix(slot, r, live):
        return lax.dot_general(
            weights[slot, :, :live * block], keys[r, :rank, :live * block],
            (((1,), (1,)), ((), ())), preferred_element_type=jnp.float32,
        )

    def finish(r, mixture, total):
        latent = (mixture * (1.0 / total) * scale_row[:, :rank]).astype(jnp.bfloat16)
        for d in range(owners):
            latents[d, r] = latent[d * local_heads:(d + 1) * local_heads]

    def pair(r, s, live_r, live_s):
        top_r = score(0, r, live_r)
        top_s = score(1, s, live_s)
        total_r = weigh(0, live_r, top_r)
        mixture_r = mix(0, r, live_r)
        total_s = weigh(1, live_s, top_s)
        finish(r, mixture_r, total_r)
        mixture_s = mix(1, s, live_s)
        finish(s, mixture_s, total_s)
        for b in range(live_r, blocks):
            fetch(r, b).wait()
        for b in range(live_s, blocks):
            fetch(s, b).wait()

    for first in range(0, requests, 2):
        swap = (lengths[first] < lengths[first + 1]).astype(jnp.int32)
        longer, shorter = first + swap, first + 1 - swap
        live = [(lengths[r] + (block - 1)) // block for r in (longer, shorter)]
        for live_r in range(1, blocks + 1):
            for live_s in range(1, live_r + 1):
                @pl.when((live[0] == live_r) & (live[1] == live_s))
                def _():
                    pair(longer, shorter, live_r, live_s)

    for out, k in zip(outs, order(owners)):
        out[...] = latents[me ^ k]


def in_hbm(*arrays):
    return [pltpu.with_memory_space_constraint(array, pltpu.HBM) for array in arrays]


def attend(query, cache, scales, lengths, owners):
    requests, heads, channels = query.shape
    cache_len = cache.shape[1]
    rank = channels - ROPE_DIM
    part = jax.ShapeDtypeStruct((requests, heads // owners, rank), jnp.bfloat16)
    return pl.pallas_call(
        functools.partial(attend_kernel, owners),
        out_shape=[part] * owners,
        in_specs=[pl.BlockSpec(memory_space=pl.ANY)] * 4,
        out_specs=[pl.BlockSpec(memory_space=pltpu.VMEM)] * owners,
        scratch_shapes=[
            pltpu.VMEM((owners,) + part.shape, part.dtype),
            pltpu.SMEM((requests,), jnp.int32),
            pltpu.VMEM((requests, channels, heads), jnp.bfloat16),
            pltpu.VMEM((channels,), jnp.float32),
            pltpu.VMEM((requests, channels, cache_len), jnp.bfloat16),
            pltpu.VMEM((requests, heads, channels), jnp.bfloat16),
            pltpu.VMEM((2, heads, cache_len), jnp.float32),
            pltpu.VMEM((2, heads, cache_len), jnp.bfloat16),
            pltpu.SemaphoreType.DMA((requests, cache_len // min(BLOCK, cache_len))),
            pltpu.SemaphoreType.DMA((3,)),
        ],
        compiler_params=pltpu.CompilerParams(vmem_limit_bytes=24 * 2**20),
        cost_estimate=pl.CostEstimate(
            flops=4 * requests * heads * channels * cache_len,
            bytes_accessed=2 * requests * channels * cache_len,
            transcendentals=requests * heads * cache_len,
        ),
        name="attend",
    )(*in_hbm(lengths, jnp.swapaxes(query, 1, 2), scales, jnp.swapaxes(cache, 1, 2)))


def stage_kernel(maps_hbm, after, maps, sem):
    copy = pltpu.make_async_copy(maps_hbm, maps, sem)
    copy.start()
    copy.wait()


def stage(maps, after):
    return pl.pallas_call(
        stage_kernel,
        out_shape=jax.ShapeDtypeStruct(maps.shape, maps.dtype),
        in_specs=[pl.BlockSpec(memory_space=pl.ANY)] * 2,
        out_specs=pl.BlockSpec(memory_space=pltpu.VMEM),
        scratch_shapes=[pltpu.SemaphoreType.DMA(())],
        compiler_params=pltpu.CompilerParams(vmem_limit_bytes=8 * 2**20),
        cost_estimate=pl.CostEstimate(
            flops=0, bytes_accessed=4 * maps.size, transcendentals=0
        ),
        name="stage",
    )(*in_hbm(maps), after)


def project_kernel(owners, *refs):
    parts, maps, outs, rows = refs[:owners], refs[owners], refs[owners + 1:-1], refs[-1]
    requests, local_heads, rank = parts[0].shape
    width = maps.shape[2]
    batch = owners * requests
    for b in range(batch):
        for k in range(rank // LANES):
            rows[k, b * local_heads:(b + 1) * local_heads] = parts[b // requests][
                b % requests, :, k * LANES:(k + 1) * LANES
            ].astype(jnp.float32)
    for h in range(0, local_heads, 2):
        pair = jnp.concatenate(
            [
                jnp.concatenate(
                    [rows[k, pl.ds(h + i, batch, stride=local_heads), :] for i in range(2)], axis=0
                ).astype(jnp.bfloat16)
                for k in range(rank // LANES)
            ],
            axis=1,
        )
        both = jnp.concatenate([maps[h], maps[h + 1]], axis=1)
        values = jnp.dot(pair, both, preferred_element_type=jnp.float32)
        for i in range(2):
            mine = values[i * batch:(i + 1) * batch, i * width:(i + 1) * width]
            for d, out in enumerate(outs):
                out[h + i] = mine[d * requests:(d + 1) * requests].astype(jnp.bfloat16)


def project(latents, maps):
    owners = len(latents)
    requests, local_heads, rank = latents[0].shape
    width = maps.shape[2]
    return pl.pallas_call(
        functools.partial(project_kernel, owners),
        out_shape=[jax.ShapeDtypeStruct((local_heads, requests, width), jnp.bfloat16)] * owners,
        in_specs=[pl.BlockSpec(memory_space=pltpu.VMEM)] * (owners + 1),
        out_specs=[pl.BlockSpec(memory_space=pltpu.VMEM)] * owners,
        scratch_shapes=[pltpu.VMEM((rank // LANES, owners * requests * local_heads, LANES), jnp.float32)],
        compiler_params=pltpu.CompilerParams(vmem_limit_bytes=24 * 2**20),
        cost_estimate=pl.CostEstimate(
            flops=2 * owners * requests * local_heads * rank * width,
            bytes_accessed=2 * local_heads * rank * width,
            transcendentals=0,
        ),
        name="project",
    )(*latents, maps)


def assemble_kernel(owners, *refs):
    parts, out, sems = refs[:owners], refs[owners], refs[owners + 1]
    me = lax.axis_index("tp")
    copies = [
        pltpu.make_async_copy(part, out.at[me ^ k], sems.at[k])
        for k, part in zip(order(owners), parts)
    ]
    for copy in copies:
        copy.start()
    for copy in copies:
        copy.wait()


def assemble(parts):
    owners = len(parts)
    return pl.pallas_call(
        functools.partial(assemble_kernel, owners),
        out_shape=pltpu.HBM((owners,) + parts[0].shape, parts[0].dtype),
        in_specs=[pl.BlockSpec(memory_space=pltpu.VMEM)] * owners,
        out_specs=pl.BlockSpec(memory_space=pltpu.HBM),
        scratch_shapes=[pltpu.SemaphoreType.DMA((owners,))],
        compiler_params=pltpu.CompilerParams(vmem_limit_bytes=2 * 2**20),
        name="assemble",
    )(*parts)


def exchange(parts):
    owners = len(parts)
    return [
        lax.ppermute(part, "tp", [(i, i ^ k) for i in range(owners)]) if k else part
        for k, part in zip(order(owners), parts)
    ]


def on_device(query, cache, scales, lengths, value_up):
    owners = lax.axis_size("tp")
    latents = attend(query, cache, scales, lengths, owners)
    maps = stage(value_up, latents[0])
    values = exchange(project(exchange(latents), maps))
    returned = assemble(values)
    _, local_heads, requests, width = returned.shape
    returned = returned.reshape(owners * local_heads, requests, width)
    return jnp.swapaxes(returned, 0, 1).reshape(requests, owners * local_heads * width)


def solution(mesh):
    in_specs = (
        P(("grp", "tp"), None, None),
        P(("grp", "tp"), None, None),
        P(),
        P(("grp", "tp")),
        P("tp", None, None),
    )
    out_specs = P(("grp", "tp"), None)
    return jax.shard_map(
        on_device, mesh=mesh, in_specs=in_specs, out_specs=out_specs, check_vma=False
    )
```

```python
import functools
import math

import jax
import jax.numpy as jnp
from jax import lax
from jax.experimental import pallas as pl
from jax.experimental.pallas import tpu as pltpu
from jax.sharding import PartitionSpec as P

ROPE_DIM = 64
SOFTMAX_SCALE = (1.0 + 0.1 * math.log(40.0)) ** 2 / math.sqrt(192.0)
EXP2_SCALE = SOFTMAX_SCALE * math.log2(math.e)
BLOCK = 512
LANES = 128


def order(owners):
    return [0] + list(range(owners - 1, 0, -1))


def attend_kernel(owners, lengths_hbm, query_hbm, scales_hbm, cache, *refs):
    outs, refs = refs[:owners], refs[owners:]
    latents, lengths, query, scales, keys, scaled, scores, weights, sems, small_sems = refs
    requests, channels, heads = query.shape
    local_heads, rank = latents.shape[2:]
    cache_len = cache.shape[2]
    block = min(BLOCK, cache_len)
    blocks = cache_len // block
    me = lax.axis_index("tp")

    def fetch(r, b):
        span = pl.ds(b * block, block)
        return pltpu.make_async_copy(cache.at[r, :, span], keys.at[r, :, span], sems.at[r, b])

    small = [
        pltpu.make_async_copy(source, target, small_sems.at[i])
        for i, (source, target) in enumerate(
            [(lengths_hbm, lengths), (query_hbm, query), (scales_hbm, scales)]
        )
    ]
    for copy in small:
        copy.start()
    for b in range(blocks):
        for r in range(requests):
            fetch(r, b).start()
    small[1].wait()
    small[2].wait()
    scale_row = scales[...].reshape(1, channels)
    for r in range(requests):
        scaled[r] = (query[r].astype(jnp.float32).T * scale_row).astype(jnp.bfloat16)
    small[0].wait()

    def score(slot, r, live):
        top = None
        for b in range(live):
            fetch(r, b).wait()
            span = slice(b * block, (b + 1) * block)
            part = jnp.dot(scaled[r], keys[r, :, span], preferred_element_type=jnp.float32)
            if b == live - 1:
                place = b * block + lax.broadcasted_iota(jnp.int32, part.shape, 1)
                part = jnp.where(place < lengths[r], part, -jnp.inf)
            scores[slot, :, span] = part
            high = jnp.max(part, axis=1, keepdims=True)
            top = high if top is None else jnp.maximum(top, high)
        return top

    def weigh(slot, live, top):
        total = jnp.zeros_like(top)
        for b in range(live):
            span = slice(b * block, (b + 1) * block)
            weight = jnp.exp2((scores[slot, :, span] - top) * EXP2_SCALE)
            total += jnp.sum(weight, axis=1, keepdims=True)
            weights[slot, :, span] = weight.astype(jnp.bfloat16)
        return total

    def mix(slot, r, live):
        return lax.dot_general(
            keys[r, :rank, :live * block], weights[slot, :, :live * block],
            (((1,), (1,)), ((), ())), preferred_element_type=jnp.float32,
        )

    def finish(r, mixture, total):
        latent = (mixture.T * (1.0 / total) * scale_row[:, :rank]).astype(jnp.bfloat16)
        for d in range(owners):
            latents[d, r] = latent[d * local_heads:(d + 1) * local_heads]

    def pair(r, s, live_r, live_s):
        top_r = score(0, r, live_r)
        top_s = score(1, s, live_s)
        total_r = weigh(0, live_r, top_r)
        mixture_r = mix(0, r, live_r)
        total_s = weigh(1, live_s, top_s)
        finish(r, mixture_r, total_r)
        mixture_s = mix(1, s, live_s)
        finish(s, mixture_s, total_s)
        for b in range(live_r, blocks):
            fetch(r, b).wait()
        for b in range(live_s, blocks):
            fetch(s, b).wait()

    for first in range(0, requests, 2):
        swap = (lengths[first] < lengths[first + 1]).astype(jnp.int32)
        longer, shorter = first + swap, first + 1 - swap
        live = [(lengths[r] + (block - 1)) // block for r in (longer, shorter)]
        for live_r in range(1, blocks + 1):
            for live_s in range(1, live_r + 1):
                @pl.when((live[0] == live_r) & (live[1] == live_s))
                def _():
                    pair(longer, shorter, live_r, live_s)

    for out, k in zip(outs, order(owners)):
        out[...] = latents[me ^ k]


def in_hbm(*arrays):
    return [pltpu.with_memory_space_constraint(array, pltpu.HBM) for array in arrays]


def attend(query, cache, scales, lengths, owners):
    requests, heads, channels = query.shape
    cache_len = cache.shape[1]
    rank = channels - ROPE_DIM
    part = jax.ShapeDtypeStruct((requests, heads // owners, rank), jnp.bfloat16)
    return pl.pallas_call(
        functools.partial(attend_kernel, owners),
        out_shape=[part] * owners,
        in_specs=[pl.BlockSpec(memory_space=pl.ANY)] * 4,
        out_specs=[pl.BlockSpec(memory_space=pltpu.VMEM)] * owners,
        scratch_shapes=[
            pltpu.VMEM((owners,) + part.shape, part.dtype),
            pltpu.SMEM((requests,), jnp.int32),
            pltpu.VMEM((requests, channels, heads), jnp.bfloat16),
            pltpu.VMEM((channels,), jnp.float32),
            pltpu.VMEM((requests, channels, cache_len), jnp.bfloat16),
            pltpu.VMEM((requests, heads, channels), jnp.bfloat16),
            pltpu.VMEM((2, heads, cache_len), jnp.float32),
            pltpu.VMEM((2, heads, cache_len), jnp.bfloat16),
            pltpu.SemaphoreType.DMA((requests, cache_len // min(BLOCK, cache_len))),
            pltpu.SemaphoreType.DMA((3,)),
        ],
        compiler_params=pltpu.CompilerParams(vmem_limit_bytes=24 * 2**20),
        cost_estimate=pl.CostEstimate(
            flops=4 * requests * heads * channels * cache_len,
            bytes_accessed=2 * requests * channels * cache_len,
            transcendentals=requests * heads * cache_len,
        ),
        name="attend",
    )(*in_hbm(lengths, jnp.swapaxes(query, 1, 2), scales, jnp.swapaxes(cache, 1, 2)))


def stage_kernel(maps_hbm, after, maps, sem):
    copy = pltpu.make_async_copy(maps_hbm, maps, sem)
    copy.start()
    copy.wait()


def stage(maps, after):
    return pl.pallas_call(
        stage_kernel,
        out_shape=jax.ShapeDtypeStruct(maps.shape, maps.dtype),
        in_specs=[pl.BlockSpec(memory_space=pl.ANY)] * 2,
        out_specs=pl.BlockSpec(memory_space=pltpu.VMEM),
        scratch_shapes=[pltpu.SemaphoreType.DMA(())],
        compiler_params=pltpu.CompilerParams(vmem_limit_bytes=8 * 2**20),
        cost_estimate=pl.CostEstimate(
            flops=0, bytes_accessed=4 * maps.size, transcendentals=0
        ),
        name="stage",
    )(*in_hbm(maps), after)


def project_kernel(owners, *refs):
    parts, maps, outs, rows = refs[:owners], refs[owners], refs[owners + 1:-1], refs[-1]
    requests, local_heads, rank = parts[0].shape
    width = maps.shape[2]
    batch = owners * requests
    for b in range(batch):
        for k in range(rank // LANES):
            rows[k, b * local_heads:(b + 1) * local_heads] = parts[b // requests][
                b % requests, :, k * LANES:(k + 1) * LANES
            ].astype(jnp.float32)
    for h in range(0, local_heads, 2):
        pair = jnp.concatenate(
            [
                jnp.concatenate(
                    [rows[k, pl.ds(h + i, batch, stride=local_heads), :] for i in range(2)], axis=0
                ).astype(jnp.bfloat16)
                for k in range(rank // LANES)
            ],
            axis=1,
        )
        both = jnp.concatenate([maps[h], maps[h + 1]], axis=1)
        values = jnp.dot(pair, both, preferred_element_type=jnp.float32)
        for i in range(2):
            mine = values[i * batch:(i + 1) * batch, i * width:(i + 1) * width]
            for d, out in enumerate(outs):
                out[h + i] = mine[d * requests:(d + 1) * requests].astype(jnp.bfloat16)


def project(latents, maps):
    owners = len(latents)
    requests, local_heads, rank = latents[0].shape
    width = maps.shape[2]
    return pl.pallas_call(
        functools.partial(project_kernel, owners),
        out_shape=[jax.ShapeDtypeStruct((local_heads, requests, width), jnp.bfloat16)] * owners,
        in_specs=[pl.BlockSpec(memory_space=pltpu.VMEM)] * (owners + 1),
        out_specs=[pl.BlockSpec(memory_space=pltpu.VMEM)] * owners,
        scratch_shapes=[pltpu.VMEM((rank // LANES, owners * requests * local_heads, LANES), jnp.float32)],
        compiler_params=pltpu.CompilerParams(vmem_limit_bytes=24 * 2**20),
        cost_estimate=pl.CostEstimate(
            flops=2 * owners * requests * local_heads * rank * width,
            bytes_accessed=2 * local_heads * rank * width,
            transcendentals=0,
        ),
        name="project",
    )(*latents, maps)


def assemble_kernel(owners, *refs):
    parts, out, sems = refs[:owners], refs[owners], refs[owners + 1]
    me = lax.axis_index("tp")
    copies = [
        pltpu.make_async_copy(part, out.at[me ^ k], sems.at[k])
        for k, part in zip(order(owners), parts)
    ]
    for copy in copies:
        copy.start()
    for copy in copies:
        copy.wait()


def assemble(parts):
    owners = len(parts)
    return pl.pallas_call(
        functools.partial(assemble_kernel, owners),
        out_shape=pltpu.HBM((owners,) + parts[0].shape, parts[0].dtype),
        in_specs=[pl.BlockSpec(memory_space=pltpu.VMEM)] * owners,
        out_specs=pl.BlockSpec(memory_space=pltpu.HBM),
        scratch_shapes=[pltpu.SemaphoreType.DMA((owners,))],
        compiler_params=pltpu.CompilerParams(vmem_limit_bytes=2 * 2**20),
        name="assemble",
    )(*parts)


def exchange(parts):
    owners = len(parts)
    return [
        lax.ppermute(part, "tp", [(i, i ^ k) for i in range(owners)]) if k else part
        for k, part in zip(order(owners), parts)
    ]


def on_device(query, cache, scales, lengths, value_up):
    owners = lax.axis_size("tp")
    latents = attend(query, cache, scales, lengths, owners)
    maps = stage(value_up, latents[0])
    values = exchange(project(exchange(latents), maps))
    returned = assemble(values)
    _, local_heads, requests, width = returned.shape
    returned = returned.reshape(owners * local_heads, requests, width)
    return jnp.swapaxes(returned, 0, 1).reshape(requests, owners * local_heads * width)


def solution(mesh):
    in_specs = (
        P(("grp", "tp"), None, None),
        P(("grp", "tp"), None, None),
        P(),
        P(("grp", "tp")),
        P("tp", None, None),
    )
    out_specs = P(("grp", "tp"), None)
    return jax.shard_map(
        on_device, mesh=mesh, in_specs=in_specs, out_specs=out_specs, check_vma=False
    )
```

```python
import functools
import math

import jax
import jax.numpy as jnp
from jax import lax
from jax.experimental import pallas as pl
from jax.experimental.pallas import tpu as pltpu
from jax.sharding import PartitionSpec as P

ROPE_DIM = 64
SOFTMAX_SCALE = (1.0 + 0.1 * math.log(40.0)) ** 2 / math.sqrt(192.0)
EXP2_SCALE = SOFTMAX_SCALE * math.log2(math.e)
BLOCK = 512
LANES = 128


def order(owners):
    return [0] + list(range(owners - 1, 0, -1))


def attend_kernel(owners, lengths_hbm, query_hbm, scales_hbm, cache, *refs):
    outs, refs = refs[:owners], refs[owners:]
    latents, lengths, query, scales, keys, scaled, scores, weights, sems, small_sems = refs
    requests, channels, heads = query.shape
    local_heads, rank = latents.shape[2:]
    cache_len = cache.shape[2]
    block = min(BLOCK, cache_len)
    blocks = cache_len // block
    me = lax.axis_index("tp")

    def fetch(r, b):
        span = pl.ds(b * block, block)
        return pltpu.make_async_copy(cache.at[r, :, span], keys.at[r, :, span], sems.at[r, b])

    small = [
        pltpu.make_async_copy(source, target, small_sems.at[i])
        for i, (source, target) in enumerate(
            [(lengths_hbm, lengths), (query_hbm, query), (scales_hbm, scales)]
        )
    ]
    for copy in small:
        copy.start()
    for b in range(blocks):
        for r in range(requests):
            fetch(r, b).start()
    small[1].wait()
    small[2].wait()
    scale_row = scales[...].reshape(1, channels)
    for r in range(requests):
        scaled[r] = (query[r].astype(jnp.float32).T * scale_row).astype(jnp.bfloat16)
    small[0].wait()

    def score(slot, r, live):
        top = None
        for b in range(live):
            fetch(r, b).wait()
            span = slice(b * block, (b + 1) * block)
            part = jnp.dot(scaled[r], keys[r, :, span], preferred_element_type=jnp.float32)
            if b == live - 1:
                place = b * block + lax.broadcasted_iota(jnp.int32, part.shape, 1)
                part = jnp.where(place < lengths[r], part, -jnp.inf)
            scores[slot, :, span] = part
            high = jnp.max(part, axis=1, keepdims=True)
            top = high if top is None else jnp.maximum(top, high)
        return top

    def weigh(slot, live, top):
        total = jnp.zeros_like(top)
        for b in range(live):
            span = slice(b * block, (b + 1) * block)
            weight = jnp.exp2((scores[slot, :, span] - top) * EXP2_SCALE)
            total += jnp.sum(weight, axis=1, keepdims=True)
            weights[slot, :, span] = weight.astype(jnp.bfloat16)
        return total

    def mix(slot, r, live):
        return lax.dot_general(
            weights[slot, :, :live * block], keys[r, :rank, :live * block],
            (((1,), (1,)), ((), ())), preferred_element_type=jnp.float32,
        )

    def finish(r, mixture, total):
        latent = (mixture * (1.0 / total) * scale_row[:, :rank]).astype(jnp.bfloat16)
        for d in range(owners):
            latents[d, r] = latent[d * local_heads:(d + 1) * local_heads]

    def pair(r, s, live_r, live_s):
        top_r = score(0, r, live_r)
        top_s = score(1, s, live_s)
        total_r = weigh(0, live_r, top_r)
        mixture_r = mix(0, r, live_r)
        total_s = weigh(1, live_s, top_s)
        finish(r, mixture_r, total_r)
        mixture_s = mix(1, s, live_s)
        finish(s, mixture_s, total_s)
        for b in range(live_r, blocks):
            fetch(r, b).wait()
        for b in range(live_s, blocks):
            fetch(s, b).wait()

    for first in range(0, requests, 2):
        swap = (lengths[first] < lengths[first + 1]).astype(jnp.int32)
        longer, shorter = first + swap, first + 1 - swap
        live = [(lengths[r] + (block - 1)) // block for r in (longer, shorter)]
        for live_r in range(1, blocks + 1):
            for live_s in range(1, live_r + 1):
                @pl.when((live[0] == live_r) & (live[1] == live_s))
                def _():
                    pair(longer, shorter, live_r, live_s)

    for out, k in zip(outs, order(owners)):
        out[...] = latents[me ^ k]


def in_hbm(*arrays):
    return [pltpu.with_memory_space_constraint(array, pltpu.HBM) for array in arrays]


def attend(query, cache, scales, lengths, owners):
    requests, heads, channels = query.shape
    cache_len = cache.shape[1]
    rank = channels - ROPE_DIM
    part = jax.ShapeDtypeStruct((requests, heads // owners, rank), jnp.bfloat16)
    return pl.pallas_call(
        functools.partial(attend_kernel, owners),
        out_shape=[part] * owners,
        in_specs=[pl.BlockSpec(memory_space=pl.ANY)] * 4,
        out_specs=[pl.BlockSpec(memory_space=pltpu.VMEM)] * owners,
        scratch_shapes=[
            pltpu.VMEM((owners,) + part.shape, part.dtype),
            pltpu.SMEM((requests,), jnp.int32),
            pltpu.VMEM((requests, channels, heads), jnp.bfloat16),
            pltpu.VMEM((channels,), jnp.float32),
            pltpu.VMEM((requests, channels, cache_len), jnp.bfloat16),
            pltpu.VMEM((requests, heads, channels), jnp.bfloat16),
            pltpu.VMEM((2, heads, cache_len), jnp.float32),
            pltpu.VMEM((2, heads, cache_len), jnp.bfloat16),
            pltpu.SemaphoreType.DMA((requests, cache_len // min(BLOCK, cache_len))),
            pltpu.SemaphoreType.DMA((3,)),
        ],
        compiler_params=pltpu.CompilerParams(vmem_limit_bytes=24 * 2**20),
        cost_estimate=pl.CostEstimate(
            flops=4 * requests * heads * channels * cache_len,
            bytes_accessed=2 * requests * channels * cache_len,
            transcendentals=requests * heads * cache_len,
        ),
        name="attend",
    )(*in_hbm(lengths, jnp.swapaxes(query, 1, 2), scales, jnp.swapaxes(cache, 1, 2)))


def stage_kernel(maps_hbm, after, maps, sems):
    count = sems.shape[0]
    size = maps.shape[0] // count
    copies = [
        pltpu.make_async_copy(
            maps_hbm.at[pl.ds(i * size, size)], maps.at[pl.ds(i * size, size)], sems.at[i]
        )
        for i in range(count)
    ]
    for copy in copies:
        copy.start()
    for copy in copies:
        copy.wait()


def stage(maps, after):
    return pl.pallas_call(
        stage_kernel,
        out_shape=jax.ShapeDtypeStruct(maps.shape, maps.dtype),
        in_specs=[pl.BlockSpec(memory_space=pl.ANY)] * 2,
        out_specs=pl.BlockSpec(memory_space=pltpu.VMEM),
        scratch_shapes=[pltpu.SemaphoreType.DMA((math.gcd(maps.shape[0], 8),))],
        compiler_params=pltpu.CompilerParams(vmem_limit_bytes=8 * 2**20),
        cost_estimate=pl.CostEstimate(
            flops=0, bytes_accessed=4 * maps.size, transcendentals=0
        ),
        name="stage",
    )(*in_hbm(maps), after)


def project_kernel(count, *refs):
    parts, maps, outs, rows = refs[:count], refs[count], refs[-1 - count:-1], refs[-1]
    requests, local_heads, rank = parts[0].shape
    width = maps.shape[2]
    batch = count * requests
    group = min(max(1, 16 // batch), local_heads)
    for b in range(batch):
        for k in range(rank // LANES):
            rows[k, b * local_heads:(b + 1) * local_heads] = parts[b // requests][
                b % requests, :, k * LANES:(k + 1) * LANES
            ].astype(jnp.float32)
    for first in range(0, local_heads, group):
        heads = range(first, first + group)
        mixed = jnp.concatenate(
            [
                jnp.concatenate(
                    [rows[k, pl.ds(h, batch, stride=local_heads), :] for h in heads], axis=0
                ).astype(jnp.bfloat16)
                for k in range(rank // LANES)
            ],
            axis=1,
        )
        wide = jnp.concatenate([maps[h] for h in heads], axis=1)
        values = jnp.dot(mixed, wide, preferred_element_type=jnp.float32)
        for i, h in enumerate(heads):
            own = values[i * batch:(i + 1) * batch, i * width:(i + 1) * width]
            for d, out in enumerate(outs):
                out[h] = own[d * requests:(d + 1) * requests].astype(jnp.bfloat16)


def project(parts, maps, earlier):
    count = len(parts)
    requests, local_heads, rank = parts[0].shape
    width = maps.shape[2]
    return pl.pallas_call(
        functools.partial(project_kernel, count),
        out_shape=[jax.ShapeDtypeStruct((local_heads, requests, width), jnp.bfloat16)] * count,
        in_specs=[pl.BlockSpec(memory_space=pltpu.VMEM)] * (count + 1)
        + [pl.BlockSpec(memory_space=pl.ANY)] * len(earlier),
        out_specs=[pl.BlockSpec(memory_space=pltpu.VMEM)] * count,
        scratch_shapes=[pltpu.VMEM((rank // LANES, count * requests * local_heads, LANES), jnp.float32)],
        compiler_params=pltpu.CompilerParams(vmem_limit_bytes=24 * 2**20),
        cost_estimate=pl.CostEstimate(
            flops=2 * count * requests * local_heads * rank * width,
            bytes_accessed=2 * local_heads * rank * width,
            transcendentals=0,
        ),
        name="project",
    )(*parts, maps, *earlier)


def assemble_kernel(partners, *refs):
    parts, (out, sems) = refs[:len(partners)], refs[-2:]
    me = lax.axis_index("tp")
    copies = [
        pltpu.make_async_copy(part, out.at[me ^ k], sems.at[i])
        for i, (k, part) in enumerate(zip(partners, parts))
    ]
    for copy in copies:
        copy.start()
    for copy in copies:
        copy.wait()


def assemble(parts, partners, owners, begun):
    return pl.pallas_call(
        functools.partial(assemble_kernel, partners),
        out_shape=pltpu.HBM((owners,) + parts[0].shape, parts[0].dtype),
        in_specs=[pl.BlockSpec(memory_space=pltpu.VMEM)] * len(parts)
        + [pl.BlockSpec(memory_space=pltpu.HBM)] * len(begun),
        out_specs=pl.BlockSpec(memory_space=pltpu.HBM),
        scratch_shapes=[pltpu.SemaphoreType.DMA((len(parts),))],
        input_output_aliases={len(parts): 0} if begun else {},
        compiler_params=pltpu.CompilerParams(vmem_limit_bytes=2 * 2**20),
        name="assemble",
    )(*parts, *begun)


def exchange(parts, partners, owners):
    return [
        lax.ppermute(part, "tp", [(i, i ^ k) for i in range(owners)]) if k else part
        for k, part in zip(partners, parts)
    ]


def on_device(query, cache, scales, lengths, value_up):
    owners = lax.axis_size("tp")
    latents = attend(query, cache, scales, lengths, owners)
    maps = stage(value_up, latents[0])
    partners = order(owners)
    received = exchange(latents, partners, owners)
    groups = [slice(0, owners // 2), slice(owners // 2, owners)]
    values = []
    for some in groups:
        earlier = values[0][:1] if values else []
        values.append(exchange(project(received[some], maps, earlier), partners[some], owners))
    begun = []
    for some, parts in zip(groups, values):
        begun = [assemble(parts, partners[some], owners, begun)]
    returned = begun[0]
    _, local_heads, requests, width = returned.shape
    returned = returned.reshape(owners * local_heads, requests, width)
    return jnp.swapaxes(returned, 0, 1).reshape(requests, owners * local_heads * width)


def solution(mesh):
    in_specs = (
        P(("grp", "tp"), None, None),
        P(("grp", "tp"), None, None),
        P(),
        P(("grp", "tp")),
        P("tp", None, None),
    )
    out_specs = P(("grp", "tp"), None)
    return jax.shard_map(
        on_device, mesh=mesh, in_specs=in_specs, out_specs=out_specs, check_vma=False
    )
```

```python
import functools
import math

import jax
import jax.numpy as jnp
from jax import lax
from jax.experimental import pallas as pl
from jax.experimental.pallas import tpu as pltpu
from jax.sharding import PartitionSpec as P

ROPE_DIM = 64
SOFTMAX_SCALE = (1.0 + 0.1 * math.log(40.0)) ** 2 / math.sqrt(192.0)
EXP2_SCALE = SOFTMAX_SCALE * math.log2(math.e)
BLOCK = 512
LANES = 128


def order(owners):
    return [0] + list(range(owners - 1, 0, -1))


def attend_kernel(owners, lengths_hbm, query_hbm, scales_hbm, cache, maps_hbm, *refs):
    outs, maps, refs = refs[:owners], refs[owners], refs[owners + 1:]
    latents, lengths, query, scales, keys, scaled, scores, weights, sems, small_sems = refs
    requests, channels, heads = query.shape
    local_heads, rank = latents.shape[2:]
    cache_len = cache.shape[2]
    block = min(BLOCK, cache_len)
    blocks = cache_len // block
    me = lax.axis_index("tp")

    def fetch(r, b):
        span = pl.ds(b * block, block)
        return pltpu.make_async_copy(cache.at[r, :, span], keys.at[r, :, span], sems.at[r, b])

    small = [
        pltpu.make_async_copy(source, target, small_sems.at[i])
        for i, (source, target) in enumerate(
            [(lengths_hbm, lengths), (query_hbm, query), (scales_hbm, scales)]
        )
    ]
    for copy in small:
        copy.start()
    for r in range(requests):
        fetch(r, 0).start()
    small[0].wait()
    pairs = []
    for first in range(0, requests, 2):
        swap = (lengths[first] < lengths[first + 1]).astype(jnp.int32)
        pairs.append((first + swap, first + 1 - swap))
    for r in [r for pair in pairs for r in pair]:
        for b in range(1, blocks):
            @pl.when(b * block < lengths[r])
            def _():
                fetch(r, b).start()
    maps_copy = pltpu.make_async_copy(maps_hbm, maps, small_sems.at[3])
    maps_copy.start()
    small[1].wait()
    small[2].wait()
    scale_row = scales[...].reshape(1, channels)
    for r in range(requests):
        scaled[r] = (query[r].astype(jnp.float32).T * scale_row).astype(jnp.bfloat16)

    def spread(column):
        return jnp.broadcast_to(column, (heads, LANES))

    def score(slot, r, live):
        top = None
        for b in range(live):
            fetch(r, b).wait()
            part = jnp.dot(
                scaled[r], keys[r, :, b * block:(b + 1) * block],
                preferred_element_type=jnp.float32,
            )
            if b == live - 1:
                place = b * block + lax.broadcasted_iota(jnp.int32, part.shape, 1)
                part = jnp.where(place < lengths[r], part, -jnp.inf)
            for at in range(0, block, LANES):
                piece = part[:, at:at + LANES]
                scores[slot, :, b * block + at:b * block + at + LANES] = piece
                top = piece if top is None else jnp.maximum(top, piece)
        return spread(jnp.max(top, axis=1, keepdims=True))

    def weigh(slot, live, top):
        total = None
        for at in range(0, live * block, LANES):
            weight = jnp.exp2((scores[slot, :, at:at + LANES] - top) * EXP2_SCALE)
            total = weight if total is None else total + weight
            weights[slot, :, at:at + LANES] = weight.astype(jnp.bfloat16)
        return jnp.sum(total, axis=1, keepdims=True)

    def mix(slot, r, live):
        return lax.dot_general(
            weights[slot, :, :live * block], keys[r, :rank, :live * block],
            (((1,), (1,)), ((), ())), preferred_element_type=jnp.float32,
        )

    def finish(r, mixture, total):
        latent = (mixture * (1.0 / total) * scale_row[:, :rank]).astype(jnp.bfloat16)
        for d in range(owners):
            latents[d, r] = latent[d * local_heads:(d + 1) * local_heads]

    def pair(r, s, live_r, live_s):
        top_r = score(0, r, live_r)
        top_s = score(1, s, live_s)
        total_r = weigh(0, live_r, top_r)
        mixture_r = mix(0, r, live_r)
        total_s = weigh(1, live_s, top_s)
        finish(r, mixture_r, total_r)
        mixture_s = mix(1, s, live_s)
        finish(s, mixture_s, total_s)

    for longer, shorter in pairs:
        live = [(lengths[r] + (block - 1)) // block for r in (longer, shorter)]
        for live_r in range(1, blocks + 1):
            for live_s in range(1, live_r + 1):
                @pl.when((live[0] == live_r) & (live[1] == live_s))
                def _():
                    pair(longer, shorter, live_r, live_s)

    for out, k in zip(outs, order(owners)):
        out[...] = latents[me ^ k]
    maps_copy.wait()


def in_hbm(*arrays):
    return [pltpu.with_memory_space_constraint(array, pltpu.HBM) for array in arrays]


def attend(query, cache, scales, lengths, maps, owners):
    requests, heads, channels = query.shape
    cache_len = cache.shape[1]
    rank = channels - ROPE_DIM
    part = jax.ShapeDtypeStruct((requests, heads // owners, rank), jnp.bfloat16)
    return pl.pallas_call(
        functools.partial(attend_kernel, owners),
        out_shape=[part] * owners + [jax.ShapeDtypeStruct(maps.shape, maps.dtype)],
        in_specs=[pl.BlockSpec(memory_space=pl.ANY)] * 5,
        out_specs=[pl.BlockSpec(memory_space=pltpu.VMEM)] * (owners + 1),
        scratch_shapes=[
            pltpu.VMEM((owners,) + part.shape, part.dtype),
            pltpu.SMEM((requests,), jnp.int32),
            pltpu.VMEM((requests, channels, heads), jnp.bfloat16),
            pltpu.VMEM((channels,), jnp.float32),
            pltpu.VMEM((requests, channels, cache_len), jnp.bfloat16),
            pltpu.VMEM((requests, heads, channels), jnp.bfloat16),
            pltpu.VMEM((2, heads, cache_len), jnp.float32),
            pltpu.VMEM((2, heads, cache_len), jnp.bfloat16),
            pltpu.SemaphoreType.DMA((requests, cache_len // min(BLOCK, cache_len))),
            pltpu.SemaphoreType.DMA((4,)),
        ],
        compiler_params=pltpu.CompilerParams(vmem_limit_bytes=24 * 2**20),
        cost_estimate=pl.CostEstimate(
            flops=4 * requests * heads * channels * cache_len,
            bytes_accessed=2 * requests * channels * cache_len,
            transcendentals=requests * heads * cache_len,
        ),
        name="attend",
    )(*in_hbm(lengths, jnp.swapaxes(query, 1, 2), scales, jnp.swapaxes(cache, 1, 2), maps))


def project_kernel(count, *refs):
    parts, maps, outs, rows = refs[:count], refs[count], refs[-1 - count:-1], refs[-1]
    requests, local_heads, rank = parts[0].shape
    width = maps.shape[2]
    batch = count * requests
    group = min(max(1, 16 // batch), local_heads)
    for b in range(batch):
        for k in range(rank // LANES):
            rows[k, b * local_heads:(b + 1) * local_heads] = parts[b // requests][
                b % requests, :, k * LANES:(k + 1) * LANES
            ].astype(jnp.float32)
    for first in range(0, local_heads, group):
        heads = range(first, first + group)
        mixed = jnp.concatenate(
            [
                jnp.concatenate(
                    [rows[k, pl.ds(h, batch, stride=local_heads), :] for h in heads], axis=0
                ).astype(jnp.bfloat16)
                for k in range(rank // LANES)
            ],
            axis=1,
        )
        wide = jnp.concatenate([maps[h] for h in heads], axis=1)
        values = jnp.dot(mixed, wide, preferred_element_type=jnp.float32)
        for i, h in enumerate(heads):
            own = values[i * batch:(i + 1) * batch, i * width:(i + 1) * width]
            for d, out in enumerate(outs):
                out[h] = own[d * requests:(d + 1) * requests].astype(jnp.bfloat16)


def project(parts, maps, earlier):
    count = len(parts)
    requests, local_heads, rank = parts[0].shape
    width = maps.shape[2]
    return pl.pallas_call(
        functools.partial(project_kernel, count),
        out_shape=[jax.ShapeDtypeStruct((local_heads, requests, width), jnp.bfloat16)] * count,
        in_specs=[pl.BlockSpec(memory_space=pltpu.VMEM)] * (count + 1)
        + [pl.BlockSpec(memory_space=pl.ANY)] * len(earlier),
        out_specs=[pl.BlockSpec(memory_space=pltpu.VMEM)] * count,
        scratch_shapes=[pltpu.VMEM((rank // LANES, count * requests * local_heads, LANES), jnp.float32)],
        compiler_params=pltpu.CompilerParams(vmem_limit_bytes=24 * 2**20),
        cost_estimate=pl.CostEstimate(
            flops=2 * count * requests * local_heads * rank * width,
            bytes_accessed=2 * local_heads * rank * width,
            transcendentals=0,
        ),
        name="project",
    )(*parts, maps, *earlier)


def assemble_kernel(partners, *refs):
    parts, (out, sems) = refs[:len(partners)], refs[-2:]
    me = lax.axis_index("tp")
    copies = [
        pltpu.make_async_copy(part, out.at[me ^ k], sems.at[i])
        for i, (k, part) in enumerate(zip(partners, parts))
    ]
    for copy in copies:
        copy.start()
    for copy in copies:
        copy.wait()


def assemble(parts, partners, owners, begun):
    return pl.pallas_call(
        functools.partial(assemble_kernel, partners),
        out_shape=pltpu.HBM((owners,) + parts[0].shape, parts[0].dtype),
        in_specs=[pl.BlockSpec(memory_space=pltpu.VMEM)] * len(parts)
        + [pl.BlockSpec(memory_space=pltpu.HBM)] * len(begun),
        out_specs=pl.BlockSpec(memory_space=pltpu.HBM),
        scratch_shapes=[pltpu.SemaphoreType.DMA((len(parts),))],
        input_output_aliases={len(parts): 0} if begun else {},
        compiler_params=pltpu.CompilerParams(vmem_limit_bytes=2 * 2**20),
        name="assemble",
    )(*parts, *begun)


def exchange(parts, partners, owners):
    return [
        lax.ppermute(part, "tp", [(i, i ^ k) for i in range(owners)]) if k else part
        for k, part in zip(partners, parts)
    ]


def on_device(query, cache, scales, lengths, value_up):
    owners = lax.axis_size("tp")
    *latents, maps = attend(query, cache, scales, lengths, value_up, owners)
    partners = order(owners)
    received = exchange(latents, partners, owners)
    groups = [slice(0, owners // 2), slice(owners // 2, owners)]
    values = []
    for some in groups:
        earlier = values[0][:1] if values else []
        values.append(exchange(project(received[some], maps, earlier), partners[some], owners))
    begun = []
    for some, parts in zip(groups, values):
        begun = [assemble(parts, partners[some], owners, begun)]
    returned = begun[0]
    _, local_heads, requests, width = returned.shape
    returned = returned.reshape(owners * local_heads, requests, width)
    return jnp.swapaxes(returned, 0, 1).reshape(requests, owners * local_heads * width)


def solution(mesh):
    in_specs = (
        P(("grp", "tp"), None, None),
        P(("grp", "tp"), None, None),
        P(),
        P(("grp", "tp")),
        P("tp", None, None),
    )
    out_specs = P(("grp", "tp"), None)
    return jax.shard_map(
        on_device, mesh=mesh, in_specs=in_specs, out_specs=out_specs, check_vma=False
    )
```

```python
import functools
import math

import jax
import jax.numpy as jnp
from jax import lax
from jax.experimental import pallas as pl
from jax.experimental.pallas import tpu as pltpu
from jax.sharding import PartitionSpec as P

ROPE_DIM = 64
SOFTMAX_SCALE = (1.0 + 0.1 * math.log(40.0)) ** 2 / math.sqrt(192.0)
EXP2_SCALE = SOFTMAX_SCALE * math.log2(math.e)
BLOCK = 512
LANES = 128


def order(owners):
    return [0] + list(range(owners - 1, 0, -1))


def attend_kernel(owners, lengths_hbm, query_hbm, scales_hbm, cache, *refs):
    outs, (latents, lengths, query, scales, keys, sems, small_sems) = refs[:owners], refs[owners:]
    requests, channels, heads = query.shape
    local_heads, rank = latents.shape[2:]
    cache_len = cache.shape[2]
    block = min(BLOCK, cache_len)
    blocks = cache_len // block
    me = lax.axis_index("tp")

    def fetch(r, b):
        span = pl.ds(b * block, block)
        return pltpu.make_async_copy(cache.at[r, :, span], keys.at[r, :, span], sems.at[r, b])

    small = [
        pltpu.make_async_copy(source, target, small_sems.at[i])
        for i, (source, target) in enumerate(
            [(lengths_hbm, lengths), (query_hbm, query), (scales_hbm, scales)]
        )
    ]
    for copy in small:
        copy.start()
    fetch(0, 0).start()
    small[0].wait()
    for r in range(requests):
        for b in range(blocks):
            if (r, b) != (0, 0):
                @pl.when(b * block < lengths[r])
                def _():
                    fetch(r, b).start()
    small[1].wait()
    small[2].wait()

    scale_row = scales[...].reshape(1, channels)

    def request(r, live):
        scaled = (query[r].astype(jnp.float32).T * scale_row).astype(jnp.bfloat16)
        parts = []
        for b in range(live):
            fetch(r, b).wait()
            part = jnp.dot(
                scaled, keys[r, :, b * block:(b + 1) * block],
                preferred_element_type=jnp.float32,
            )
            if b == live - 1:
                place = b * block + lax.broadcasted_iota(jnp.int32, part.shape, 1)
                part = jnp.where(place < lengths[r], part, -jnp.inf)
            parts.append(part)
        top = jnp.max(parts[0], axis=1, keepdims=True)
        for part in parts[1:]:
            top = jnp.maximum(top, jnp.max(part, axis=1, keepdims=True))
        total = jnp.zeros_like(top)
        weights = []
        for part in parts:
            weight = jnp.exp2((part - top) * EXP2_SCALE)
            total += jnp.sum(weight, axis=1, keepdims=True)
            weights.append(weight.astype(jnp.bfloat16))
        mixture = lax.dot_general(
            jnp.concatenate(weights, axis=1), keys[r, :rank, :live * block],
            (((1,), (1,)), ((), ())), preferred_element_type=jnp.float32,
        )
        latent = (mixture * (1.0 / total) * scale_row[:, :rank]).astype(jnp.bfloat16)
        for d in range(owners):
            latents[d, r] = latent[d * local_heads:(d + 1) * local_heads]

    for r in range(requests):
        for live in range(1, blocks + 1):
            @pl.when((lengths[r] > (live - 1) * block) & (lengths[r] <= live * block))
            def _():
                request(r, live)

    for out, k in zip(outs, order(owners)):
        out[...] = latents[me ^ k]


def in_hbm(*arrays):
    return [pltpu.with_memory_space_constraint(array, pltpu.HBM) for array in arrays]


def attend(query, cache, scales, lengths, owners):
    requests, heads, channels = query.shape
    cache_len = cache.shape[1]
    rank = channels - ROPE_DIM
    part = jax.ShapeDtypeStruct((requests, heads // owners, rank), jnp.bfloat16)
    return pl.pallas_call(
        functools.partial(attend_kernel, owners),
        out_shape=[part] * owners,
        in_specs=[pl.BlockSpec(memory_space=pl.ANY)] * 4,
        out_specs=[pl.BlockSpec(memory_space=pltpu.VMEM)] * owners,
        scratch_shapes=[
            pltpu.VMEM((owners,) + part.shape, part.dtype),
            pltpu.SMEM((requests,), jnp.int32),
            pltpu.VMEM((requests, channels, heads), jnp.bfloat16),
            pltpu.VMEM((channels,), jnp.float32),
            pltpu.VMEM((requests, channels, cache_len), jnp.bfloat16),
            pltpu.SemaphoreType.DMA((requests, cache_len // min(BLOCK, cache_len))),
            pltpu.SemaphoreType.DMA((3,)),
        ],
        compiler_params=pltpu.CompilerParams(vmem_limit_bytes=24 * 2**20),
        cost_estimate=pl.CostEstimate(
            flops=4 * requests * heads * channels * cache_len,
            bytes_accessed=2 * requests * channels * cache_len,
            transcendentals=requests * heads * cache_len,
        ),
        name="attend",
    )(*in_hbm(lengths, jnp.swapaxes(query, 1, 2), scales, jnp.swapaxes(cache, 1, 2)))


def stage_kernel(maps_hbm, after, maps, sem):
    copy = pltpu.make_async_copy(maps_hbm, maps, sem)
    copy.start()
    copy.wait()


def stage(maps, after):
    return pl.pallas_call(
        stage_kernel,
        out_shape=jax.ShapeDtypeStruct(maps.shape, maps.dtype),
        in_specs=[pl.BlockSpec(memory_space=pl.ANY)] * 2,
        out_specs=pl.BlockSpec(memory_space=pltpu.VMEM),
        scratch_shapes=[pltpu.SemaphoreType.DMA(())],
        compiler_params=pltpu.CompilerParams(vmem_limit_bytes=8 * 2**20),
        cost_estimate=pl.CostEstimate(
            flops=0, bytes_accessed=4 * maps.size, transcendentals=0
        ),
        name="stage",
    )(*in_hbm(maps), after)


def project_kernel(owners, *refs):
    parts, maps, outs, rows = refs[:owners], refs[owners], refs[owners + 1:-1], refs[-1]
    requests, local_heads, rank = parts[0].shape
    width = maps.shape[2]
    batch = owners * requests
    for b in range(batch):
        for k in range(rank // LANES):
            rows[k, b * local_heads:(b + 1) * local_heads] = parts[b // requests][
                b % requests, :, k * LANES:(k + 1) * LANES
            ].astype(jnp.float32)
    for h in range(0, local_heads, 2):
        pair = jnp.concatenate(
            [
                jnp.concatenate(
                    [rows[k, pl.ds(h + i, batch, stride=local_heads), :] for i in range(2)], axis=0
                ).astype(jnp.bfloat16)
                for k in range(rank // LANES)
            ],
            axis=1,
        )
        both = jnp.concatenate([maps[h], maps[h + 1]], axis=1)
        values = jnp.dot(pair, both, preferred_element_type=jnp.float32)
        for i in range(2):
            mine = values[i * batch:(i + 1) * batch, i * width:(i + 1) * width]
            for d, out in enumerate(outs):
                out[h + i] = mine[d * requests:(d + 1) * requests].astype(jnp.bfloat16)


def project(latents, maps):
    owners = len(latents)
    requests, local_heads, rank = latents[0].shape
    width = maps.shape[2]
    return pl.pallas_call(
        functools.partial(project_kernel, owners),
        out_shape=[jax.ShapeDtypeStruct((local_heads, requests, width), jnp.bfloat16)] * owners,
        in_specs=[pl.BlockSpec(memory_space=pltpu.VMEM)] * (owners + 1),
        out_specs=[pl.BlockSpec(memory_space=pltpu.VMEM)] * owners,
        scratch_shapes=[pltpu.VMEM((rank // LANES, owners * requests * local_heads, LANES), jnp.float32)],
        compiler_params=pltpu.CompilerParams(vmem_limit_bytes=24 * 2**20),
        cost_estimate=pl.CostEstimate(
            flops=2 * owners * requests * local_heads * rank * width,
            bytes_accessed=2 * local_heads * rank * width,
            transcendentals=0,
        ),
        name="project",
    )(*latents, maps)


def assemble_kernel(owners, *refs):
    parts, out, sems = refs[:owners], refs[owners], refs[owners + 1]
    me = lax.axis_index("tp")
    copies = [
        pltpu.make_async_copy(part, out.at[me ^ k], sems.at[k])
        for k, part in zip(order(owners), parts)
    ]
    for copy in copies:
        copy.start()
    for copy in copies:
        copy.wait()


def assemble(parts):
    owners = len(parts)
    return pl.pallas_call(
        functools.partial(assemble_kernel, owners),
        out_shape=pltpu.HBM((owners,) + parts[0].shape, parts[0].dtype),
        in_specs=[pl.BlockSpec(memory_space=pltpu.VMEM)] * owners,
        out_specs=pl.BlockSpec(memory_space=pltpu.HBM),
        scratch_shapes=[pltpu.SemaphoreType.DMA((owners,))],
        compiler_params=pltpu.CompilerParams(vmem_limit_bytes=2 * 2**20),
        name="assemble",
    )(*parts)


def exchange(parts):
    owners = len(parts)
    return [
        lax.ppermute(part, "tp", [(i, i ^ k) for i in range(owners)]) if k else part
        for k, part in zip(order(owners), parts)
    ]


def on_device(query, cache, scales, lengths, value_up):
    owners = lax.axis_size("tp")
    latents = attend(query, cache, scales, lengths, owners)
    maps = stage(value_up, latents[0])
    values = exchange(project(exchange(latents), maps))
    returned = assemble(values)
    _, local_heads, requests, width = returned.shape
    returned = returned.reshape(owners * local_heads, requests, width)
    return jnp.swapaxes(returned, 0, 1).reshape(requests, owners * local_heads * width)


def solution(mesh):
    in_specs = (
        P(("grp", "tp"), None, None),
        P(("grp", "tp"), None, None),
        P(),
        P(("grp", "tp")),
        P("tp", None, None),
    )
    out_specs = P(("grp", "tp"), None)
    return jax.shard_map(
        on_device, mesh=mesh, in_specs=in_specs, out_specs=out_specs, check_vma=False
    )
```

```python
import functools
import math

import jax
import jax.numpy as jnp
from jax import lax
from jax.experimental import pallas as pl
from jax.experimental.pallas import tpu as pltpu
from jax.sharding import PartitionSpec as P

ROPE_DIM = 64
SOFTMAX_SCALE = (1.0 + 0.1 * math.log(40.0)) ** 2 / math.sqrt(192.0)
EXP2_SCALE = SOFTMAX_SCALE * math.log2(math.e)
BLOCK = 512
LANES = 128
GROUP_ROWS = 16


def order(owners):
    return [0] + list(range(owners - 1, 0, -1))


def attend_kernel(owners, lengths_hbm, query_hbm, scales_hbm, cache, *refs):
    outs, (latents, lengths, query, scales, keys, sems, small_sems) = refs[:owners], refs[owners:]
    requests, channels, heads = query.shape
    rows, rank = outs[0].shape
    cache_len = cache.shape[2]
    block = min(BLOCK, cache_len)
    blocks = cache_len // block
    me = lax.axis_index("tp")

    def fetch(r, b):
        span = pl.ds(b * block, block)
        return pltpu.make_async_copy(cache.at[r, :, span], keys.at[r, :, span], sems.at[r, b])

    small = [
        pltpu.make_async_copy(source, target, small_sems.at[i])
        for i, (source, target) in enumerate(
            [(lengths_hbm, lengths), (query_hbm, query), (scales_hbm, scales)]
        )
    ]
    for copy in small:
        copy.start()
    fetch(0, 0).start()
    small[0].wait()
    for r in range(requests):
        for b in range(blocks):
            if (r, b) != (0, 0):
                @pl.when(b * block < lengths[r])
                def _():
                    fetch(r, b).start()
    small[1].wait()
    small[2].wait()

    scale_row = scales[...].reshape(1, channels)

    def request(r, live):
        scaled = (query[r].astype(jnp.float32).T * scale_row).astype(jnp.bfloat16)
        parts = []
        for b in range(live):
            fetch(r, b).wait()
            part = jnp.dot(
                scaled, keys[r, :, b * block:(b + 1) * block],
                preferred_element_type=jnp.float32,
            )
            if b == live - 1:
                place = b * block + lax.broadcasted_iota(jnp.int32, part.shape, 1)
                part = jnp.where(place < lengths[r], part, -jnp.inf)
            parts.append(part)
        top = jnp.max(parts[0], axis=1, keepdims=True)
        for part in parts[1:]:
            top = jnp.maximum(top, jnp.max(part, axis=1, keepdims=True))
        total = jnp.zeros_like(top)
        weights = []
        for part in parts:
            weight = jnp.exp2((part - top) * EXP2_SCALE)
            total += jnp.sum(weight, axis=1, keepdims=True)
            weights.append(weight.astype(jnp.bfloat16))
        mixture = lax.dot_general(
            jnp.concatenate(weights, axis=1), keys[r, :rank, :live * block],
            (((1,), (1,)), ((), ())), preferred_element_type=jnp.float32,
        )
        latent = mixture * (1.0 / total) * scale_row[:, :rank]
        for at in range(0, rank, LANES):
            latents[at // LANES, pl.ds(r, heads, stride=requests), :] = latent[:, at:at + LANES]

    for r in range(requests):
        for live in range(1, blocks + 1):
            @pl.when((lengths[r] > (live - 1) * block) & (lengths[r] <= live * block))
            def _():
                request(r, live)

    for out, k in zip(outs, order(owners)):
        mine = pl.ds(pl.multiple_of((me ^ k) * rows, rows), rows)
        for at in range(0, rank, LANES):
            out[:, at:at + LANES] = latents[at // LANES, mine, :].astype(jnp.bfloat16)


def in_hbm(*arrays):
    return [pltpu.with_memory_space_constraint(array, pltpu.HBM) for array in arrays]


def attend(query, cache, scales, lengths, owners):
    requests, heads, channels = query.shape
    cache_len = cache.shape[1]
    rank = channels - ROPE_DIM
    part = jax.ShapeDtypeStruct((heads // owners * requests, rank), jnp.bfloat16)
    return pl.pallas_call(
        functools.partial(attend_kernel, owners),
        out_shape=[part] * owners,
        in_specs=[pl.BlockSpec(memory_space=pl.ANY)] * 4,
        out_specs=[pl.BlockSpec(memory_space=pltpu.VMEM)] * owners,
        scratch_shapes=[
            pltpu.VMEM((rank // LANES, heads * requests, LANES), jnp.float32),
            pltpu.SMEM((requests,), jnp.int32),
            pltpu.VMEM((requests, channels, heads), jnp.bfloat16),
            pltpu.VMEM((channels,), jnp.float32),
            pltpu.VMEM((requests, channels, cache_len), jnp.bfloat16),
            pltpu.SemaphoreType.DMA((requests, cache_len // min(BLOCK, cache_len))),
            pltpu.SemaphoreType.DMA((3,)),
        ],
        compiler_params=pltpu.CompilerParams(vmem_limit_bytes=24 * 2**20),
        cost_estimate=pl.CostEstimate(
            flops=4 * requests * heads * channels * cache_len,
            bytes_accessed=2 * requests * channels * cache_len,
            transcendentals=requests * heads * cache_len,
        ),
        name="attend",
    )(*in_hbm(lengths, jnp.swapaxes(query, 1, 2), scales, jnp.swapaxes(cache, 1, 2)))


def stage_kernel(maps_hbm, after, maps, sem):
    copy = pltpu.make_async_copy(maps_hbm, maps, sem)
    copy.start()
    copy.wait()


def stage(maps, after):
    return pl.pallas_call(
        stage_kernel,
        out_shape=jax.ShapeDtypeStruct(maps.shape, maps.dtype),
        in_specs=[pl.BlockSpec(memory_space=pl.ANY)] * 2,
        out_specs=pl.BlockSpec(memory_space=pltpu.VMEM),
        scratch_shapes=[pltpu.SemaphoreType.DMA(())],
        compiler_params=pltpu.CompilerParams(vmem_limit_bytes=8 * 2**20),
        cost_estimate=pl.CostEstimate(
            flops=0, bytes_accessed=4 * maps.size, transcendentals=0
        ),
        name="stage",
    )(*in_hbm(maps), after)


def project_kernel(count, *refs):
    parts, maps, outs = refs[:count], refs[count], refs[count + 1:]
    local_heads, requests, width = outs[0].shape
    group = min(GROUP_ROWS // requests, local_heads)
    rows = group * requests
    for first in range(0, local_heads, group):
        here = slice(first * requests, first * requests + rows)
        mixed = jnp.concatenate([part[here, :] for part in parts], axis=0)
        wide = jnp.concatenate([maps[first + i] for i in range(group)], axis=1)
        values = jnp.dot(mixed, wide, preferred_element_type=jnp.float32)
        head = lax.broadcasted_iota(jnp.int32, (rows, width), 0) // requests
        for d, out in enumerate(outs):
            block = values[d * rows:(d + 1) * rows]
            own = block[:, :width]
            for i in range(1, group):
                own = jnp.where(head == i, block[:, i * width:(i + 1) * width], own)
            out[first:first + group] = own.astype(jnp.bfloat16).reshape(group, requests, width)


def project(parts, maps, requests):
    count = len(parts)
    local_heads, rank, width = maps.shape
    return pl.pallas_call(
        functools.partial(project_kernel, count),
        out_shape=[jax.ShapeDtypeStruct((local_heads, requests, width), jnp.bfloat16)] * count,
        in_specs=[pl.BlockSpec(memory_space=pltpu.VMEM)] * (count + 1),
        out_specs=[pl.BlockSpec(memory_space=pltpu.VMEM)] * count,
        compiler_params=pltpu.CompilerParams(vmem_limit_bytes=24 * 2**20),
        cost_estimate=pl.CostEstimate(
            flops=2 * count * requests * local_heads * rank * width,
            bytes_accessed=2 * local_heads * rank * width,
            transcendentals=0,
        ),
        name="project",
    )(*parts, maps)


def assemble_kernel(owners, *refs):
    parts, out, sems = refs[:owners], refs[owners], refs[owners + 1]
    me = lax.axis_index("tp")
    copies = [
        pltpu.make_async_copy(part, out.at[me ^ k], sems.at[k])
        for k, part in zip(order(owners), parts)
    ]
    for copy in copies:
        copy.start()
    for copy in copies:
        copy.wait()


def assemble(parts):
    owners = len(parts)
    return pl.pallas_call(
        functools.partial(assemble_kernel, owners),
        out_shape=pltpu.HBM((owners,) + parts[0].shape, parts[0].dtype),
        in_specs=[pl.BlockSpec(memory_space=pltpu.VMEM)] * owners,
        out_specs=pl.BlockSpec(memory_space=pltpu.HBM),
        scratch_shapes=[pltpu.SemaphoreType.DMA((owners,))],
        compiler_params=pltpu.CompilerParams(vmem_limit_bytes=2 * 2**20),
        name="assemble",
    )(*parts)


def exchange(parts):
    owners = len(parts)
    return [
        lax.ppermute(part, "tp", [(i, i ^ k) for i in range(owners)]) if k else part
        for k, part in zip(order(owners), parts)
    ]


def on_device(query, cache, scales, lengths, value_up):
    owners = lax.axis_size("tp")
    latents = attend(query, cache, scales, lengths, owners)
    maps = stage(value_up, latents[0])
    values = exchange(project(exchange(latents), maps, query.shape[0]))
    returned = assemble(values)
    _, local_heads, requests, width = returned.shape
    returned = returned.reshape(owners * local_heads, requests, width)
    return jnp.swapaxes(returned, 0, 1).reshape(requests, owners * local_heads * width)


def solution(mesh):
    in_specs = (
        P(("grp", "tp"), None, None),
        P(("grp", "tp"), None, None),
        P(),
        P(("grp", "tp")),
        P("tp", None, None),
    )
    out_specs = P(("grp", "tp"), None)
    return jax.shard_map(
        on_device, mesh=mesh, in_specs=in_specs, out_specs=out_specs, check_vma=False
    )
```

```python
import functools
import itertools
import math

import jax
import jax.numpy as jnp
from jax import lax
from jax.experimental import pallas as pl
from jax.experimental.pallas import tpu as pltpu
from jax.sharding import PartitionSpec as P

ROPE_DIM = 64
SOFTMAX_SCALE = (1.0 + 0.1 * math.log(40.0)) ** 2 / math.sqrt(192.0)
EXP2_SCALE = SOFTMAX_SCALE * math.log2(math.e)
BLOCK = 512
LANES = 128
GROUP_ROWS = 16


def order(owners):
    return [0] + list(range(owners - 1, 0, -1))


def attend_kernel(owners, lengths_hbm, query_hbm, scales_hbm, cache, *refs):
    outs, (latents, lengths, query, scales, keys, sems, small_sems) = refs[:owners], refs[owners:]
    requests, channels, heads = query.shape
    rows, rank = outs[0].shape
    cache_len = cache.shape[2]
    block = min(BLOCK, cache_len)
    blocks = cache_len // block
    me = lax.axis_index("tp")

    def fetch(r, b):
        span = pl.ds(b * block, block)
        return pltpu.make_async_copy(cache.at[r, :, span], keys.at[r, :, span], sems.at[r, b])

    small = [
        pltpu.make_async_copy(source, target, small_sems.at[i])
        for i, (source, target) in enumerate(
            [(lengths_hbm, lengths), (query_hbm, query), (scales_hbm, scales)]
        )
    ]
    for copy in small:
        copy.start()
    for r in range(requests):
        fetch(r, 0).start()
    small[0].wait()
    for r in range(requests):
        for b in range(1, blocks):
            @pl.when(b * block < lengths[r])
            def _():
                fetch(r, b).start()
    small[1].wait()
    small[2].wait()

    scale_row = scales[...].reshape(1, channels)

    def score(scaled, r, b, live):
        fetch(r, b).wait()
        part = jnp.dot(
            scaled[r], keys[r, :, b * block:(b + 1) * block], preferred_element_type=jnp.float32
        )
        if b == live - 1:
            place = b * block + lax.broadcasted_iota(jnp.int32, part.shape, 1)
            part = jnp.where(place < lengths[r], part, -jnp.inf)
        return part

    def weigh(part, r, b):
        top = jnp.max(part, axis=1, keepdims=True)
        weight = jnp.exp2((part - top) * EXP2_SCALE)
        total = jnp.sum(weight, axis=1, keepdims=True)
        mixture = lax.dot_general(
            weight.astype(jnp.bfloat16), keys[r, :rank, b * block:(b + 1) * block],
            (((1,), (1,)), ((), ())), preferred_element_type=jnp.float32,
        )
        return top, total, mixture

    def merge(one, two):
        top = jnp.maximum(one[0], two[0])
        first = jnp.exp2((one[0] - top) * EXP2_SCALE)
        second = jnp.exp2((two[0] - top) * EXP2_SCALE)
        return (top,) + tuple(x * first + y * second for x, y in zip(one[1:], two[1:]))

    def finish(r, total, mixture):
        latent = mixture * (1.0 / total) * scale_row[:, :rank]
        for at in range(0, rank, LANES):
            latents[at // LANES, pl.ds(r, heads, stride=requests), :] = latent[:, at:at + LANES]

    def several(group, live):
        scaled = {
            r: (query[r].astype(jnp.float32).T * scale_row).astype(jnp.bfloat16) for r in group
        }
        units = [(r, b, n) for r, n in zip(group, live) for b in range(n)]
        part = score(scaled, *units[0])
        state = None
        for i, (r, b, n) in enumerate(units):
            ahead = score(scaled, *units[i + 1]) if i + 1 < len(units) else None
            done = weigh(part, r, b)
            state = done if b == 0 else merge(state, done)
            if b == n - 1:
                finish(r, *state[1:])
            part = ahead

    for first in range(0, requests, 2):
        group = tuple(range(first, min(first + 2, requests)))
        count = [(lengths[r] + (block - 1)) // block for r in group]
        for live in itertools.product(range(1, blocks + 1), repeat=len(group)):
            @pl.when(functools.reduce(jnp.logical_and, [c == n for c, n in zip(count, live)]))
            def _():
                several(group, live)

    for out, k in zip(outs, order(owners)):
        mine = pl.ds(pl.multiple_of((me ^ k) * rows, rows), rows)
        for at in range(0, rank, LANES):
            out[:, at:at + LANES] = latents[at // LANES, mine, :].astype(jnp.bfloat16)


def in_hbm(*arrays):
    return [pltpu.with_memory_space_constraint(array, pltpu.HBM) for array in arrays]


def attend(query, cache, scales, lengths, owners):
    requests, heads, channels = query.shape
    cache_len = cache.shape[1]
    rank = channels - ROPE_DIM
    part = jax.ShapeDtypeStruct((heads // owners * requests, rank), jnp.bfloat16)
    return pl.pallas_call(
        functools.partial(attend_kernel, owners),
        out_shape=[part] * owners,
        in_specs=[pl.BlockSpec(memory_space=pl.ANY)] * 4,
        out_specs=[pl.BlockSpec(memory_space=pltpu.VMEM)] * owners,
        scratch_shapes=[
            pltpu.VMEM((rank // LANES, heads * requests, LANES), jnp.float32),
            pltpu.SMEM((requests,), jnp.int32),
            pltpu.VMEM((requests, channels, heads), jnp.bfloat16),
            pltpu.VMEM((channels,), jnp.float32),
            pltpu.VMEM((requests, channels, cache_len), jnp.bfloat16),
            pltpu.SemaphoreType.DMA((requests, cache_len // min(BLOCK, cache_len))),
            pltpu.SemaphoreType.DMA((3,)),
        ],
        compiler_params=pltpu.CompilerParams(vmem_limit_bytes=24 * 2**20),
        cost_estimate=pl.CostEstimate(
            flops=4 * requests * heads * channels * cache_len,
            bytes_accessed=2 * requests * channels * cache_len,
            transcendentals=requests * heads * cache_len,
        ),
        name="attend",
    )(*in_hbm(lengths, jnp.swapaxes(query, 1, 2), scales, jnp.swapaxes(cache, 1, 2)))


def stage_kernel(maps_hbm, after, maps, sem):
    copy = pltpu.make_async_copy(maps_hbm, maps, sem)
    copy.start()
    copy.wait()


def stage(maps, after):
    return pl.pallas_call(
        stage_kernel,
        out_shape=jax.ShapeDtypeStruct(maps.shape, maps.dtype),
        in_specs=[pl.BlockSpec(memory_space=pl.ANY)] * 2,
        out_specs=pl.BlockSpec(memory_space=pltpu.VMEM),
        scratch_shapes=[pltpu.SemaphoreType.DMA(())],
        compiler_params=pltpu.CompilerParams(vmem_limit_bytes=8 * 2**20),
        cost_estimate=pl.CostEstimate(
            flops=0, bytes_accessed=4 * maps.size, transcendentals=0
        ),
        name="stage",
    )(*in_hbm(maps), after)


def project_kernel(count, *refs):
    parts, maps, outs = refs[:count], refs[count], refs[count + 1:]
    local_heads, requests, width = outs[0].shape
    group = min(GROUP_ROWS // requests, local_heads)
    rows = group * requests
    for first in range(0, local_heads, group):
        here = slice(first * requests, first * requests + rows)
        mixed = jnp.concatenate([part[here, :] for part in parts], axis=0)
        wide = jnp.concatenate([maps[first + i] for i in range(group)], axis=1)
        values = jnp.dot(mixed, wide, preferred_element_type=jnp.float32)
        head = lax.broadcasted_iota(jnp.int32, (rows, width), 0) // requests
        for d, out in enumerate(outs):
            block = values[d * rows:(d + 1) * rows]
            own = block[:, :width]
            for i in range(1, group):
                own = jnp.where(head == i, block[:, i * width:(i + 1) * width], own)
            out[first:first + group] = own.astype(jnp.bfloat16).reshape(group, requests, width)


def project(parts, maps, requests):
    count = len(parts)
    local_heads, rank, width = maps.shape
    return pl.pallas_call(
        functools.partial(project_kernel, count),
        out_shape=[jax.ShapeDtypeStruct((local_heads, requests, width), jnp.bfloat16)] * count,
        in_specs=[pl.BlockSpec(memory_space=pltpu.VMEM)] * (count + 1),
        out_specs=[pl.BlockSpec(memory_space=pltpu.VMEM)] * count,
        compiler_params=pltpu.CompilerParams(vmem_limit_bytes=24 * 2**20),
        cost_estimate=pl.CostEstimate(
            flops=2 * count * requests * local_heads * rank * width,
            bytes_accessed=2 * local_heads * rank * width,
            transcendentals=0,
        ),
        name="project",
    )(*parts, maps)


def assemble_kernel(owners, *refs):
    parts, out, sems = refs[:owners], refs[owners], refs[owners + 1]
    me = lax.axis_index("tp")
    copies = [
        pltpu.make_async_copy(part, out.at[me ^ k], sems.at[k])
        for k, part in zip(order(owners), parts)
    ]
    for copy in copies:
        copy.start()
    for copy in copies:
        copy.wait()


def assemble(parts):
    owners = len(parts)
    return pl.pallas_call(
        functools.partial(assemble_kernel, owners),
        out_shape=pltpu.HBM((owners,) + parts[0].shape, parts[0].dtype),
        in_specs=[pl.BlockSpec(memory_space=pltpu.VMEM)] * owners,
        out_specs=pl.BlockSpec(memory_space=pltpu.HBM),
        scratch_shapes=[pltpu.SemaphoreType.DMA((owners,))],
        compiler_params=pltpu.CompilerParams(vmem_limit_bytes=2 * 2**20),
        name="assemble",
    )(*parts)


def exchange(parts):
    owners = len(parts)
    return [
        lax.ppermute(part, "tp", [(i, i ^ k) for i in range(owners)]) if k else part
        for k, part in zip(order(owners), parts)
    ]


def on_device(query, cache, scales, lengths, value_up):
    owners = lax.axis_size("tp")
    latents = attend(query, cache, scales, lengths, owners)
    maps = stage(value_up, latents[0])
    values = exchange(project(exchange(latents), maps, query.shape[0]))
    returned = assemble(values)
    _, local_heads, requests, width = returned.shape
    returned = returned.reshape(owners * local_heads, requests, width)
    return jnp.swapaxes(returned, 0, 1).reshape(requests, owners * local_heads * width)


def solution(mesh):
    in_specs = (
        P(("grp", "tp"), None, None),
        P(("grp", "tp"), None, None),
        P(),
        P(("grp", "tp")),
        P("tp", None, None),
    )
    out_specs = P(("grp", "tp"), None)
    return jax.shard_map(
        on_device, mesh=mesh, in_specs=in_specs, out_specs=out_specs, check_vma=False
    )
```

```python
import functools
import itertools
import math

import jax
import jax.numpy as jnp
from jax import lax
from jax.experimental import pallas as pl
from jax.experimental.pallas import tpu as pltpu
from jax.sharding import PartitionSpec as P

ROPE_DIM = 64
SOFTMAX_SCALE = (1.0 + 0.1 * math.log(40.0)) ** 2 / math.sqrt(192.0)
EXP2_SCALE = SOFTMAX_SCALE * math.log2(math.e)
BLOCK = 512
EAGER = 2
LANES = 128
GROUP_ROWS = 16


def order(owners):
    return [0] + list(range(owners - 1, 0, -1))


def attend_kernel(owners, lengths_hbm, query_hbm, scales_hbm, cache, *refs):
    outs, (latents, lengths, query, scales, keys, sems, small_sems) = refs[:owners], refs[owners:]
    requests, channels, heads = query.shape
    rows, rank = outs[0].shape
    cache_len = cache.shape[2]
    block = min(BLOCK, cache_len)
    blocks = cache_len // block
    me = lax.axis_index("tp")

    def fetch(r, b):
        span = pl.ds(b * block, block)
        return pltpu.make_async_copy(cache.at[r, :, span], keys.at[r, :, span], sems.at[r, b])

    small = [
        pltpu.make_async_copy(source, target, small_sems.at[i])
        for i, (source, target) in enumerate(
            [(lengths_hbm, lengths), (query_hbm, query), (scales_hbm, scales)]
        )
    ]
    for copy in small:
        copy.start()
    eager = min(EAGER, blocks)
    for b in range(eager):
        for r in range(requests):
            fetch(r, b).start()
    small[0].wait()
    for r in range(requests):
        for b in range(eager, blocks):
            @pl.when(b * block < lengths[r])
            def _():
                fetch(r, b).start()
    small[1].wait()
    small[2].wait()

    scale_row = scales[...].reshape(1, channels)

    def score(scaled, r, b, live):
        fetch(r, b).wait()
        part = jnp.dot(
            scaled[r], keys[r, :, b * block:(b + 1) * block], preferred_element_type=jnp.float32
        )
        if b == live - 1:
            place = b * block + lax.broadcasted_iota(jnp.int32, part.shape, 1)
            part = jnp.where(place < lengths[r], part, -jnp.inf)
        return part

    def weigh(part, r, b):
        top = jnp.max(part, axis=1, keepdims=True)
        weight = jnp.exp2((part - top) * EXP2_SCALE)
        total = jnp.sum(weight, axis=1, keepdims=True)
        mixture = lax.dot_general(
            weight.astype(jnp.bfloat16), keys[r, :rank, b * block:(b + 1) * block],
            (((1,), (1,)), ((), ())), preferred_element_type=jnp.float32,
        )
        return top, total, mixture

    def merge(one, two):
        top = jnp.maximum(one[0], two[0])
        first = jnp.exp2((one[0] - top) * EXP2_SCALE)
        second = jnp.exp2((two[0] - top) * EXP2_SCALE)
        return (top,) + tuple(x * first + y * second for x, y in zip(one[1:], two[1:]))

    def finish(r, total, mixture):
        latent = mixture * (1.0 / total) * scale_row[:, :rank]
        for at in range(0, rank, LANES):
            latents[at // LANES, pl.ds(r, heads, stride=requests), :] = latent[:, at:at + LANES]

    def several(group, live):
        scaled = {
            r: (query[r].astype(jnp.float32).T * scale_row).astype(jnp.bfloat16) for r in group
        }
        units = [(r, b, n) for r, n in zip(group, live) for b in range(n)]
        part = score(scaled, *units[0])
        state = None
        for i, (r, b, n) in enumerate(units):
            ahead = score(scaled, *units[i + 1]) if i + 1 < len(units) else None
            done = weigh(part, r, b)
            state = done if b == 0 else merge(state, done)
            if b == n - 1:
                finish(r, *state[1:])
            part = ahead
        for r, n in zip(group, live):
            for b in range(n, eager):
                fetch(r, b).wait()

    for first in range(0, requests, 2):
        group = tuple(range(first, min(first + 2, requests)))
        count = [(lengths[r] + (block - 1)) // block for r in group]
        for live in itertools.product(range(1, blocks + 1), repeat=len(group)):
            @pl.when(functools.reduce(jnp.logical_and, [c == n for c, n in zip(count, live)]))
            def _():
                several(group, live)

    for out, k in zip(outs, order(owners)):
        mine = pl.ds(pl.multiple_of((me ^ k) * rows, rows), rows)
        for at in range(0, rank, LANES):
            out[:, at:at + LANES] = latents[at // LANES, mine, :].astype(jnp.bfloat16)


def in_hbm(*arrays):
    return [pltpu.with_memory_space_constraint(array, pltpu.HBM) for array in arrays]


def attend(query, cache, scales, lengths, owners):
    requests, heads, channels = query.shape
    cache_len = cache.shape[1]
    rank = channels - ROPE_DIM
    part = jax.ShapeDtypeStruct((heads // owners * requests, rank), jnp.bfloat16)
    return pl.pallas_call(
        functools.partial(attend_kernel, owners),
        out_shape=[part] * owners,
        in_specs=[pl.BlockSpec(memory_space=pl.ANY)] * 4,
        out_specs=[pl.BlockSpec(memory_space=pltpu.VMEM)] * owners,
        scratch_shapes=[
            pltpu.VMEM((rank // LANES, heads * requests, LANES), jnp.float32),
            pltpu.SMEM((requests,), jnp.int32),
            pltpu.VMEM((requests, channels, heads), jnp.bfloat16),
            pltpu.VMEM((channels,), jnp.float32),
            pltpu.VMEM((requests, channels, cache_len), jnp.bfloat16),
            pltpu.SemaphoreType.DMA((requests, cache_len // min(BLOCK, cache_len))),
            pltpu.SemaphoreType.DMA((3,)),
        ],
        compiler_params=pltpu.CompilerParams(vmem_limit_bytes=24 * 2**20),
        cost_estimate=pl.CostEstimate(
            flops=4 * requests * heads * channels * cache_len,
            bytes_accessed=2 * requests * channels * cache_len,
            transcendentals=requests * heads * cache_len,
        ),
        name="attend",
    )(*in_hbm(lengths, jnp.swapaxes(query, 1, 2), scales, jnp.swapaxes(cache, 1, 2)))


def stage_kernel(maps_hbm, after, maps, sem):
    copy = pltpu.make_async_copy(maps_hbm, maps, sem)
    copy.start()
    copy.wait()


def stage(maps, after):
    return pl.pallas_call(
        stage_kernel,
        out_shape=jax.ShapeDtypeStruct(maps.shape, maps.dtype),
        in_specs=[pl.BlockSpec(memory_space=pl.ANY)] * 2,
        out_specs=pl.BlockSpec(memory_space=pltpu.VMEM),
        scratch_shapes=[pltpu.SemaphoreType.DMA(())],
        compiler_params=pltpu.CompilerParams(vmem_limit_bytes=8 * 2**20),
        cost_estimate=pl.CostEstimate(
            flops=0, bytes_accessed=4 * maps.size, transcendentals=0
        ),
        name="stage",
    )(*in_hbm(maps), after)


def project_kernel(count, *refs):
    parts, maps, outs = refs[:count], refs[count], refs[count + 1:]
    local_heads, requests, width = outs[0].shape
    group = min(GROUP_ROWS // requests, local_heads)
    rows = group * requests
    for first in range(0, local_heads, group):
        here = slice(first * requests, first * requests + rows)
        mixed = jnp.concatenate([part[here, :] for part in parts], axis=0)
        wide = jnp.concatenate([maps[first + i] for i in range(group)], axis=1)
        values = jnp.dot(mixed, wide, preferred_element_type=jnp.float32)
        head = lax.broadcasted_iota(jnp.int32, (rows, width), 0) // requests
        for d, out in enumerate(outs):
            block = values[d * rows:(d + 1) * rows]
            own = block[:, :width]
            for i in range(1, group):
                own = jnp.where(head == i, block[:, i * width:(i + 1) * width], own)
            out[first:first + group] = own.astype(jnp.bfloat16).reshape(group, requests, width)


def project(parts, maps, requests):
    count = len(parts)
    local_heads, rank, width = maps.shape
    return pl.pallas_call(
        functools.partial(project_kernel, count),
        out_shape=[jax.ShapeDtypeStruct((local_heads, requests, width), jnp.bfloat16)] * count,
        in_specs=[pl.BlockSpec(memory_space=pltpu.VMEM)] * (count + 1),
        out_specs=[pl.BlockSpec(memory_space=pltpu.VMEM)] * count,
        compiler_params=pltpu.CompilerParams(vmem_limit_bytes=24 * 2**20),
        cost_estimate=pl.CostEstimate(
            flops=2 * count * requests * local_heads * rank * width,
            bytes_accessed=2 * local_heads * rank * width,
            transcendentals=0,
        ),
        name="project",
    )(*parts, maps)


def assemble_kernel(owners, *refs):
    parts, out, sems = refs[:owners], refs[owners], refs[owners + 1]
    me = lax.axis_index("tp")
    copies = [
        pltpu.make_async_copy(part, out.at[me ^ k], sems.at[k])
        for k, part in zip(order(owners), parts)
    ]
    for copy in copies:
        copy.start()
    for copy in copies:
        copy.wait()


def assemble(parts):
    owners = len(parts)
    return pl.pallas_call(
        functools.partial(assemble_kernel, owners),
        out_shape=pltpu.HBM((owners,) + parts[0].shape, parts[0].dtype),
        in_specs=[pl.BlockSpec(memory_space=pltpu.VMEM)] * owners,
        out_specs=pl.BlockSpec(memory_space=pltpu.HBM),
        scratch_shapes=[pltpu.SemaphoreType.DMA((owners,))],
        compiler_params=pltpu.CompilerParams(vmem_limit_bytes=2 * 2**20),
        name="assemble",
    )(*parts)


def exchange(parts):
    owners = len(parts)
    return [
        lax.ppermute(part, "tp", [(i, i ^ k) for i in range(owners)]) if k else part
        for k, part in zip(order(owners), parts)
    ]


def on_device(query, cache, scales, lengths, value_up):
    owners = lax.axis_size("tp")
    latents = attend(query, cache, scales, lengths, owners)
    maps = stage(value_up, latents[0])
    values = exchange(project(exchange(latents), maps, query.shape[0]))
    returned = assemble(values)
    _, local_heads, requests, width = returned.shape
    returned = returned.reshape(owners * local_heads, requests, width)
    return jnp.swapaxes(returned, 0, 1).reshape(requests, owners * local_heads * width)


def solution(mesh):
    in_specs = (
        P(("grp", "tp"), None, None),
        P(("grp", "tp"), None, None),
        P(),
        P(("grp", "tp")),
        P("tp", None, None),
    )
    out_specs = P(("grp", "tp"), None)
    return jax.shard_map(
        on_device, mesh=mesh, in_specs=in_specs, out_specs=out_specs, check_vma=False
    )
```

```python
import functools
import itertools
import math

import jax
import jax.numpy as jnp
from jax import lax
from jax.experimental import pallas as pl
from jax.experimental.pallas import tpu as pltpu
from jax.sharding import PartitionSpec as P

ROPE_DIM = 64
SOFTMAX_SCALE = (1.0 + 0.1 * math.log(40.0)) ** 2 / math.sqrt(192.0)
EXP2_SCALE = SOFTMAX_SCALE * math.log2(math.e)
BLOCK = 512
LANES = 128
GROUP_ROWS = 16


def order(owners):
    return [0] + list(range(owners - 1, 0, -1))


def attend_kernel(owners, lengths_hbm, query_hbm, scales_hbm, cache, *refs):
    outs, (latents, lengths, query, scales, keys, sems, small_sems) = refs[:owners], refs[owners:]
    requests, channels, heads = query.shape
    rows, rank = outs[0].shape
    cache_len = cache.shape[2]
    block = min(BLOCK, cache_len)
    blocks = cache_len // block
    me = lax.axis_index("tp")

    def fetch(r, b):
        span = pl.ds(b * block, block)
        return pltpu.make_async_copy(cache.at[r, :, span], keys.at[r, :, span], sems.at[r, b])

    def ask(r):
        return pltpu.make_async_copy(query_hbm.at[r], query.at[r], small_sems.at[2 + r])

    lengths_copy = pltpu.make_async_copy(lengths_hbm, lengths, small_sems.at[0])
    scales_copy = pltpu.make_async_copy(scales_hbm, scales, small_sems.at[1])
    lengths_copy.start()
    scales_copy.start()
    for r in range(requests):
        ask(r).start()
        fetch(r, 0).start()
    lengths_copy.wait()
    for r in range(requests):
        for b in range(1, blocks):
            @pl.when(b * block < lengths[r])
            def _():
                fetch(r, b).start()
    scales_copy.wait()
    scale_row = scales[...].reshape(1, channels)

    def scale(r):
        ask(r).wait()
        return (query[r].astype(jnp.float32).T * scale_row).astype(jnp.bfloat16)

    def score(scaled, r, b, live):
        if r not in scaled:
            scaled[r] = scale(r)
        fetch(r, b).wait()
        span = slice(b * block, (b + 1) * block)
        part = jnp.dot(
            scaled[r][:, :rank], keys[r, :rank, span], preferred_element_type=jnp.float32
        ) + jnp.dot(
            scaled[r][:, rank:], keys[r, rank:, span], preferred_element_type=jnp.float32
        )
        if b == live - 1:
            place = b * block + lax.broadcasted_iota(jnp.int32, part.shape, 1)
            part = jnp.where(place < lengths[r], part, -jnp.inf)
        return part

    def weigh(part, r, b):
        top = jnp.max(part, axis=1, keepdims=True)
        weight = jnp.exp2((part - top) * EXP2_SCALE)
        total = jnp.sum(weight, axis=1, keepdims=True)
        mixture = lax.dot_general(
            weight.astype(jnp.bfloat16), keys[r, :rank, b * block:(b + 1) * block],
            (((1,), (1,)), ((), ())), preferred_element_type=jnp.float32,
        )
        return top, total, mixture

    def merge(one, two):
        top = jnp.maximum(one[0], two[0])
        first = jnp.exp2((one[0] - top) * EXP2_SCALE)
        second = jnp.exp2((two[0] - top) * EXP2_SCALE)
        return (top,) + tuple(x * first + y * second for x, y in zip(one[1:], two[1:]))

    def finish(r, total, mixture):
        latent = mixture * (1.0 / total) * scale_row[:, :rank]
        for at in range(0, rank, LANES):
            latents[at // LANES, pl.ds(r, heads, stride=requests), :] = latent[:, at:at + LANES]

    def several(group, live):
        scaled = {}
        units = [(r, b, n) for r, n in zip(group, live) for b in range(n)]
        part = score(scaled, *units[0])
        state = None
        for i, (r, b, n) in enumerate(units):
            ahead = score(scaled, *units[i + 1]) if i + 1 < len(units) else None
            done = weigh(part, r, b)
            state = done if b == 0 else merge(state, done)
            if b == n - 1:
                finish(r, *state[1:])
            part = ahead

    for first in range(0, requests, 2):
        group = tuple(range(first, min(first + 2, requests)))
        count = [(lengths[r] + (block - 1)) // block for r in group]
        for live in itertools.product(range(1, blocks + 1), repeat=len(group)):
            @pl.when(functools.reduce(jnp.logical_and, [c == n for c, n in zip(count, live)]))
            def _():
                several(group, live)

    for out, k in zip(outs, order(owners)):
        mine = pl.ds(pl.multiple_of((me ^ k) * rows, rows), rows)
        for at in range(0, rank, LANES):
            out[:, at:at + LANES] = latents[at // LANES, mine, :].astype(jnp.bfloat16)


def in_hbm(*arrays):
    return [pltpu.with_memory_space_constraint(array, pltpu.HBM) for array in arrays]


def attend(query, cache, scales, lengths, owners):
    requests, heads, channels = query.shape
    cache_len = cache.shape[1]
    rank = channels - ROPE_DIM
    part = jax.ShapeDtypeStruct((heads // owners * requests, rank), jnp.bfloat16)
    return pl.pallas_call(
        functools.partial(attend_kernel, owners),
        out_shape=[part] * owners,
        in_specs=[pl.BlockSpec(memory_space=pl.ANY)] * 4,
        out_specs=[pl.BlockSpec(memory_space=pltpu.VMEM)] * owners,
        scratch_shapes=[
            pltpu.VMEM((rank // LANES, heads * requests, LANES), jnp.float32),
            pltpu.SMEM((requests,), jnp.int32),
            pltpu.VMEM((requests, channels, heads), jnp.bfloat16),
            pltpu.VMEM((channels,), jnp.float32),
            pltpu.VMEM((requests, channels, cache_len), jnp.bfloat16),
            pltpu.SemaphoreType.DMA((requests, cache_len // min(BLOCK, cache_len))),
            pltpu.SemaphoreType.DMA((2 + requests,)),
        ],
        compiler_params=pltpu.CompilerParams(vmem_limit_bytes=24 * 2**20),
        cost_estimate=pl.CostEstimate(
            flops=4 * requests * heads * channels * cache_len,
            bytes_accessed=2 * requests * channels * cache_len,
            transcendentals=requests * heads * cache_len,
        ),
        name="attend",
    )(*in_hbm(lengths, jnp.swapaxes(query, 1, 2), scales, jnp.swapaxes(cache, 1, 2)))


def stage_kernel(maps_hbm, after, maps, sem):
    copy = pltpu.make_async_copy(maps_hbm, maps, sem)
    copy.start()
    copy.wait()


def stage(maps, after):
    return pl.pallas_call(
        stage_kernel,
        out_shape=jax.ShapeDtypeStruct(maps.shape, maps.dtype),
        in_specs=[pl.BlockSpec(memory_space=pl.ANY)] * 2,
        out_specs=pl.BlockSpec(memory_space=pltpu.VMEM),
        scratch_shapes=[pltpu.SemaphoreType.DMA(())],
        compiler_params=pltpu.CompilerParams(vmem_limit_bytes=8 * 2**20),
        cost_estimate=pl.CostEstimate(
            flops=0, bytes_accessed=4 * maps.size, transcendentals=0
        ),
        name="stage",
    )(*in_hbm(maps), after)


def project_kernel(count, *refs):
    parts, maps, outs = refs[:count], refs[count], refs[count + 1:]
    local_heads, requests, width = outs[0].shape
    group = min(GROUP_ROWS // requests, local_heads)
    rows = group * requests
    for first in range(0, local_heads, group):
        here = slice(first * requests, first * requests + rows)
        mixed = jnp.concatenate([part[here, :] for part in parts], axis=0)
        wide = jnp.concatenate([maps[first + i] for i in range(group)], axis=1)
        values = jnp.dot(mixed, wide, preferred_element_type=jnp.float32)
        head = lax.broadcasted_iota(jnp.int32, (rows, width), 0) // requests
        for d, out in enumerate(outs):
            block = values[d * rows:(d + 1) * rows]
            own = block[:, :width]
            for i in range(1, group):
                own = jnp.where(head == i, block[:, i * width:(i + 1) * width], own)
            out[first:first + group] = own.astype(jnp.bfloat16).reshape(group, requests, width)


def project(parts, maps, requests):
    count = len(parts)
    local_heads, rank, width = maps.shape
    return pl.pallas_call(
        functools.partial(project_kernel, count),
        out_shape=[jax.ShapeDtypeStruct((local_heads, requests, width), jnp.bfloat16)] * count,
        in_specs=[pl.BlockSpec(memory_space=pltpu.VMEM)] * (count + 1),
        out_specs=[pl.BlockSpec(memory_space=pltpu.VMEM)] * count,
        compiler_params=pltpu.CompilerParams(vmem_limit_bytes=24 * 2**20),
        cost_estimate=pl.CostEstimate(
            flops=2 * count * requests * local_heads * rank * width,
            bytes_accessed=2 * local_heads * rank * width,
            transcendentals=0,
        ),
        name="project",
    )(*parts, maps)


def assemble_kernel(owners, *refs):
    parts, out, sems = refs[:owners], refs[owners], refs[owners + 1]
    me = lax.axis_index("tp")
    copies = [
        pltpu.make_async_copy(part, out.at[me ^ k], sems.at[k])
        for k, part in zip(order(owners), parts)
    ]
    for copy in copies:
        copy.start()
    for copy in copies:
        copy.wait()


def assemble(parts):
    owners = len(parts)
    return pl.pallas_call(
        functools.partial(assemble_kernel, owners),
        out_shape=pltpu.HBM((owners,) + parts[0].shape, parts[0].dtype),
        in_specs=[pl.BlockSpec(memory_space=pltpu.VMEM)] * owners,
        out_specs=pl.BlockSpec(memory_space=pltpu.HBM),
        scratch_shapes=[pltpu.SemaphoreType.DMA((owners,))],
        compiler_params=pltpu.CompilerParams(vmem_limit_bytes=2 * 2**20),
        name="assemble",
    )(*parts)


def exchange(parts):
    owners = len(parts)
    return [
        lax.ppermute(part, "tp", [(i, i ^ k) for i in range(owners)]) if k else part
        for k, part in zip(order(owners), parts)
    ]


def on_device(query, cache, scales, lengths, value_up):
    owners = lax.axis_size("tp")
    latents = attend(query, cache, scales, lengths, owners)
    maps = stage(value_up, latents[0])
    values = exchange(project(exchange(latents), maps, query.shape[0]))
    returned = assemble(values)
    _, local_heads, requests, width = returned.shape
    returned = returned.reshape(owners * local_heads, requests, width)
    return jnp.swapaxes(returned, 0, 1).reshape(requests, owners * local_heads * width)


def solution(mesh):
    in_specs = (
        P(("grp", "tp"), None, None),
        P(("grp", "tp"), None, None),
        P(),
        P(("grp", "tp")),
        P("tp", None, None),
    )
    out_specs = P(("grp", "tp"), None)
    return jax.shard_map(
        on_device, mesh=mesh, in_specs=in_specs, out_specs=out_specs, check_vma=False
    )
```

```python
import functools
import itertools
import math

import jax
import jax.numpy as jnp
from jax import lax
from jax.experimental import pallas as pl
from jax.experimental.pallas import tpu as pltpu
from jax.sharding import PartitionSpec as P

ROPE_DIM = 64
SOFTMAX_SCALE = (1.0 + 0.1 * math.log(40.0)) ** 2 / math.sqrt(192.0)
EXP2_SCALE = SOFTMAX_SCALE * math.log2(math.e)
BLOCK = 512
LANES = 128
GROUP_ROWS = 16


def order(owners):
    return [0] + list(range(owners - 1, 0, -1))


def attend_kernel(owners, lengths_hbm, query_hbm, scales_hbm, cache, *refs):
    outs, (latents, lengths, query, scales, keys, sems, small_sems) = refs[:owners], refs[owners:]
    requests, channels, heads = query.shape
    rows, rank = outs[0].shape
    cache_len = cache.shape[2]
    block = min(BLOCK, cache_len)
    blocks = cache_len // block
    me = lax.axis_index("tp")

    def fetch(r, b):
        span = pl.ds(b * block, block)
        return pltpu.make_async_copy(cache.at[r, :, span], keys.at[r, :, span], sems.at[r, b])

    def ask(r):
        return pltpu.make_async_copy(query_hbm.at[r], query.at[r], small_sems.at[2 + r])

    lengths_copy = pltpu.make_async_copy(lengths_hbm, lengths, small_sems.at[0])
    scales_copy = pltpu.make_async_copy(scales_hbm, scales, small_sems.at[1])
    lengths_copy.start()
    scales_copy.start()
    for r in range(requests):
        ask(r).start()
        fetch(r, 0).start()
    lengths_copy.wait()
    for r in range(requests):
        for b in range(1, blocks):
            @pl.when(b * block < lengths[r])
            def _():
                fetch(r, b).start()
    scales_copy.wait()
    scale_row = scales[...].reshape(1, channels)

    def scale(r):
        ask(r).wait()
        return (query[r].astype(jnp.float32).T * scale_row).astype(jnp.bfloat16)

    def score(scaled, r, b, live):
        if r not in scaled:
            scaled[r] = scale(r)
        fetch(r, b).wait()
        span = slice(b * block, (b + 1) * block)
        part = jnp.dot(scaled[r], keys[r, :, span], preferred_element_type=jnp.float32)
        if b == live - 1:
            place = b * block + lax.broadcasted_iota(jnp.int32, part.shape, 1)
            part = jnp.where(place < lengths[r], part, -jnp.inf)
        return part

    def weigh(part, r, b):
        top = jnp.max(part, axis=1, keepdims=True)
        weight = jnp.exp2((part - top) * EXP2_SCALE)
        total = jnp.sum(weight, axis=1, keepdims=True)
        mixture = lax.dot_general(
            weight.astype(jnp.bfloat16), keys[r, :rank, b * block:(b + 1) * block],
            (((1,), (1,)), ((), ())), preferred_element_type=jnp.float32,
        )
        return top, total, mixture

    def merge(one, two):
        top = jnp.maximum(one[0], two[0])
        first = jnp.exp2((one[0] - top) * EXP2_SCALE)
        second = jnp.exp2((two[0] - top) * EXP2_SCALE)
        return (top,) + tuple(x * first + y * second for x, y in zip(one[1:], two[1:]))

    def finish(r, total, mixture):
        latent = mixture * (1.0 / total) * scale_row[:, :rank]
        for at in range(0, rank, LANES):
            latents[at // LANES, pl.ds(r, heads, stride=requests), :] = latent[:, at:at + LANES]

    def several(group, live):
        scaled = {}
        units = [(r, 0, n) for r, n in zip(group, live)]
        units += [(r, b, n) for r, n in zip(group, live) for b in range(1, n)]
        part = score(scaled, *units[0])
        state = {}
        for i, (r, b, n) in enumerate(units):
            ahead = score(scaled, *units[i + 1]) if i + 1 < len(units) else None
            done = weigh(part, r, b)
            state[r] = merge(state[r], done) if b else done
            if b == n - 1:
                finish(r, *state[r][1:])
            part = ahead

    for first in range(0, requests, 2):
        group = tuple(range(first, min(first + 2, requests)))
        count = [(lengths[r] + (block - 1)) // block for r in group]
        for live in itertools.product(range(1, blocks + 1), repeat=len(group)):
            @pl.when(functools.reduce(jnp.logical_and, [c == n for c, n in zip(count, live)]))
            def _():
                several(group, live)

    for out, k in zip(outs, order(owners)):
        mine = pl.ds(pl.multiple_of((me ^ k) * rows, rows), rows)
        for at in range(0, rank, LANES):
            out[:, at:at + LANES] = latents[at // LANES, mine, :].astype(jnp.bfloat16)


def in_hbm(*arrays):
    return [pltpu.with_memory_space_constraint(array, pltpu.HBM) for array in arrays]


def attend(query, cache, scales, lengths, owners):
    requests, heads, channels = query.shape
    cache_len = cache.shape[1]
    rank = channels - ROPE_DIM
    part = jax.ShapeDtypeStruct((heads // owners * requests, rank), jnp.bfloat16)
    return pl.pallas_call(
        functools.partial(attend_kernel, owners),
        out_shape=[part] * owners,
        in_specs=[pl.BlockSpec(memory_space=pl.ANY)] * 4,
        out_specs=[pl.BlockSpec(memory_space=pltpu.VMEM)] * owners,
        scratch_shapes=[
            pltpu.VMEM((rank // LANES, heads * requests, LANES), jnp.float32),
            pltpu.SMEM((requests,), jnp.int32),
            pltpu.VMEM((requests, channels, heads), jnp.bfloat16),
            pltpu.VMEM((channels,), jnp.float32),
            pltpu.VMEM((requests, channels, cache_len), jnp.bfloat16),
            pltpu.SemaphoreType.DMA((requests, cache_len // min(BLOCK, cache_len))),
            pltpu.SemaphoreType.DMA((2 + requests,)),
        ],
        compiler_params=pltpu.CompilerParams(vmem_limit_bytes=24 * 2**20),
        cost_estimate=pl.CostEstimate(
            flops=4 * requests * heads * channels * cache_len,
            bytes_accessed=2 * requests * channels * cache_len,
            transcendentals=requests * heads * cache_len,
        ),
        name="attend",
    )(*in_hbm(lengths, jnp.swapaxes(query, 1, 2), scales, jnp.swapaxes(cache, 1, 2)))


def stage_kernel(maps_hbm, after, maps, sem):
    copy = pltpu.make_async_copy(maps_hbm, maps, sem)
    copy.start()
    copy.wait()


def stage(maps, after):
    return pl.pallas_call(
        stage_kernel,
        out_shape=jax.ShapeDtypeStruct(maps.shape, maps.dtype),
        in_specs=[pl.BlockSpec(memory_space=pl.ANY)] * 2,
        out_specs=pl.BlockSpec(memory_space=pltpu.VMEM),
        scratch_shapes=[pltpu.SemaphoreType.DMA(())],
        compiler_params=pltpu.CompilerParams(vmem_limit_bytes=8 * 2**20),
        cost_estimate=pl.CostEstimate(
            flops=0, bytes_accessed=4 * maps.size, transcendentals=0
        ),
        name="stage",
    )(*in_hbm(maps), after)


def project_kernel(count, *refs):
    parts, maps, outs = refs[:count], refs[count], refs[count + 1:]
    local_heads, requests, width = outs[0].shape
    group = min(GROUP_ROWS // requests, local_heads)
    rows = group * requests
    for first in range(0, local_heads, group):
        here = slice(first * requests, first * requests + rows)
        mixed = jnp.concatenate([part[here, :] for part in parts], axis=0)
        wide = jnp.concatenate([maps[first + i] for i in range(group)], axis=1)
        values = jnp.dot(mixed, wide, preferred_element_type=jnp.float32)
        head = lax.broadcasted_iota(jnp.int32, (rows, width), 0) // requests
        for d, out in enumerate(outs):
            block = values[d * rows:(d + 1) * rows]
            own = block[:, :width]
            for i in range(1, group):
                own = jnp.where(head == i, block[:, i * width:(i + 1) * width], own)
            out[first:first + group] = own.astype(jnp.bfloat16).reshape(group, requests, width)


def project(parts, maps, requests):
    count = len(parts)
    local_heads, rank, width = maps.shape
    return pl.pallas_call(
        functools.partial(project_kernel, count),
        out_shape=[jax.ShapeDtypeStruct((local_heads, requests, width), jnp.bfloat16)] * count,
        in_specs=[pl.BlockSpec(memory_space=pltpu.VMEM)] * (count + 1),
        out_specs=[pl.BlockSpec(memory_space=pltpu.VMEM)] * count,
        compiler_params=pltpu.CompilerParams(vmem_limit_bytes=24 * 2**20),
        cost_estimate=pl.CostEstimate(
            flops=2 * count * requests * local_heads * rank * width,
            bytes_accessed=2 * local_heads * rank * width,
            transcendentals=0,
        ),
        name="project",
    )(*parts, maps)


def assemble_kernel(owners, *refs):
    parts, out, sems = refs[:owners], refs[owners], refs[owners + 1]
    me = lax.axis_index("tp")
    copies = [
        pltpu.make_async_copy(part, out.at[me ^ k], sems.at[k])
        for k, part in zip(order(owners), parts)
    ]
    for copy in copies:
        copy.start()
    for copy in copies:
        copy.wait()


def assemble(parts):
    owners = len(parts)
    return pl.pallas_call(
        functools.partial(assemble_kernel, owners),
        out_shape=pltpu.HBM((owners,) + parts[0].shape, parts[0].dtype),
        in_specs=[pl.BlockSpec(memory_space=pltpu.VMEM)] * owners,
        out_specs=pl.BlockSpec(memory_space=pltpu.HBM),
        scratch_shapes=[pltpu.SemaphoreType.DMA((owners,))],
        compiler_params=pltpu.CompilerParams(vmem_limit_bytes=2 * 2**20),
        name="assemble",
    )(*parts)


def exchange(parts):
    owners = len(parts)
    return [
        lax.ppermute(part, "tp", [(i, i ^ k) for i in range(owners)]) if k else part
        for k, part in zip(order(owners), parts)
    ]


def on_device(query, cache, scales, lengths, value_up):
    owners = lax.axis_size("tp")
    latents = attend(query, cache, scales, lengths, owners)
    maps = stage(value_up, latents[0])
    values = exchange(project(exchange(latents), maps, query.shape[0]))
    returned = assemble(values)
    _, local_heads, requests, width = returned.shape
    returned = returned.reshape(owners * local_heads, requests, width)
    return jnp.swapaxes(returned, 0, 1).reshape(requests, owners * local_heads * width)


def solution(mesh):
    in_specs = (
        P(("grp", "tp"), None, None),
        P(("grp", "tp"), None, None),
        P(),
        P(("grp", "tp")),
        P("tp", None, None),
    )
    out_specs = P(("grp", "tp"), None)
    return jax.shard_map(
        on_device, mesh=mesh, in_specs=in_specs, out_specs=out_specs, check_vma=False
    )
```

```python
import functools
import itertools
import math

import jax
import jax.numpy as jnp
from jax import lax
from jax.experimental import pallas as pl
from jax.experimental.pallas import tpu as pltpu
from jax.sharding import PartitionSpec as P

ROPE_DIM = 64
SOFTMAX_SCALE = (1.0 + 0.1 * math.log(40.0)) ** 2 / math.sqrt(192.0)
EXP2_SCALE = SOFTMAX_SCALE * math.log2(math.e)
BLOCK = 512
LANES = 128
GROUP_ROWS = 16


def order(owners):
    return [0] + list(range(owners - 1, 0, -1))


def attend_kernel(owners, lengths_hbm, query_hbm, scales_hbm, cache, *refs):
    outs, (latents, lengths, query, scales, keys, sems, small_sems) = refs[:owners], refs[owners:]
    requests, channels, heads = query.shape
    rows, rank = outs[0].shape
    cache_len = cache.shape[2]
    block = min(BLOCK, cache_len)
    blocks = cache_len // block
    me = lax.axis_index("tp")

    def fetch(r, b):
        span = pl.ds(b * block, block)
        return pltpu.make_async_copy(cache.at[r, :, span], keys.at[r, :, span], sems.at[r, b])

    def ask(r):
        return pltpu.make_async_copy(query_hbm.at[r], query.at[r], small_sems.at[2 + r])

    lengths_copy = pltpu.make_async_copy(lengths_hbm, lengths, small_sems.at[0])
    scales_copy = pltpu.make_async_copy(scales_hbm, scales, small_sems.at[1])
    lengths_copy.start()
    scales_copy.start()
    for r in range(requests):
        ask(r).start()
        fetch(r, 0).start()
    lengths_copy.wait()
    for r in range(requests):
        for b in range(1, blocks):
            @pl.when(b * block < lengths[r])
            def _():
                fetch(r, b).start()
    scales_copy.wait()
    scale_row = scales[...].reshape(1, channels)

    def scale(r):
        ask(r).wait()
        return (query[r].astype(jnp.float32).T * scale_row).astype(jnp.bfloat16)

    def score(scaled, r, b, live):
        if r not in scaled:
            scaled[r] = scale(r)
        fetch(r, b).wait()
        span = slice(b * block, (b + 1) * block)
        part = jnp.dot(scaled[r], keys[r, :, span], preferred_element_type=jnp.float32)
        part = part.T
        if b == live - 1:
            place = b * block + lax.broadcasted_iota(jnp.int32, part.shape, 0)
            part = jnp.where(place < lengths[r], part, -jnp.inf)
        return part

    def weigh(part, r, b):
        top = jnp.max(part, axis=0, keepdims=True)
        weight = jnp.exp2((part - top) * EXP2_SCALE)
        total = jnp.sum(weight, axis=0, keepdims=True)
        mixture = jnp.dot(
            keys[r, :rank, b * block:(b + 1) * block], weight.astype(jnp.bfloat16),
            preferred_element_type=jnp.float32,
        )
        return top, total, mixture

    def merge(one, two):
        top = jnp.maximum(one[0], two[0])
        first = jnp.exp2((one[0] - top) * EXP2_SCALE)
        second = jnp.exp2((two[0] - top) * EXP2_SCALE)
        return (top,) + tuple(x * first + y * second for x, y in zip(one[1:], two[1:]))

    def finish(r, total, mixture):
        latent = (mixture * (1.0 / total)).T * scale_row[:, :rank]
        for at in range(0, rank, LANES):
            latents[at // LANES, pl.ds(r, heads, stride=requests), :] = latent[:, at:at + LANES]

    def several(group, live):
        scaled = {}
        units = [(r, 0, n) for r, n in zip(group, live)]
        units += [(r, b, n) for r, n in zip(group, live) for b in range(1, n)]
        part = score(scaled, *units[0])
        state = {}
        for i, (r, b, n) in enumerate(units):
            ahead = score(scaled, *units[i + 1]) if i + 1 < len(units) else None
            done = weigh(part, r, b)
            state[r] = merge(state[r], done) if b else done
            if b == n - 1:
                finish(r, *state[r][1:])
            part = ahead

    for first in range(0, requests, 2):
        group = tuple(range(first, min(first + 2, requests)))
        count = [(lengths[r] + (block - 1)) // block for r in group]
        for live in itertools.product(range(1, blocks + 1), repeat=len(group)):
            @pl.when(functools.reduce(jnp.logical_and, [c == n for c, n in zip(count, live)]))
            def _():
                several(group, live)

    for out, k in zip(outs, order(owners)):
        mine = pl.ds(pl.multiple_of((me ^ k) * rows, rows), rows)
        for at in range(0, rank, LANES):
            out[:, at:at + LANES] = latents[at // LANES, mine, :].astype(jnp.bfloat16)


def in_hbm(*arrays):
    return [pltpu.with_memory_space_constraint(array, pltpu.HBM) for array in arrays]


def attend(query, cache, scales, lengths, owners):
    requests, heads, channels = query.shape
    cache_len = cache.shape[1]
    rank = channels - ROPE_DIM
    part = jax.ShapeDtypeStruct((heads // owners * requests, rank), jnp.bfloat16)
    return pl.pallas_call(
        functools.partial(attend_kernel, owners),
        out_shape=[part] * owners,
        in_specs=[pl.BlockSpec(memory_space=pl.ANY)] * 4,
        out_specs=[pl.BlockSpec(memory_space=pltpu.VMEM)] * owners,
        scratch_shapes=[
            pltpu.VMEM((rank // LANES, heads * requests, LANES), jnp.float32),
            pltpu.SMEM((requests,), jnp.int32),
            pltpu.VMEM((requests, channels, heads), jnp.bfloat16),
            pltpu.VMEM((channels,), jnp.float32),
            pltpu.VMEM((requests, channels, cache_len), jnp.bfloat16),
            pltpu.SemaphoreType.DMA((requests, cache_len // min(BLOCK, cache_len))),
            pltpu.SemaphoreType.DMA((2 + requests,)),
        ],
        compiler_params=pltpu.CompilerParams(vmem_limit_bytes=24 * 2**20),
        cost_estimate=pl.CostEstimate(
            flops=4 * requests * heads * channels * cache_len,
            bytes_accessed=2 * requests * channels * cache_len,
            transcendentals=requests * heads * cache_len,
        ),
        name="attend",
    )(*in_hbm(lengths, jnp.swapaxes(query, 1, 2), scales, jnp.swapaxes(cache, 1, 2)))


def stage_kernel(maps_hbm, after, maps, sem):
    copy = pltpu.make_async_copy(maps_hbm, maps, sem)
    copy.start()
    copy.wait()


def stage(maps, after):
    return pl.pallas_call(
        stage_kernel,
        out_shape=jax.ShapeDtypeStruct(maps.shape, maps.dtype),
        in_specs=[pl.BlockSpec(memory_space=pl.ANY)] * 2,
        out_specs=pl.BlockSpec(memory_space=pltpu.VMEM),
        scratch_shapes=[pltpu.SemaphoreType.DMA(())],
        compiler_params=pltpu.CompilerParams(vmem_limit_bytes=8 * 2**20),
        cost_estimate=pl.CostEstimate(
            flops=0, bytes_accessed=4 * maps.size, transcendentals=0
        ),
        name="stage",
    )(*in_hbm(maps), after)


def project_kernel(count, *refs):
    parts, maps, outs = refs[:count], refs[count], refs[count + 1:]
    local_heads, requests, width = outs[0].shape
    group = min(GROUP_ROWS // requests, local_heads)
    rows = group * requests
    for first in range(0, local_heads, group):
        here = slice(first * requests, first * requests + rows)
        mixed = jnp.concatenate([part[here, :] for part in parts], axis=0)
        wide = jnp.concatenate([maps[first + i] for i in range(group)], axis=1)
        values = jnp.dot(mixed, wide, preferred_element_type=jnp.float32)
        head = lax.broadcasted_iota(jnp.int32, (rows, width), 0) // requests
        for d, out in enumerate(outs):
            block = values[d * rows:(d + 1) * rows]
            own = block[:, :width]
            for i in range(1, group):
                own = jnp.where(head == i, block[:, i * width:(i + 1) * width], own)
            out[first:first + group] = own.astype(jnp.bfloat16).reshape(group, requests, width)


def project(parts, maps, requests):
    count = len(parts)
    local_heads, rank, width = maps.shape
    return pl.pallas_call(
        functools.partial(project_kernel, count),
        out_shape=[jax.ShapeDtypeStruct((local_heads, requests, width), jnp.bfloat16)] * count,
        in_specs=[pl.BlockSpec(memory_space=pltpu.VMEM)] * (count + 1),
        out_specs=[pl.BlockSpec(memory_space=pltpu.VMEM)] * count,
        compiler_params=pltpu.CompilerParams(vmem_limit_bytes=24 * 2**20),
        cost_estimate=pl.CostEstimate(
            flops=2 * count * requests * local_heads * rank * width,
            bytes_accessed=2 * local_heads * rank * width,
            transcendentals=0,
        ),
        name="project",
    )(*parts, maps)


def assemble_kernel(owners, *refs):
    parts, out, sems = refs[:owners], refs[owners], refs[owners + 1]
    me = lax.axis_index("tp")
    copies = [
        pltpu.make_async_copy(part, out.at[me ^ k], sems.at[k])
        for k, part in zip(order(owners), parts)
    ]
    for copy in copies:
        copy.start()
    for copy in copies:
        copy.wait()


def assemble(parts):
    owners = len(parts)
    return pl.pallas_call(
        functools.partial(assemble_kernel, owners),
        out_shape=pltpu.HBM((owners,) + parts[0].shape, parts[0].dtype),
        in_specs=[pl.BlockSpec(memory_space=pltpu.VMEM)] * owners,
        out_specs=pl.BlockSpec(memory_space=pltpu.HBM),
        scratch_shapes=[pltpu.SemaphoreType.DMA((owners,))],
        compiler_params=pltpu.CompilerParams(vmem_limit_bytes=2 * 2**20),
        name="assemble",
    )(*parts)


def exchange(parts):
    owners = len(parts)
    return [
        lax.ppermute(part, "tp", [(i, i ^ k) for i in range(owners)]) if k else part
        for k, part in zip(order(owners), parts)
    ]


def on_device(query, cache, scales, lengths, value_up):
    owners = lax.axis_size("tp")
    latents = attend(query, cache, scales, lengths, owners)
    maps = stage(value_up, latents[0])
    values = exchange(project(exchange(latents), maps, query.shape[0]))
    returned = assemble(values)
    _, local_heads, requests, width = returned.shape
    returned = returned.reshape(owners * local_heads, requests, width)
    return jnp.swapaxes(returned, 0, 1).reshape(requests, owners * local_heads * width)


def solution(mesh):
    in_specs = (
        P(("grp", "tp"), None, None),
        P(("grp", "tp"), None, None),
        P(),
        P(("grp", "tp")),
        P("tp", None, None),
    )
    out_specs = P(("grp", "tp"), None)
    return jax.shard_map(
        on_device, mesh=mesh, in_specs=in_specs, out_specs=out_specs, check_vma=False
    )
```

```python
import functools
import math

import jax
import jax.numpy as jnp
from jax import lax
from jax.experimental import pallas as pl
from jax.experimental.pallas import tpu as pltpu
from jax.sharding import PartitionSpec as P

ROPE_DIM = 64
SOFTMAX_SCALE = (1.0 + 0.1 * math.log(40.0)) ** 2 / math.sqrt(192.0)
EXP2_SCALE = SOFTMAX_SCALE * math.log2(math.e)
BLOCK = 512
LANES = 128
GROUP_ROWS = 16


def order(owners):
    return [0] + list(range(owners - 1, 0, -1))


def attend_kernel(owners, lengths_hbm, query_hbm, scales_hbm, cache, *refs):
    outs, refs = refs[:owners], refs[owners:]
    latents, lengths, query, scales, keys, scaled, tops, totals, mixtures, sems, small_sems = refs
    requests, channels, heads = query.shape
    rows, rank = outs[0].shape
    cache_len = cache.shape[2]
    block = min(BLOCK, cache_len)
    blocks = cache_len // block
    me = lax.axis_index("tp")

    def fetch(r, b):
        span = pl.ds(b * block, block)
        return pltpu.make_async_copy(cache.at[r, :, span], keys.at[r, :, span], sems.at[r, b])

    def ask(r):
        return pltpu.make_async_copy(query_hbm.at[r], query.at[r], small_sems.at[2 + r])

    lengths_copy = pltpu.make_async_copy(lengths_hbm, lengths, small_sems.at[0])
    scales_copy = pltpu.make_async_copy(scales_hbm, scales, small_sems.at[1])
    lengths_copy.start()
    scales_copy.start()
    for r in range(requests):
        ask(r).start()
        fetch(r, 0).start()
    lengths_copy.wait()
    for r in range(requests):
        for b in range(1, blocks):
            @pl.when(b * block < lengths[r])
            def _():
                fetch(r, b).start()
    scales_copy.wait()
    scale_row = scales[...].reshape(1, channels)

    count = [(lengths[r] + (block - 1)) // block for r in range(requests)]

    @pl.loop(0, requests)
    def _(r):
        ask(r).wait()
        scaled[r] = (query[r].astype(jnp.float32).T * scale_row).astype(jnp.bfloat16)
        tops[r] = jnp.full(tops.shape[1:], -jnp.inf, jnp.float32)
        totals[r] = jnp.zeros(totals.shape[1:], jnp.float32)
        mixtures[r] = jnp.zeros(mixtures.shape[1:], jnp.float32)

    def step(r, b):
        fetch(r, b).wait()
        span = pl.ds(pl.multiple_of(b * block, block), block)
        part = jnp.dot(scaled[r], keys[r, :, span], preferred_element_type=jnp.float32)
        place = b * block + lax.broadcasted_iota(jnp.int32, part.shape, 1)
        part = jnp.where(place < lengths[r], part, -jnp.inf)
        before = tops[r]
        top = jnp.maximum(before, jnp.max(part, axis=1, keepdims=True))
        fade = jnp.exp2((before - top) * EXP2_SCALE)
        weight = jnp.exp2((part - top[:, :1]) * EXP2_SCALE)
        tops[r] = top
        totals[r] = totals[r] * fade + jnp.sum(weight, axis=1, keepdims=True)
        mixtures[r] = mixtures[r] * fade[:, :1] + lax.dot_general(
            weight.astype(jnp.bfloat16), keys[r, :rank, span],
            (((1,), (1,)), ((), ())), preferred_element_type=jnp.float32,
        )

    for first in range(0, requests, 2):
        pair = [first, min(first + 1, requests - 1)]
        extra = count[pair[0]] - 1

        @pl.loop(0, count[pair[0]] + count[pair[1]])
        def _(u):
            late = (u - 2 >= extra).astype(jnp.int32)
            r = jnp.where(u < 2, u, late)
            b = jnp.where(u < 2, 0, u - 1 - late * extra)
            step(first + r, b)

    @pl.loop(0, requests)
    def _(r):
        latent = mixtures[r] * (1.0 / totals[r][:, :1]) * scale_row[:, :rank]
        for at in range(0, rank, LANES):
            latents[at // LANES, pl.ds(r, heads, stride=requests), :] = latent[:, at:at + LANES]

    for out, k in zip(outs, order(owners)):
        mine = pl.ds(pl.multiple_of((me ^ k) * rows, rows), rows)
        for at in range(0, rank, LANES):
            out[:, at:at + LANES] = latents[at // LANES, mine, :].astype(jnp.bfloat16)


def in_hbm(*arrays):
    return [pltpu.with_memory_space_constraint(array, pltpu.HBM) for array in arrays]


def attend(query, cache, scales, lengths, owners):
    requests, heads, channels = query.shape
    cache_len = cache.shape[1]
    rank = channels - ROPE_DIM
    part = jax.ShapeDtypeStruct((heads // owners * requests, rank), jnp.bfloat16)
    return pl.pallas_call(
        functools.partial(attend_kernel, owners),
        out_shape=[part] * owners,
        in_specs=[pl.BlockSpec(memory_space=pl.ANY)] * 4,
        out_specs=[pl.BlockSpec(memory_space=pltpu.VMEM)] * owners,
        scratch_shapes=[
            pltpu.VMEM((rank // LANES, heads * requests, LANES), jnp.float32),
            pltpu.SMEM((requests,), jnp.int32),
            pltpu.VMEM((requests, channels, heads), jnp.bfloat16),
            pltpu.VMEM((channels,), jnp.float32),
            pltpu.VMEM((requests, channels, cache_len), jnp.bfloat16),
            pltpu.VMEM((requests, heads, channels), jnp.bfloat16),
            pltpu.VMEM((requests, heads, LANES), jnp.float32),
            pltpu.VMEM((requests, heads, LANES), jnp.float32),
            pltpu.VMEM((requests, heads, rank), jnp.float32),
            pltpu.SemaphoreType.DMA((requests, cache_len // min(BLOCK, cache_len))),
            pltpu.SemaphoreType.DMA((2 + requests,)),
        ],
        compiler_params=pltpu.CompilerParams(vmem_limit_bytes=24 * 2**20),
        cost_estimate=pl.CostEstimate(
            flops=4 * requests * heads * channels * cache_len,
            bytes_accessed=2 * requests * channels * cache_len,
            transcendentals=requests * heads * cache_len,
        ),
        name="attend",
    )(*in_hbm(lengths, jnp.swapaxes(query, 1, 2), scales, jnp.swapaxes(cache, 1, 2)))


def stage_kernel(maps_hbm, after, maps, sem):
    copy = pltpu.make_async_copy(maps_hbm, maps, sem)
    copy.start()
    copy.wait()


def stage(maps, after):
    return pl.pallas_call(
        stage_kernel,
        out_shape=jax.ShapeDtypeStruct(maps.shape, maps.dtype),
        in_specs=[pl.BlockSpec(memory_space=pl.ANY)] * 2,
        out_specs=pl.BlockSpec(memory_space=pltpu.VMEM),
        scratch_shapes=[pltpu.SemaphoreType.DMA(())],
        compiler_params=pltpu.CompilerParams(vmem_limit_bytes=8 * 2**20),
        cost_estimate=pl.CostEstimate(
            flops=0, bytes_accessed=4 * maps.size, transcendentals=0
        ),
        name="stage",
    )(*in_hbm(maps), after)


def project_kernel(count, *refs):
    parts, maps, outs = refs[:count], refs[count], refs[count + 1:]
    local_heads, requests, width = outs[0].shape
    group = min(GROUP_ROWS // requests, local_heads)
    rows = group * requests
    for first in range(0, local_heads, group):
        here = slice(first * requests, first * requests + rows)
        mixed = jnp.concatenate([part[here, :] for part in parts], axis=0)
        wide = jnp.concatenate([maps[first + i] for i in range(group)], axis=1)
        values = jnp.dot(mixed, wide, preferred_element_type=jnp.float32)
        head = lax.broadcasted_iota(jnp.int32, (rows, width), 0) // requests
        for d, out in enumerate(outs):
            block = values[d * rows:(d + 1) * rows]
            own = block[:, :width]
            for i in range(1, group):
                own = jnp.where(head == i, block[:, i * width:(i + 1) * width], own)
            out[first:first + group] = own.astype(jnp.bfloat16).reshape(group, requests, width)


def project(parts, maps, requests):
    count = len(parts)
    local_heads, rank, width = maps.shape
    return pl.pallas_call(
        functools.partial(project_kernel, count),
        out_shape=[jax.ShapeDtypeStruct((local_heads, requests, width), jnp.bfloat16)] * count,
        in_specs=[pl.BlockSpec(memory_space=pltpu.VMEM)] * (count + 1),
        out_specs=[pl.BlockSpec(memory_space=pltpu.VMEM)] * count,
        compiler_params=pltpu.CompilerParams(vmem_limit_bytes=24 * 2**20),
        cost_estimate=pl.CostEstimate(
            flops=2 * count * requests * local_heads * rank * width,
            bytes_accessed=2 * local_heads * rank * width,
            transcendentals=0,
        ),
        name="project",
    )(*parts, maps)


def assemble_kernel(owners, *refs):
    parts, out, sems = refs[:owners], refs[owners], refs[owners + 1]
    me = lax.axis_index("tp")
    copies = [
        pltpu.make_async_copy(part, out.at[me ^ k], sems.at[k])
        for k, part in zip(order(owners), parts)
    ]
    for copy in copies:
        copy.start()
    for copy in copies:
        copy.wait()


def assemble(parts):
    owners = len(parts)
    return pl.pallas_call(
        functools.partial(assemble_kernel, owners),
        out_shape=pltpu.HBM((owners,) + parts[0].shape, parts[0].dtype),
        in_specs=[pl.BlockSpec(memory_space=pltpu.VMEM)] * owners,
        out_specs=pl.BlockSpec(memory_space=pltpu.HBM),
        scratch_shapes=[pltpu.SemaphoreType.DMA((owners,))],
        compiler_params=pltpu.CompilerParams(vmem_limit_bytes=2 * 2**20),
        name="assemble",
    )(*parts)


def exchange(parts):
    owners = len(parts)
    return [
        lax.ppermute(part, "tp", [(i, i ^ k) for i in range(owners)]) if k else part
        for k, part in zip(order(owners), parts)
    ]


def on_device(query, cache, scales, lengths, value_up):
    owners = lax.axis_size("tp")
    latents = attend(query, cache, scales, lengths, owners)
    maps = stage(value_up, latents[0])
    values = exchange(project(exchange(latents), maps, query.shape[0]))
    returned = assemble(values)
    _, local_heads, requests, width = returned.shape
    returned = returned.reshape(owners * local_heads, requests, width)
    return jnp.swapaxes(returned, 0, 1).reshape(requests, owners * local_heads * width)


def solution(mesh):
    in_specs = (
        P(("grp", "tp"), None, None),
        P(("grp", "tp"), None, None),
        P(),
        P(("grp", "tp")),
        P("tp", None, None),
    )
    out_specs = P(("grp", "tp"), None)
    return jax.shard_map(
        on_device, mesh=mesh, in_specs=in_specs, out_specs=out_specs, check_vma=False
    )
```

```python
import functools
import itertools
import math

import jax
import jax.numpy as jnp
from jax import lax
from jax.experimental import pallas as pl
from jax.experimental.pallas import tpu as pltpu
from jax.sharding import PartitionSpec as P

ROPE_DIM = 64
SOFTMAX_SCALE = (1.0 + 0.1 * math.log(40.0)) ** 2 / math.sqrt(192.0)
EXP2_SCALE = SOFTMAX_SCALE * math.log2(math.e)
BLOCK = 512
LANES = 128
GROUP_ROWS = 16


def order(owners):
    return [0] + list(range(owners - 1, 0, -1))


def attend_kernel(owners, lengths_hbm, query_hbm, scales_hbm, cache, *refs):
    outs, (latents, lengths, query, scales, keys, sems, small_sems) = refs[:owners], refs[owners:]
    requests, channels, heads = query.shape
    rows, rank = outs[0].shape
    cache_len = cache.shape[2]
    block = min(BLOCK, cache_len)
    blocks = cache_len // block
    me = lax.axis_index("tp")

    def fetch(r, b):
        span = pl.ds(b * block, block)
        return pltpu.make_async_copy(cache.at[r, :, span], keys.at[r, :, span], sems.at[r, b])

    def ask(r):
        return pltpu.make_async_copy(query_hbm.at[r], query.at[r], small_sems.at[2 + r])

    lengths_copy = pltpu.make_async_copy(lengths_hbm, lengths, small_sems.at[0])
    scales_copy = pltpu.make_async_copy(scales_hbm, scales, small_sems.at[1])
    lengths_copy.start()
    scales_copy.start()
    for r in range(requests):
        ask(r).start()
        fetch(r, 0).start()
    lengths_copy.wait()
    for r in range(requests):
        for b in range(1, blocks):
            @pl.when(b * block < lengths[r])
            def _():
                fetch(r, b).start()
    scales_copy.wait()
    scale_row = scales[...].reshape(1, channels)

    def scale(r):
        ask(r).wait()
        return (query[r].astype(jnp.float32).T * scale_row).astype(jnp.bfloat16)

    def score(scaled, r, b, live):
        if r not in scaled:
            scaled[r] = scale(r)
        fetch(r, b).wait()
        span = slice(b * block, (b + 1) * block)
        part = jnp.dot(scaled[r], keys[r, :, span], preferred_element_type=jnp.float32)
        if b == live - 1:
            place = b * block + lax.broadcasted_iota(jnp.int32, part.shape, 1)
            part = jnp.where(place < lengths[r], part, -jnp.inf)
        return part

    def weigh(parts):
        top = functools.reduce(
            jnp.maximum, [jnp.max(part, axis=1, keepdims=True) for part in parts]
        )
        weights = [jnp.exp2((part - top) * EXP2_SCALE) for part in parts]
        total = sum(jnp.sum(weight, axis=1, keepdims=True) for weight in weights)
        return total, jnp.concatenate([weight.astype(jnp.bfloat16) for weight in weights], axis=1)

    def mix(weights, r):
        return lax.dot_general(
            weights, keys[r, :rank, :weights.shape[1]],
            (((1,), (1,)), ((), ())), preferred_element_type=jnp.float32,
        )

    def finish(r, total, mixture):
        latent = mixture * (1.0 / total) * scale_row[:, :rank]
        for at in range(0, rank, LANES):
            latents[at // LANES, pl.ds(r, heads, stride=requests), :] = latent[:, at:at + LANES]

    def several(group, live):
        scaled = {}
        units = [(r, 0, n) for r, n in zip(group, live)]
        units += [(r, b, n) for r, n in zip(group, live) for b in range(1, n)]
        parts = {r: [] for r in group}
        for r, b, n in units:
            parts[r].append(score(scaled, r, b, n))
        for r in group:
            total, weights = weigh(parts[r])
            finish(r, total, mix(weights, r))

    for first in range(0, requests, 2):
        group = tuple(range(first, min(first + 2, requests)))
        count = [(lengths[r] + (block - 1)) // block for r in group]
        for live in itertools.product(range(1, blocks + 1), repeat=len(group)):
            @pl.when(functools.reduce(jnp.logical_and, [c == n for c, n in zip(count, live)]))
            def _():
                several(group, live)

    for out, k in zip(outs, order(owners)):
        mine = pl.ds(pl.multiple_of((me ^ k) * rows, rows), rows)
        for at in range(0, rank, LANES):
            out[:, at:at + LANES] = latents[at // LANES, mine, :].astype(jnp.bfloat16)


def in_hbm(*arrays):
    return [pltpu.with_memory_space_constraint(array, pltpu.HBM) for array in arrays]


def attend(query, cache, scales, lengths, owners):
    requests, heads, channels = query.shape
    cache_len = cache.shape[1]
    rank = channels - ROPE_DIM
    part = jax.ShapeDtypeStruct((heads // owners * requests, rank), jnp.bfloat16)
    return pl.pallas_call(
        functools.partial(attend_kernel, owners),
        out_shape=[part] * owners,
        in_specs=[pl.BlockSpec(memory_space=pl.ANY)] * 4,
        out_specs=[pl.BlockSpec(memory_space=pltpu.VMEM)] * owners,
        scratch_shapes=[
            pltpu.VMEM((rank // LANES, heads * requests, LANES), jnp.float32),
            pltpu.SMEM((requests,), jnp.int32),
            pltpu.VMEM((requests, channels, heads), jnp.bfloat16),
            pltpu.VMEM((channels,), jnp.float32),
            pltpu.VMEM((requests, channels, cache_len), jnp.bfloat16),
            pltpu.SemaphoreType.DMA((requests, cache_len // min(BLOCK, cache_len))),
            pltpu.SemaphoreType.DMA((2 + requests,)),
        ],
        compiler_params=pltpu.CompilerParams(vmem_limit_bytes=24 * 2**20),
        cost_estimate=pl.CostEstimate(
            flops=4 * requests * heads * channels * cache_len,
            bytes_accessed=2 * requests * channels * cache_len,
            transcendentals=requests * heads * cache_len,
        ),
        name="attend",
    )(*in_hbm(lengths, jnp.swapaxes(query, 1, 2), scales, jnp.swapaxes(cache, 1, 2)))


def stage_kernel(maps_hbm, after, maps, sem):
    copy = pltpu.make_async_copy(maps_hbm, maps, sem)
    copy.start()
    copy.wait()


def stage(maps, after):
    return pl.pallas_call(
        stage_kernel,
        out_shape=jax.ShapeDtypeStruct(maps.shape, maps.dtype),
        in_specs=[pl.BlockSpec(memory_space=pl.ANY)] * 2,
        out_specs=pl.BlockSpec(memory_space=pltpu.VMEM),
        scratch_shapes=[pltpu.SemaphoreType.DMA(())],
        compiler_params=pltpu.CompilerParams(vmem_limit_bytes=8 * 2**20),
        cost_estimate=pl.CostEstimate(
            flops=0, bytes_accessed=4 * maps.size, transcendentals=0
        ),
        name="stage",
    )(*in_hbm(maps), after)


def project_kernel(count, *refs):
    parts, maps, outs = refs[:count], refs[count], refs[count + 1:]
    local_heads, requests, width = outs[0].shape
    group = min(GROUP_ROWS // requests, local_heads)
    rows = group * requests
    for first in range(0, local_heads, group):
        here = slice(first * requests, first * requests + rows)
        mixed = jnp.concatenate([part[here, :] for part in parts], axis=0)
        wide = jnp.concatenate([maps[first + i] for i in range(group)], axis=1)
        values = jnp.dot(mixed, wide, preferred_element_type=jnp.float32)
        head = lax.broadcasted_iota(jnp.int32, (rows, width), 0) // requests
        for d, out in enumerate(outs):
            block = values[d * rows:(d + 1) * rows]
            own = block[:, :width]
            for i in range(1, group):
                own = jnp.where(head == i, block[:, i * width:(i + 1) * width], own)
            out[first:first + group] = own.astype(jnp.bfloat16).reshape(group, requests, width)


def project(parts, maps, requests):
    count = len(parts)
    local_heads, rank, width = maps.shape
    return pl.pallas_call(
        functools.partial(project_kernel, count),
        out_shape=[jax.ShapeDtypeStruct((local_heads, requests, width), jnp.bfloat16)] * count,
        in_specs=[pl.BlockSpec(memory_space=pltpu.VMEM)] * (count + 1),
        out_specs=[pl.BlockSpec(memory_space=pltpu.VMEM)] * count,
        compiler_params=pltpu.CompilerParams(vmem_limit_bytes=24 * 2**20),
        cost_estimate=pl.CostEstimate(
            flops=2 * count * requests * local_heads * rank * width,
            bytes_accessed=2 * local_heads * rank * width,
            transcendentals=0,
        ),
        name="project",
    )(*parts, maps)


def assemble_kernel(owners, *refs):
    parts, out, sems = refs[:owners], refs[owners], refs[owners + 1]
    me = lax.axis_index("tp")
    copies = [
        pltpu.make_async_copy(part, out.at[me ^ k], sems.at[k])
        for k, part in zip(order(owners), parts)
    ]
    for copy in copies:
        copy.start()
    for copy in copies:
        copy.wait()


def assemble(parts):
    owners = len(parts)
    return pl.pallas_call(
        functools.partial(assemble_kernel, owners),
        out_shape=pltpu.HBM((owners,) + parts[0].shape, parts[0].dtype),
        in_specs=[pl.BlockSpec(memory_space=pltpu.VMEM)] * owners,
        out_specs=pl.BlockSpec(memory_space=pltpu.HBM),
        scratch_shapes=[pltpu.SemaphoreType.DMA((owners,))],
        compiler_params=pltpu.CompilerParams(vmem_limit_bytes=2 * 2**20),
        name="assemble",
    )(*parts)


def exchange(parts):
    owners = len(parts)
    return [
        lax.ppermute(part, "tp", [(i, i ^ k) for i in range(owners)]) if k else part
        for k, part in zip(order(owners), parts)
    ]


def on_device(query, cache, scales, lengths, value_up):
    owners = lax.axis_size("tp")
    latents = attend(query, cache, scales, lengths, owners)
    maps = stage(value_up, latents[0])
    values = exchange(project(exchange(latents), maps, query.shape[0]))
    returned = assemble(values)
    _, local_heads, requests, width = returned.shape
    returned = returned.reshape(owners * local_heads, requests, width)
    return jnp.swapaxes(returned, 0, 1).reshape(requests, owners * local_heads * width)


def solution(mesh):
    in_specs = (
        P(("grp", "tp"), None, None),
        P(("grp", "tp"), None, None),
        P(),
        P(("grp", "tp")),
        P("tp", None, None),
    )
    out_specs = P(("grp", "tp"), None)
    return jax.shard_map(
        on_device, mesh=mesh, in_specs=in_specs, out_specs=out_specs, check_vma=False
    )
```

```python
import functools
import itertools
import math

import jax
import jax.numpy as jnp
from jax import lax
from jax.experimental import pallas as pl
from jax.experimental.pallas import tpu as pltpu
from jax.sharding import PartitionSpec as P

ROPE_DIM = 64
SOFTMAX_SCALE = (1.0 + 0.1 * math.log(40.0)) ** 2 / math.sqrt(192.0)
EXP2_SCALE = SOFTMAX_SCALE * math.log2(math.e)
BLOCK = 512
LANES = 128
TILE = 256
UNITS = 2
GROUP_ROWS = 16


def order(owners):
    return [0] + list(range(owners - 1, 0, -1))


def attend_kernel(owners, lengths_hbm, query_hbm, scales_hbm, cache, *refs):
    outs, refs = refs[:owners], refs[owners:]
    latents, lengths, query, scales, keys, sems, small_sems = refs
    requests, channels, heads = query.shape
    rows, rank = outs[0].shape
    cache_len = cache.shape[2]
    block = min(BLOCK, cache_len)
    blocks = cache_len // block
    me = lax.axis_index("tp")

    def fetch(r, b):
        span = pl.ds(b * block, block)
        return pltpu.make_async_copy(cache.at[r, :, span], keys.at[r, :, span], sems.at[r, b])

    def ask(r):
        return pltpu.make_async_copy(query_hbm.at[r], query.at[r], small_sems.at[2 + r])

    lengths_copy = pltpu.make_async_copy(lengths_hbm, lengths, small_sems.at[0])
    scales_copy = pltpu.make_async_copy(scales_hbm, scales, small_sems.at[1])
    lengths_copy.start()
    scales_copy.start()
    for r in range(requests):
        ask(r).start()
        fetch(r, 0).start()
    lengths_copy.wait()
    for r in range(requests):
        for b in range(1, blocks):
            @pl.when(b * block < lengths[r])
            def _():
                fetch(r, b).start()
    scales_copy.wait()
    scale_row = scales[...].reshape(1, channels)

    def scale(r):
        ask(r).wait()
        rows = (query[r].astype(jnp.float32).T * scale_row).astype(jnp.bfloat16)
        return jnp.concatenate(
            [rows, jnp.zeros((heads, -channels % TILE), jnp.bfloat16)], axis=1
        )

    def tile(r, k, at):
        rows = keys[r, k * TILE:min((k + 1) * TILE, channels), at:at + TILE]
        if rows.shape[0] == TILE:
            return rows
        return jnp.concatenate(
            [rows, jnp.zeros((TILE - rows.shape[0], TILE), jnp.bfloat16)], axis=0
        )

    def score(sums, scaled, r, b, live):
        if r not in scaled:
            scaled[r] = scale(r)
        fetch(r, b).wait()
        for k in range(-(-channels // TILE)):
            for unit in range(UNITS):
                pltpu.matmul_push_rhs(tile(r, k, b * block + unit * TILE), k % 2, unit)
            for unit in range(UNITS):
                pltpu.matmul_acc_lhs(
                    sums[unit], scaled[r][:, k * TILE:(k + 1) * TILE], load_staged_rhs=k % 2
                )
        part = jnp.concatenate([pltpu.matmul_pop(sums[unit]) for unit in range(UNITS)], axis=1)
        if b == live - 1:
            place = b * block + lax.broadcasted_iota(jnp.int32, part.shape, 1)
            part = jnp.where(place < lengths[r], part, -jnp.inf)
        return part

    def weigh(parts):
        top = functools.reduce(
            jnp.maximum, [jnp.max(part, axis=1, keepdims=True) for part in parts]
        )
        weights = [jnp.exp2((part - top) * EXP2_SCALE) for part in parts]
        total = sum(jnp.sum(weight, axis=1, keepdims=True) for weight in weights)
        return total, jnp.concatenate([weight.astype(jnp.bfloat16) for weight in weights], axis=1)

    def mix(sums, weights, r):
        for k in range(weights.shape[1] // TILE):
            span = slice(k * TILE, (k + 1) * TILE)
            for unit in range(UNITS):
                pltpu.matmul_push_rhs(
                    keys[r, unit * TILE:(unit + 1) * TILE, span], k % 2, unit, transpose=True
                )
            for unit in range(UNITS):
                pltpu.matmul_acc_lhs(sums[unit], weights[:, span], load_staged_rhs=k % 2)
        return jnp.concatenate([pltpu.matmul_pop(sums[unit]) for unit in range(UNITS)], axis=1)

    def finish(r, total, mixture):
        latent = mixture * (1.0 / total) * scale_row[:, :rank]
        for at in range(0, rank, LANES):
            latents[at // LANES, pl.ds(r, heads, stride=requests), :] = latent[:, at:at + LANES]

    def several(group, live):
        scaled = {}
        units = [(r, 0, n) for r, n in zip(group, live)]
        units += [(r, b, n) for r, n in zip(group, live) for b in range(1, n)]

        def work(*sums):
            sums = [sums[i:i + UNITS] for i in range(0, len(sums), UNITS)]
            parts = {r: [] for r in group}
            for i, (r, b, n) in enumerate(units):
                parts[r].append(score(sums[i % 2], scaled, r, b, n))
            for r in group:
                total, weights = weigh(parts[r])
                finish(r, total, mix(sums[2], weights, r))

        pl.run_scoped(
            work,
            *[pltpu.ACC(unit)((heads, TILE), jnp.float32) for _ in range(3) for unit in range(UNITS)],
        )

    for first in range(0, requests, 2):
        group = tuple(range(first, min(first + 2, requests)))
        count = [(lengths[r] + (block - 1)) // block for r in group]
        for live in itertools.product(range(1, blocks + 1), repeat=len(group)):
            @pl.when(functools.reduce(jnp.logical_and, [c == n for c, n in zip(count, live)]))
            def _():
                several(group, live)

    for out, k in zip(outs, order(owners)):
        mine = pl.ds(pl.multiple_of((me ^ k) * rows, rows), rows)
        for at in range(0, rank, LANES):
            out[:, at:at + LANES] = latents[at // LANES, mine, :].astype(jnp.bfloat16)


def in_hbm(*arrays):
    return [pltpu.with_memory_space_constraint(array, pltpu.HBM) for array in arrays]


def attend(query, cache, scales, lengths, owners):
    requests, heads, channels = query.shape
    cache_len = cache.shape[1]
    rank = channels - ROPE_DIM
    part = jax.ShapeDtypeStruct((heads // owners * requests, rank), jnp.bfloat16)
    return pl.pallas_call(
        functools.partial(attend_kernel, owners),
        out_shape=[part] * owners,
        in_specs=[pl.BlockSpec(memory_space=pl.ANY)] * 4,
        out_specs=[pl.BlockSpec(memory_space=pltpu.VMEM)] * owners,
        scratch_shapes=[
            pltpu.VMEM((rank // LANES, heads * requests, LANES), jnp.float32),
            pltpu.SMEM((requests,), jnp.int32),
            pltpu.VMEM((requests, channels, heads), jnp.bfloat16),
            pltpu.VMEM((channels,), jnp.float32),
            pltpu.VMEM((requests, channels, cache_len), jnp.bfloat16),
            pltpu.SemaphoreType.DMA((requests, cache_len // min(BLOCK, cache_len))),
            pltpu.SemaphoreType.DMA((2 + requests,)),
        ],
        compiler_params=pltpu.CompilerParams(vmem_limit_bytes=24 * 2**20),
        cost_estimate=pl.CostEstimate(
            flops=4 * requests * heads * channels * cache_len,
            bytes_accessed=2 * requests * channels * cache_len,
            transcendentals=requests * heads * cache_len,
        ),
        name="attend",
    )(*in_hbm(lengths, jnp.swapaxes(query, 1, 2), scales, jnp.swapaxes(cache, 1, 2)))


def stage_kernel(maps_hbm, after, maps, sem):
    copy = pltpu.make_async_copy(maps_hbm, maps, sem)
    copy.start()
    copy.wait()


def stage(maps, after):
    return pl.pallas_call(
        stage_kernel,
        out_shape=jax.ShapeDtypeStruct(maps.shape, maps.dtype),
        in_specs=[pl.BlockSpec(memory_space=pl.ANY)] * 2,
        out_specs=pl.BlockSpec(memory_space=pltpu.VMEM),
        scratch_shapes=[pltpu.SemaphoreType.DMA(())],
        compiler_params=pltpu.CompilerParams(vmem_limit_bytes=8 * 2**20),
        cost_estimate=pl.CostEstimate(
            flops=0, bytes_accessed=4 * maps.size, transcendentals=0
        ),
        name="stage",
    )(*in_hbm(maps), after)


def project_kernel(count, *refs):
    parts, maps, outs = refs[:count], refs[count], refs[count + 1:]
    local_heads, requests, width = outs[0].shape
    group = min(GROUP_ROWS // requests, local_heads)
    rows = group * requests
    for first in range(0, local_heads, group):
        here = slice(first * requests, first * requests + rows)
        mixed = jnp.concatenate([part[here, :] for part in parts], axis=0)
        wide = jnp.concatenate([maps[first + i] for i in range(group)], axis=1)
        values = jnp.dot(mixed, wide, preferred_element_type=jnp.float32)
        head = lax.broadcasted_iota(jnp.int32, (rows, width), 0) // requests
        for d, out in enumerate(outs):
            block = values[d * rows:(d + 1) * rows]
            own = block[:, :width]
            for i in range(1, group):
                own = jnp.where(head == i, block[:, i * width:(i + 1) * width], own)
            out[first:first + group] = own.astype(jnp.bfloat16).reshape(group, requests, width)


def project(parts, maps, requests):
    count = len(parts)
    local_heads, rank, width = maps.shape
    return pl.pallas_call(
        functools.partial(project_kernel, count),
        out_shape=[jax.ShapeDtypeStruct((local_heads, requests, width), jnp.bfloat16)] * count,
        in_specs=[pl.BlockSpec(memory_space=pltpu.VMEM)] * (count + 1),
        out_specs=[pl.BlockSpec(memory_space=pltpu.VMEM)] * count,
        compiler_params=pltpu.CompilerParams(vmem_limit_bytes=24 * 2**20),
        cost_estimate=pl.CostEstimate(
            flops=2 * count * requests * local_heads * rank * width,
            bytes_accessed=2 * local_heads * rank * width,
            transcendentals=0,
        ),
        name="project",
    )(*parts, maps)


def assemble_kernel(owners, *refs):
    parts, out, sems = refs[:owners], refs[owners], refs[owners + 1]
    me = lax.axis_index("tp")
    copies = [
        pltpu.make_async_copy(part, out.at[me ^ k], sems.at[k])
        for k, part in zip(order(owners), parts)
    ]
    for copy in copies:
        copy.start()
    for copy in copies:
        copy.wait()


def assemble(parts):
    owners = len(parts)
    return pl.pallas_call(
        functools.partial(assemble_kernel, owners),
        out_shape=pltpu.HBM((owners,) + parts[0].shape, parts[0].dtype),
        in_specs=[pl.BlockSpec(memory_space=pltpu.VMEM)] * owners,
        out_specs=pl.BlockSpec(memory_space=pltpu.HBM),
        scratch_shapes=[pltpu.SemaphoreType.DMA((owners,))],
        compiler_params=pltpu.CompilerParams(vmem_limit_bytes=2 * 2**20),
        name="assemble",
    )(*parts)


def exchange(parts):
    owners = len(parts)
    return [
        lax.ppermute(part, "tp", [(i, i ^ k) for i in range(owners)]) if k else part
        for k, part in zip(order(owners), parts)
    ]


def on_device(query, cache, scales, lengths, value_up):
    owners = lax.axis_size("tp")
    latents = attend(query, cache, scales, lengths, owners)
    maps = stage(value_up, latents[0])
    values = exchange(project(exchange(latents), maps, query.shape[0]))
    returned = assemble(values)
    _, local_heads, requests, width = returned.shape
    returned = returned.reshape(owners * local_heads, requests, width)
    return jnp.swapaxes(returned, 0, 1).reshape(requests, owners * local_heads * width)


def solution(mesh):
    in_specs = (
        P(("grp", "tp"), None, None),
        P(("grp", "tp"), None, None),
        P(),
        P(("grp", "tp")),
        P("tp", None, None),
    )
    out_specs = P(("grp", "tp"), None)
    return jax.shard_map(
        on_device, mesh=mesh, in_specs=in_specs, out_specs=out_specs, check_vma=False
    )
```

```python
import functools
import itertools
import math

import jax
import jax.numpy as jnp
from jax import lax
from jax.experimental import pallas as pl
from jax.experimental.pallas import tpu as pltpu
from jax.sharding import PartitionSpec as P

ROPE_DIM = 64
SOFTMAX_SCALE = (1.0 + 0.1 * math.log(40.0)) ** 2 / math.sqrt(192.0)
EXP2_SCALE = SOFTMAX_SCALE * math.log2(math.e)
BLOCK = 512
LANES = 128
TILE = 256
CHUNK = 32
UNITS = 2
GROUP_ROWS = 16


def order(owners):
    return [0] + list(range(owners - 1, 0, -1))


def attend_kernel(owners, lengths_hbm, query_hbm, scales_hbm, cache, *refs):
    outs, refs = refs[:owners], refs[owners:]
    latents, lengths, query, scales, keys, sems, small_sems = refs
    requests, channels, heads = query.shape
    rows, rank = outs[0].shape
    cache_len = cache.shape[2]
    block = min(BLOCK, cache_len)
    blocks = cache_len // block
    me = lax.axis_index("tp")

    def fetch(r, b):
        span = pl.ds(b * block, block)
        return pltpu.make_async_copy(cache.at[r, :, span], keys.at[r, :, span], sems.at[r, b])

    def ask(r):
        return pltpu.make_async_copy(query_hbm.at[r], query.at[r], small_sems.at[2 + r])

    lengths_copy = pltpu.make_async_copy(lengths_hbm, lengths, small_sems.at[0])
    scales_copy = pltpu.make_async_copy(scales_hbm, scales, small_sems.at[1])
    lengths_copy.start()
    scales_copy.start()
    for r in range(requests):
        ask(r).start()
        fetch(r, 0).start()
    lengths_copy.wait()
    for r in range(requests):
        for b in range(1, blocks):
            @pl.when(b * block < lengths[r])
            def _():
                fetch(r, b).start()
    scales_copy.wait()
    scale_row = scales[...].reshape(1, channels)

    def scale(r):
        ask(r).wait()
        rows = (query[r].astype(jnp.float32).T * scale_row).astype(jnp.bfloat16)
        return jnp.concatenate(
            [rows, jnp.zeros((heads, -channels % TILE), jnp.bfloat16)], axis=1
        )

    def tile(r, k, at):
        rows = keys[r, k * TILE:min((k + 1) * TILE, channels), at:at + TILE]
        if rows.shape[0] == TILE:
            return rows
        return jnp.concatenate(
            [rows, jnp.zeros((TILE - rows.shape[0], TILE), jnp.bfloat16)], axis=0
        )

    def score_steps(sums, scaled, r, b):
        def step(k):
            for unit in range(UNITS):
                pltpu.matmul_push_rhs(tile(r, k, b * block + unit * TILE), k % 2, unit)
            for unit in range(UNITS):
                pltpu.matmul_acc_lhs(
                    sums[unit], scaled[r][:, k * TILE:(k + 1) * TILE], load_staged_rhs=k % 2
                )

        return [functools.partial(step, k) for k in range(-(-channels // TILE))]

    def scores(sums, r, b, live):
        part = jnp.concatenate([pltpu.matmul_pop(sums[unit]) for unit in range(UNITS)], axis=1)
        if b == live - 1:
            place = b * block + lax.broadcasted_iota(jnp.int32, part.shape, 1)
            part = jnp.where(place < lengths[r], part, -jnp.inf)
        return part

    def weigh_steps(part, top, weights, totals):
        def step(at):
            rows = slice(at, at + CHUNK)
            weight = jnp.exp2((part[rows] - top[rows]) * EXP2_SCALE)
            totals.append(jnp.sum(weight, axis=1, keepdims=True))
            weights.append(weight.astype(jnp.bfloat16))

        return [functools.partial(step, at) for at in range(0, heads, CHUNK)]

    def mix_steps(sums, weights, r, b):
        def step(k):
            at = b * block + k * TILE
            for unit in range(UNITS):
                pltpu.matmul_push_rhs(
                    keys[r, unit * TILE:(unit + 1) * TILE, at:at + TILE], k % 2, unit,
                    transpose=True,
                )
            for unit in range(UNITS):
                pltpu.matmul_acc_lhs(
                    sums[unit], weights[:, k * TILE:(k + 1) * TILE], load_staged_rhs=k % 2
                )

        return [functools.partial(step, k) for k in range(block // TILE)]

    def interleave(one, two):
        total = max(len(one), len(two))
        for i in range(total):
            for steps in (one, two):
                for at in range(i * len(steps) // total, (i + 1) * len(steps) // total):
                    steps[at]()

    def finish(r, total, mixture):
        latent = mixture * (1.0 / total) * scale_row[:, :rank]
        for at in range(0, rank, LANES):
            latents[at // LANES, pl.ds(r, heads, stride=requests), :] = latent[:, at:at + LANES]

    def several(group, live):
        scaled = {}

        def work(*sums):
            sums = [sums[i:i + UNITS] for i in range(0, len(sums), UNITS)]
            parts = {r: [] for r in group}
            weights = {(r, b): [] for r, n in zip(group, live) for b in range(n)}
            totals = {(r, b): [] for r, b in weights}
            tops = {}

            def weigh(r, b):
                return weigh_steps(parts[r][b], tops[r], weights[r, b], totals[r, b])

            def column(pieces):
                return jnp.concatenate(pieces, axis=0)

            def top_of(r):
                return functools.reduce(
                    jnp.maximum, [jnp.max(part, axis=1, keepdims=True) for part in parts[r]]
                )

            def mix_all(r, then=()):
                pool = sums[2 + r % 2]
                for b in range(size[r]):
                    ahead = weigh(r, b + 1) if b + 1 < size[r] else then
                    interleave(mix_steps(pool, column(weights[r, b]), r, b), ahead)
                total = sum(column(totals[r, b]) for b in range(size[r]))
                finish(r, total, jnp.concatenate([pltpu.matmul_pop(x) for x in pool], axis=1))

            size = dict(zip(group, live))
            short, *rest = sorted(group, key=size.get)
            turns = [(r, 0) for r in (short, *rest)]
            turns += [(r, b) for r in (short, *rest) for b in range(1, size[r])]
            pending = []
            mixed = False
            for i, (r, b) in enumerate(turns):
                if r not in scaled:
                    scaled[r] = scale(r)
                fetch(r, b).wait()
                interleave(score_steps(sums[i % 2], scaled, r, b), pending)
                parts[r].append(scores(sums[i % 2], r, b, size[r]))
                if len(parts[short]) < size[short]:
                    continue
                if short not in tops:
                    tops[short] = top_of(short)
                    pending = weigh(short, 0)
                elif not mixed and i + 1 < len(turns):
                    pending, mixed = [], True
                    mix_all(short)
                else:
                    pending = []
            for step in pending:
                step()
            for r in rest:
                tops[r] = top_of(r)
                ahead = weigh(r, 0)
                if mixed:
                    for step in ahead:
                        step()
                else:
                    mix_all(short, ahead)
                mix_all(r)
            if not rest:
                mix_all(short)

        pl.run_scoped(
            work,
            *[pltpu.ACC(unit)((heads, TILE), jnp.float32) for _ in range(4) for unit in range(UNITS)],
        )

    for first in range(0, requests, 2):
        group = tuple(range(first, min(first + 2, requests)))
        count = [(lengths[r] + (block - 1)) // block for r in group]
        for live in itertools.product(range(1, blocks + 1), repeat=len(group)):
            @pl.when(functools.reduce(jnp.logical_and, [c == n for c, n in zip(count, live)]))
            def _():
                several(group, live)

    for out, k in zip(outs, order(owners)):
        mine = pl.ds(pl.multiple_of((me ^ k) * rows, rows), rows)
        for at in range(0, rank, LANES):
            out[:, at:at + LANES] = latents[at // LANES, mine, :].astype(jnp.bfloat16)


def in_hbm(*arrays):
    return [pltpu.with_memory_space_constraint(array, pltpu.HBM) for array in arrays]


def attend(query, cache, scales, lengths, owners):
    requests, heads, channels = query.shape
    cache_len = cache.shape[1]
    rank = channels - ROPE_DIM
    part = jax.ShapeDtypeStruct((heads // owners * requests, rank), jnp.bfloat16)
    return pl.pallas_call(
        functools.partial(attend_kernel, owners),
        out_shape=[part] * owners,
        in_specs=[pl.BlockSpec(memory_space=pl.ANY)] * 4,
        out_specs=[pl.BlockSpec(memory_space=pltpu.VMEM)] * owners,
        scratch_shapes=[
            pltpu.VMEM((rank // LANES, heads * requests, LANES), jnp.float32),
            pltpu.SMEM((requests,), jnp.int32),
            pltpu.VMEM((requests, channels, heads), jnp.bfloat16),
            pltpu.VMEM((channels,), jnp.float32),
            pltpu.VMEM((requests, channels, cache_len), jnp.bfloat16),
            pltpu.SemaphoreType.DMA((requests, cache_len // min(BLOCK, cache_len))),
            pltpu.SemaphoreType.DMA((2 + requests,)),
        ],
        compiler_params=pltpu.CompilerParams(vmem_limit_bytes=24 * 2**20),
        cost_estimate=pl.CostEstimate(
            flops=4 * requests * heads * channels * cache_len,
            bytes_accessed=2 * requests * channels * cache_len,
            transcendentals=requests * heads * cache_len,
        ),
        name="attend",
    )(*in_hbm(lengths, jnp.swapaxes(query, 1, 2), scales, jnp.swapaxes(cache, 1, 2)))


def stage_kernel(maps_hbm, after, maps, sem):
    copy = pltpu.make_async_copy(maps_hbm, maps, sem)
    copy.start()
    copy.wait()


def stage(maps, after):
    return pl.pallas_call(
        stage_kernel,
        out_shape=jax.ShapeDtypeStruct(maps.shape, maps.dtype),
        in_specs=[pl.BlockSpec(memory_space=pl.ANY)] * 2,
        out_specs=pl.BlockSpec(memory_space=pltpu.VMEM),
        scratch_shapes=[pltpu.SemaphoreType.DMA(())],
        compiler_params=pltpu.CompilerParams(vmem_limit_bytes=8 * 2**20),
        cost_estimate=pl.CostEstimate(
            flops=0, bytes_accessed=4 * maps.size, transcendentals=0
        ),
        name="stage",
    )(*in_hbm(maps), after)


def project_kernel(count, *refs):
    parts, maps, outs = refs[:count], refs[count], refs[count + 1:]
    local_heads, requests, width = outs[0].shape
    group = min(GROUP_ROWS // requests, local_heads)
    rows = group * requests
    for first in range(0, local_heads, group):
        here = slice(first * requests, first * requests + rows)
        mixed = jnp.concatenate([part[here, :] for part in parts], axis=0)
        wide = jnp.concatenate([maps[first + i] for i in range(group)], axis=1)
        values = jnp.dot(mixed, wide, preferred_element_type=jnp.float32)
        head = lax.broadcasted_iota(jnp.int32, (rows, width), 0) // requests
        for d, out in enumerate(outs):
            block = values[d * rows:(d + 1) * rows]
            own = block[:, :width]
            for i in range(1, group):
                own = jnp.where(head == i, block[:, i * width:(i + 1) * width], own)
            out[first:first + group] = own.astype(jnp.bfloat16).reshape(group, requests, width)


def project(parts, maps, requests):
    count = len(parts)
    local_heads, rank, width = maps.shape
    return pl.pallas_call(
        functools.partial(project_kernel, count),
        out_shape=[jax.ShapeDtypeStruct((local_heads, requests, width), jnp.bfloat16)] * count,
        in_specs=[pl.BlockSpec(memory_space=pltpu.VMEM)] * (count + 1),
        out_specs=[pl.BlockSpec(memory_space=pltpu.VMEM)] * count,
        compiler_params=pltpu.CompilerParams(vmem_limit_bytes=24 * 2**20),
        cost_estimate=pl.CostEstimate(
            flops=2 * count * requests * local_heads * rank * width,
            bytes_accessed=2 * local_heads * rank * width,
            transcendentals=0,
        ),
        name="project",
    )(*parts, maps)


def assemble_kernel(owners, *refs):
    parts, out, sems = refs[:owners], refs[owners], refs[owners + 1]
    me = lax.axis_index("tp")
    copies = [
        pltpu.make_async_copy(part, out.at[me ^ k], sems.at[k])
        for k, part in zip(order(owners), parts)
    ]
    for copy in copies:
        copy.start()
    for copy in copies:
        copy.wait()


def assemble(parts):
    owners = len(parts)
    return pl.pallas_call(
        functools.partial(assemble_kernel, owners),
        out_shape=pltpu.HBM((owners,) + parts[0].shape, parts[0].dtype),
        in_specs=[pl.BlockSpec(memory_space=pltpu.VMEM)] * owners,
        out_specs=pl.BlockSpec(memory_space=pltpu.HBM),
        scratch_shapes=[pltpu.SemaphoreType.DMA((owners,))],
        compiler_params=pltpu.CompilerParams(vmem_limit_bytes=2 * 2**20),
        name="assemble",
    )(*parts)


def exchange(parts):
    owners = len(parts)
    return [
        lax.ppermute(part, "tp", [(i, i ^ k) for i in range(owners)]) if k else part
        for k, part in zip(order(owners), parts)
    ]


def on_device(query, cache, scales, lengths, value_up):
    owners = lax.axis_size("tp")
    latents = attend(query, cache, scales, lengths, owners)
    maps = stage(value_up, latents[0])
    values = exchange(project(exchange(latents), maps, query.shape[0]))
    returned = assemble(values)
    _, local_heads, requests, width = returned.shape
    returned = returned.reshape(owners * local_heads, requests, width)
    return jnp.swapaxes(returned, 0, 1).reshape(requests, owners * local_heads * width)


def solution(mesh):
    in_specs = (
        P(("grp", "tp"), None, None),
        P(("grp", "tp"), None, None),
        P(),
        P(("grp", "tp")),
        P("tp", None, None),
    )
    out_specs = P(("grp", "tp"), None)
    return jax.shard_map(
        on_device, mesh=mesh, in_specs=in_specs, out_specs=out_specs, check_vma=False
    )
```

```python
import functools
import itertools
import math

import jax
import jax.numpy as jnp
from jax import lax
from jax.experimental import pallas as pl
from jax.experimental.pallas import tpu as pltpu
from jax.sharding import PartitionSpec as P

ROPE_DIM = 64
SOFTMAX_SCALE = (1.0 + 0.1 * math.log(40.0)) ** 2 / math.sqrt(192.0)
EXP2_SCALE = SOFTMAX_SCALE * math.log2(math.e)
BLOCK = 512
LANES = 128
GROUP_ROWS = 16


def order(owners):
    return [0] + list(range(owners - 1, 0, -1))


def attend_kernel(owners, lengths_hbm, query_hbm, scales_hbm, cache, *refs):
    outs, (latents, lengths, query, scales, keys, sems, small_sems) = refs[:owners], refs[owners:]
    requests, channels, heads = query.shape
    rows, rank = outs[0].shape
    cache_len = cache.shape[2]
    block = min(BLOCK, cache_len)
    blocks = cache_len // block
    me = lax.axis_index("tp")

    def fetch(r, b):
        span = pl.ds(b * block, block)
        return pltpu.make_async_copy(cache.at[r, :, span], keys.at[r, :, span], sems.at[r, b])

    def ask(r):
        return pltpu.make_async_copy(query_hbm.at[r], query.at[r], small_sems.at[2 + r])

    lengths_copy = pltpu.make_async_copy(lengths_hbm, lengths, small_sems.at[0])
    scales_copy = pltpu.make_async_copy(scales_hbm, scales, small_sems.at[1])
    lengths_copy.start()
    scales_copy.start()
    for r in range(requests):
        ask(r).start()
        fetch(r, 0).start()
    lengths_copy.wait()
    for r in range(requests):
        for b in range(1, blocks):
            @pl.when(b * block < lengths[r])
            def _():
                fetch(r, b).start()
    scales_copy.wait()
    scale_row = scales[...].reshape(1, channels)

    def scale(r):
        ask(r).wait()
        return (query[r].astype(jnp.float32).T * scale_row).astype(jnp.bfloat16)

    def score(scaled, r, at, width, last):
        if r not in scaled:
            scaled[r] = scale(r)
        fetch(r, at // block).wait()
        part = jnp.dot(
            scaled[r], keys[r, :, at:at + width], preferred_element_type=jnp.float32
        )
        if last:
            place = at + lax.broadcasted_iota(jnp.int32, part.shape, 1)
            part = jnp.where(place < lengths[r], part, -jnp.inf)
        return part

    def weigh(parts):
        top = functools.reduce(
            jnp.maximum, [jnp.max(part, axis=1, keepdims=True) for part in parts]
        )
        weights = [jnp.exp2((part - top) * EXP2_SCALE) for part in parts]
        total = sum(jnp.sum(weight, axis=1, keepdims=True) for weight in weights)
        return total, jnp.concatenate([weight.astype(jnp.bfloat16) for weight in weights], axis=1)

    def mix(weights, r):
        return lax.dot_general(
            weights, keys[r, :rank, :weights.shape[1]],
            (((1,), (1,)), ((), ())), preferred_element_type=jnp.float32,
        )

    def finish(r, total, mixture):
        latent = mixture * (1.0 / total) * scale_row[:, :rank]
        for at in range(0, rank, LANES):
            latents[at // LANES, pl.ds(r, heads, stride=requests), :] = latent[:, at:at + LANES]

    def several(group, live):
        scaled = {}
        units = []
        for r, size in zip(group, live):
            cuts = list(range(0, size, block)) + [size]
            units += [(i > 0, r, at, end - at, end == size) for i, (at, end) in enumerate(zip(cuts, cuts[1:]))]
        units.sort(key=lambda unit: unit[0])
        parts = {r: [] for r in group}
        for _, r, at, width, last in units:
            parts[r].append(score(scaled, r, at, width, last))
        for r in group:
            total, weights = weigh(parts[r])
            finish(r, total, mix(weights, r))

    for first in range(0, requests, 2):
        group = tuple(range(first, min(first + 2, requests)))
        sizes = [block // 2] + [(b + 1) * block for b in range(blocks)]
        for live in itertools.product(range(len(sizes)), repeat=len(group)):
            fits = [
                (lengths[r] > (sizes[i - 1] if i else 0)) & (lengths[r] <= sizes[i])
                for r, i in zip(group, live)
            ]

            @pl.when(functools.reduce(jnp.logical_and, fits))
            def _():
                several(group, [sizes[i] for i in live])

    for out, k in zip(outs, order(owners)):
        mine = pl.ds(pl.multiple_of((me ^ k) * rows, rows), rows)
        for at in range(0, rank, LANES):
            out[:, at:at + LANES] = latents[at // LANES, mine, :].astype(jnp.bfloat16)


def in_hbm(*arrays):
    return [pltpu.with_memory_space_constraint(array, pltpu.HBM) for array in arrays]


def attend(query, cache, scales, lengths, owners):
    requests, heads, channels = query.shape
    cache_len = cache.shape[1]
    rank = channels - ROPE_DIM
    part = jax.ShapeDtypeStruct((heads // owners * requests, rank), jnp.bfloat16)
    return pl.pallas_call(
        functools.partial(attend_kernel, owners),
        out_shape=[part] * owners,
        in_specs=[pl.BlockSpec(memory_space=pl.ANY)] * 4,
        out_specs=[pl.BlockSpec(memory_space=pltpu.VMEM)] * owners,
        scratch_shapes=[
            pltpu.VMEM((rank // LANES, heads * requests, LANES), jnp.float32),
            pltpu.SMEM((requests,), jnp.int32),
            pltpu.VMEM((requests, channels, heads), jnp.bfloat16),
            pltpu.VMEM((channels,), jnp.float32),
            pltpu.VMEM((requests, channels, cache_len), jnp.bfloat16),
            pltpu.SemaphoreType.DMA((requests, cache_len // min(BLOCK, cache_len))),
            pltpu.SemaphoreType.DMA((2 + requests,)),
        ],
        compiler_params=pltpu.CompilerParams(vmem_limit_bytes=24 * 2**20),
        cost_estimate=pl.CostEstimate(
            flops=4 * requests * heads * channels * cache_len,
            bytes_accessed=2 * requests * channels * cache_len,
            transcendentals=requests * heads * cache_len,
        ),
        name="attend",
    )(*in_hbm(lengths, jnp.swapaxes(query, 1, 2), scales, jnp.swapaxes(cache, 1, 2)))


def stage_kernel(maps_hbm, after, maps, sem):
    copy = pltpu.make_async_copy(maps_hbm, maps, sem)
    copy.start()
    copy.wait()


def stage(maps, after):
    return pl.pallas_call(
        stage_kernel,
        out_shape=jax.ShapeDtypeStruct(maps.shape, maps.dtype),
        in_specs=[pl.BlockSpec(memory_space=pl.ANY)] * 2,
        out_specs=pl.BlockSpec(memory_space=pltpu.VMEM),
        scratch_shapes=[pltpu.SemaphoreType.DMA(())],
        compiler_params=pltpu.CompilerParams(vmem_limit_bytes=8 * 2**20),
        cost_estimate=pl.CostEstimate(
            flops=0, bytes_accessed=4 * maps.size, transcendentals=0
        ),
        name="stage",
    )(*in_hbm(maps), after)


def project_kernel(count, *refs):
    parts, maps, outs = refs[:count], refs[count], refs[count + 1:]
    local_heads, requests, width = outs[0].shape
    group = min(GROUP_ROWS // requests, local_heads)
    rows = group * requests
    for first in range(0, local_heads, group):
        here = slice(first * requests, first * requests + rows)
        mixed = jnp.concatenate([part[here, :] for part in parts], axis=0)
        wide = jnp.concatenate([maps[first + i] for i in range(group)], axis=1)
        values = jnp.dot(mixed, wide, preferred_element_type=jnp.float32)
        head = lax.broadcasted_iota(jnp.int32, (rows, width), 0) // requests
        for d, out in enumerate(outs):
            block = values[d * rows:(d + 1) * rows]
            own = block[:, :width]
            for i in range(1, group):
                own = jnp.where(head == i, block[:, i * width:(i + 1) * width], own)
            out[first:first + group] = own.astype(jnp.bfloat16).reshape(group, requests, width)


def project(parts, maps, requests):
    count = len(parts)
    local_heads, rank, width = maps.shape
    return pl.pallas_call(
        functools.partial(project_kernel, count),
        out_shape=[jax.ShapeDtypeStruct((local_heads, requests, width), jnp.bfloat16)] * count,
        in_specs=[pl.BlockSpec(memory_space=pltpu.VMEM)] * (count + 1),
        out_specs=[pl.BlockSpec(memory_space=pltpu.VMEM)] * count,
        compiler_params=pltpu.CompilerParams(vmem_limit_bytes=24 * 2**20),
        cost_estimate=pl.CostEstimate(
            flops=2 * count * requests * local_heads * rank * width,
            bytes_accessed=2 * local_heads * rank * width,
            transcendentals=0,
        ),
        name="project",
    )(*parts, maps)


def assemble_kernel(owners, *refs):
    parts, out, sems = refs[:owners], refs[owners], refs[owners + 1]
    me = lax.axis_index("tp")
    copies = [
        pltpu.make_async_copy(part, out.at[me ^ k], sems.at[k])
        for k, part in zip(order(owners), parts)
    ]
    for copy in copies:
        copy.start()
    for copy in copies:
        copy.wait()


def assemble(parts):
    owners = len(parts)
    return pl.pallas_call(
        functools.partial(assemble_kernel, owners),
        out_shape=pltpu.HBM((owners,) + parts[0].shape, parts[0].dtype),
        in_specs=[pl.BlockSpec(memory_space=pltpu.VMEM)] * owners,
        out_specs=pl.BlockSpec(memory_space=pltpu.HBM),
        scratch_shapes=[pltpu.SemaphoreType.DMA((owners,))],
        compiler_params=pltpu.CompilerParams(vmem_limit_bytes=2 * 2**20),
        name="assemble",
    )(*parts)


def exchange(parts):
    owners = len(parts)
    return [
        lax.ppermute(part, "tp", [(i, i ^ k) for i in range(owners)]) if k else part
        for k, part in zip(order(owners), parts)
    ]


def on_device(query, cache, scales, lengths, value_up):
    owners = lax.axis_size("tp")
    latents = attend(query, cache, scales, lengths, owners)
    maps = stage(value_up, latents[0])
    values = exchange(project(exchange(latents), maps, query.shape[0]))
    returned = assemble(values)
    _, local_heads, requests, width = returned.shape
    returned = returned.reshape(owners * local_heads, requests, width)
    return jnp.swapaxes(returned, 0, 1).reshape(requests, owners * local_heads * width)


def solution(mesh):
    in_specs = (
        P(("grp", "tp"), None, None),
        P(("grp", "tp"), None, None),
        P(),
        P(("grp", "tp")),
        P("tp", None, None),
    )
    out_specs = P(("grp", "tp"), None)
    return jax.shard_map(
        on_device, mesh=mesh, in_specs=in_specs, out_specs=out_specs, check_vma=False
    )
```

```python
import functools
import itertools
import math

import jax
import jax.numpy as jnp
from jax import lax
from jax.experimental import pallas as pl
from jax.experimental.pallas import tpu as pltpu
from jax.sharding import PartitionSpec as P

ROPE_DIM = 64
SOFTMAX_SCALE = (1.0 + 0.1 * math.log(40.0)) ** 2 / math.sqrt(192.0)
EXP2_SCALE = SOFTMAX_SCALE * math.log2(math.e)
BLOCK = 512
LANES = 128
GROUP_ROWS = 16


def order(owners):
    return [0] + list(range(owners - 1, 0, -1))


def choose(place, first, cases, act):
    if len(cases) == 1:
        act(cases[0])
        return
    half = len(cases) // 2
    lax.cond(
        place < first + half,
        lambda: choose(place, first, cases[:half], act),
        lambda: choose(place, first + half, cases[half:], act),
    )


def attend_kernel(owners, lengths_hbm, query_hbm, scales_hbm, cache, *refs):
    outs, (latents, lengths, query, scales, keys, sems, small_sems) = refs[:owners], refs[owners:]
    requests, channels, heads = query.shape
    rows, rank = outs[0].shape
    cache_len = cache.shape[2]
    block = min(BLOCK, cache_len)
    blocks = cache_len // block
    me = lax.axis_index("tp")

    def fetch(r, b):
        span = pl.ds(b * block, block)
        return pltpu.make_async_copy(cache.at[r, :, span], keys.at[r, :, span], sems.at[r, b])

    def ask(r):
        return pltpu.make_async_copy(query_hbm.at[r], query.at[r], small_sems.at[2 + r])

    lengths_copy = pltpu.make_async_copy(lengths_hbm, lengths, small_sems.at[0])
    scales_copy = pltpu.make_async_copy(scales_hbm, scales, small_sems.at[1])
    lengths_copy.start()
    scales_copy.start()
    for r in range(requests):
        ask(r).start()
        fetch(r, 0).start()
    lengths_copy.wait()
    for r in range(requests):
        for b in range(1, blocks):
            @pl.when(b * block < lengths[r])
            def _():
                fetch(r, b).start()
    scales_copy.wait()
    scale_row = scales[...].reshape(1, channels)

    def scale(r):
        ask(r).wait()
        return (query[r].astype(jnp.float32).T * scale_row).astype(jnp.bfloat16)

    def score(scaled, r, at, width, last):
        if r not in scaled:
            scaled[r] = scale(r)
        fetch(r, at // block).wait()
        part = jnp.dot(
            scaled[r], keys[r, :, at:at + width], preferred_element_type=jnp.float32
        )
        if last:
            place = at + lax.broadcasted_iota(jnp.int32, part.shape, 1)
            part = jnp.where(place < lengths[r], part, -jnp.inf)
        return part

    def weigh(parts):
        top = functools.reduce(
            jnp.maximum, [jnp.max(part, axis=1, keepdims=True) for part in parts]
        )
        weights = [jnp.exp2((part - top) * EXP2_SCALE) for part in parts]
        total = sum(jnp.sum(weight, axis=1, keepdims=True) for weight in weights)
        return total, jnp.concatenate([weight.astype(jnp.bfloat16) for weight in weights], axis=1)

    def mix(weights, r):
        return lax.dot_general(
            weights, keys[r, :rank, :weights.shape[1]],
            (((1,), (1,)), ((), ())), preferred_element_type=jnp.float32,
        )

    def finish(r, total, mixture):
        latent = mixture * (1.0 / total) * scale_row[:, :rank]
        for at in range(0, rank, LANES):
            latents[at // LANES, pl.ds(r, heads, stride=requests), :] = latent[:, at:at + LANES]

    def several(group, live):
        scaled = {}
        units = []
        for r, size in zip(group, live):
            cuts = list(range(0, size, block)) + [size]
            units += [(i > 0, r, at, end - at, end == size) for i, (at, end) in enumerate(zip(cuts, cuts[1:]))]
        units.sort(key=lambda unit: unit[0])
        parts = {r: [] for r in group}
        for _, r, at, width, last in units:
            parts[r].append(score(scaled, r, at, width, last))
        for r in group:
            total, weights = weigh(parts[r])
            finish(r, total, mix(weights, r))

    for first in range(0, requests, 2):
        group = tuple(range(first, min(first + 2, requests)))
        sizes = [block // 2] + [(b + 1) * block for b in range(blocks)]
        cases = list(itertools.product(sizes, repeat=len(group)))
        place = 0
        for r in group:
            rank_of = sum((lengths[r] > size).astype(jnp.int32) for size in sizes[:-1])
            place = place * len(sizes) + rank_of
        choose(place, 0, cases, functools.partial(several, group))

    for out, k in zip(outs, order(owners)):
        mine = pl.ds(pl.multiple_of((me ^ k) * rows, rows), rows)
        for at in range(0, rank, LANES):
            out[:, at:at + LANES] = latents[at // LANES, mine, :].astype(jnp.bfloat16)


def in_hbm(*arrays):
    return [pltpu.with_memory_space_constraint(array, pltpu.HBM) for array in arrays]


def attend(query, cache, scales, lengths, owners):
    requests, heads, channels = query.shape
    cache_len = cache.shape[1]
    rank = channels - ROPE_DIM
    part = jax.ShapeDtypeStruct((heads // owners * requests, rank), jnp.bfloat16)
    return pl.pallas_call(
        functools.partial(attend_kernel, owners),
        out_shape=[part] * owners,
        in_specs=[pl.BlockSpec(memory_space=pl.ANY)] * 4,
        out_specs=[pl.BlockSpec(memory_space=pltpu.VMEM)] * owners,
        scratch_shapes=[
            pltpu.VMEM((rank // LANES, heads * requests, LANES), jnp.float32),
            pltpu.SMEM((requests,), jnp.int32),
            pltpu.VMEM((requests, channels, heads), jnp.bfloat16),
            pltpu.VMEM((channels,), jnp.float32),
            pltpu.VMEM((requests, channels, cache_len), jnp.bfloat16),
            pltpu.SemaphoreType.DMA((requests, cache_len // min(BLOCK, cache_len))),
            pltpu.SemaphoreType.DMA((2 + requests,)),
        ],
        compiler_params=pltpu.CompilerParams(vmem_limit_bytes=24 * 2**20),
        cost_estimate=pl.CostEstimate(
            flops=4 * requests * heads * channels * cache_len,
            bytes_accessed=2 * requests * channels * cache_len,
            transcendentals=requests * heads * cache_len,
        ),
        name="attend",
    )(*in_hbm(lengths, jnp.swapaxes(query, 1, 2), scales, jnp.swapaxes(cache, 1, 2)))


def stage_kernel(maps_hbm, after, maps, sem):
    copy = pltpu.make_async_copy(maps_hbm, maps, sem)
    copy.start()
    copy.wait()


def stage(maps, after):
    return pl.pallas_call(
        stage_kernel,
        out_shape=jax.ShapeDtypeStruct(maps.shape, maps.dtype),
        in_specs=[pl.BlockSpec(memory_space=pl.ANY)] * 2,
        out_specs=pl.BlockSpec(memory_space=pltpu.VMEM),
        scratch_shapes=[pltpu.SemaphoreType.DMA(())],
        compiler_params=pltpu.CompilerParams(vmem_limit_bytes=8 * 2**20),
        cost_estimate=pl.CostEstimate(
            flops=0, bytes_accessed=4 * maps.size, transcendentals=0
        ),
        name="stage",
    )(*in_hbm(maps), after)


def project_kernel(count, *refs):
    parts, maps, outs = refs[:count], refs[count], refs[count + 1:]
    local_heads, requests, width = outs[0].shape
    group = min(GROUP_ROWS // requests, local_heads)
    rows = group * requests
    for first in range(0, local_heads, group):
        here = slice(first * requests, first * requests + rows)
        mixed = jnp.concatenate([part[here, :] for part in parts], axis=0)
        wide = jnp.concatenate([maps[first + i] for i in range(group)], axis=1)
        values = jnp.dot(mixed, wide, preferred_element_type=jnp.float32)
        head = lax.broadcasted_iota(jnp.int32, (rows, width), 0) // requests
        for d, out in enumerate(outs):
            block = values[d * rows:(d + 1) * rows]
            own = block[:, :width]
            for i in range(1, group):
                own = jnp.where(head == i, block[:, i * width:(i + 1) * width], own)
            out[first:first + group] = own.astype(jnp.bfloat16).reshape(group, requests, width)


def project(parts, maps, requests):
    count = len(parts)
    local_heads, rank, width = maps.shape
    return pl.pallas_call(
        functools.partial(project_kernel, count),
        out_shape=[jax.ShapeDtypeStruct((local_heads, requests, width), jnp.bfloat16)] * count,
        in_specs=[pl.BlockSpec(memory_space=pltpu.VMEM)] * (count + 1),
        out_specs=[pl.BlockSpec(memory_space=pltpu.VMEM)] * count,
        compiler_params=pltpu.CompilerParams(vmem_limit_bytes=24 * 2**20),
        cost_estimate=pl.CostEstimate(
            flops=2 * count * requests * local_heads * rank * width,
            bytes_accessed=2 * local_heads * rank * width,
            transcendentals=0,
        ),
        name="project",
    )(*parts, maps)


def assemble_kernel(owners, *refs):
    parts, out, sems = refs[:owners], refs[owners], refs[owners + 1]
    me = lax.axis_index("tp")
    copies = [
        pltpu.make_async_copy(part, out.at[me ^ k], sems.at[k])
        for k, part in zip(order(owners), parts)
    ]
    for copy in copies:
        copy.start()
    for copy in copies:
        copy.wait()


def assemble(parts):
    owners = len(parts)
    return pl.pallas_call(
        functools.partial(assemble_kernel, owners),
        out_shape=pltpu.HBM((owners,) + parts[0].shape, parts[0].dtype),
        in_specs=[pl.BlockSpec(memory_space=pltpu.VMEM)] * owners,
        out_specs=pl.BlockSpec(memory_space=pltpu.HBM),
        scratch_shapes=[pltpu.SemaphoreType.DMA((owners,))],
        compiler_params=pltpu.CompilerParams(vmem_limit_bytes=2 * 2**20),
        name="assemble",
    )(*parts)


def exchange(parts):
    owners = len(parts)
    return [
        lax.ppermute(part, "tp", [(i, i ^ k) for i in range(owners)]) if k else part
        for k, part in zip(order(owners), parts)
    ]


def on_device(query, cache, scales, lengths, value_up):
    owners = lax.axis_size("tp")
    latents = attend(query, cache, scales, lengths, owners)
    maps = stage(value_up, latents[0])
    values = exchange(project(exchange(latents), maps, query.shape[0]))
    returned = assemble(values)
    _, local_heads, requests, width = returned.shape
    returned = returned.reshape(owners * local_heads, requests, width)
    return jnp.swapaxes(returned, 0, 1).reshape(requests, owners * local_heads * width)


def solution(mesh):
    in_specs = (
        P(("grp", "tp"), None, None),
        P(("grp", "tp"), None, None),
        P(),
        P(("grp", "tp")),
        P("tp", None, None),
    )
    out_specs = P(("grp", "tp"), None)
    return jax.shard_map(
        on_device, mesh=mesh, in_specs=in_specs, out_specs=out_specs, check_vma=False
    )
```

```python
import functools
import itertools
import math

import jax
import jax.numpy as jnp
from jax import lax
from jax.experimental import pallas as pl
from jax.experimental.pallas import tpu as pltpu
from jax.sharding import PartitionSpec as P

ROPE_DIM = 64
SOFTMAX_SCALE = (1.0 + 0.1 * math.log(40.0)) ** 2 / math.sqrt(192.0)
EXP2_SCALE = SOFTMAX_SCALE * math.log2(math.e)
BLOCK = 512
LANES = 128
GROUP_ROWS = 16


def order(owners):
    return [0] + list(range(owners - 1, 0, -1))


def choose(count, cases, act):
    if len(cases) == 1:
        act(cases[0])
        return
    lax.cond(
        functools.reduce(jnp.logical_and, [c == n for c, n in zip(count, cases[0])]),
        lambda: act(cases[0]),
        lambda: choose(count, cases[1:], act),
    )


def attend_kernel(owners, lengths_hbm, query_hbm, scales_hbm, cache, *refs):
    outs, (latents, lengths, query, scales, keys, sems, small_sems) = refs[:owners], refs[owners:]
    requests, channels, heads = query.shape
    rows, rank = outs[0].shape
    cache_len = cache.shape[2]
    block = min(BLOCK, cache_len)
    blocks = cache_len // block
    me = lax.axis_index("tp")

    def fetch(r, b):
        span = pl.ds(b * block, block)
        return pltpu.make_async_copy(cache.at[r, :, span], keys.at[r, :, span], sems.at[r, b])

    def ask(r):
        return pltpu.make_async_copy(query_hbm.at[r], query.at[r], small_sems.at[2 + r])

    lengths_copy = pltpu.make_async_copy(lengths_hbm, lengths, small_sems.at[0])
    scales_copy = pltpu.make_async_copy(scales_hbm, scales, small_sems.at[1])
    lengths_copy.start()
    scales_copy.start()
    for r in range(requests):
        ask(r).start()
        fetch(r, 0).start()
    lengths_copy.wait()
    for r in range(requests):
        for b in range(1, blocks):
            @pl.when(b * block < lengths[r])
            def _():
                fetch(r, b).start()
    scales_copy.wait()
    scale_row = scales[...].reshape(1, channels)

    def scale(r):
        ask(r).wait()
        return (query[r].astype(jnp.float32).T * scale_row).astype(jnp.bfloat16)

    def score(scaled, r, b, live):
        if r not in scaled:
            scaled[r] = scale(r)
        fetch(r, b).wait()
        span = slice(b * block, (b + 1) * block)
        part = jnp.dot(scaled[r], keys[r, :, span], preferred_element_type=jnp.float32)
        if b == live - 1:
            place = b * block + lax.broadcasted_iota(jnp.int32, part.shape, 1)
            part = jnp.where(place < lengths[r], part, -jnp.inf)
        return part

    def weigh(parts):
        top = functools.reduce(
            jnp.maximum, [jnp.max(part, axis=1, keepdims=True) for part in parts]
        )
        weights = [jnp.exp2((part - top) * EXP2_SCALE) for part in parts]
        total = sum(jnp.sum(weight, axis=1, keepdims=True) for weight in weights)
        return total, jnp.concatenate([weight.astype(jnp.bfloat16) for weight in weights], axis=1)

    def mix(weights, r):
        return lax.dot_general(
            weights, keys[r, :rank, :weights.shape[1]],
            (((1,), (1,)), ((), ())), preferred_element_type=jnp.float32,
        )

    def finish(r, total, mixture):
        latent = mixture * (1.0 / total) * scale_row[:, :rank]
        for at in range(0, rank, LANES):
            latents[at // LANES, pl.ds(r, heads, stride=requests), :] = latent[:, at:at + LANES]

    def several(group, live):
        scaled = {}
        units = [(r, 0, n) for r, n in zip(group, live)]
        units += [(r, b, n) for r, n in zip(group, live) for b in range(1, n)]
        parts = {r: [] for r in group}
        for r, b, n in units:
            parts[r].append(score(scaled, r, b, n))
        for r in group:
            total, weights = weigh(parts[r])
            finish(r, total, mix(weights, r))

    for first in range(0, requests, 2):
        group = tuple(range(first, min(first + 2, requests)))
        count = [(lengths[r] + (block - 1)) // block for r in group]
        cases = list(itertools.product(range(1, blocks + 1), repeat=len(group)))
        cases.sort(key=lambda live: (sum(live) <= blocks, sum(live), -max(live)))
        choose(count, cases, functools.partial(several, group))

    for out, k in zip(outs, order(owners)):
        mine = pl.ds(pl.multiple_of((me ^ k) * rows, rows), rows)
        for at in range(0, rank, LANES):
            out[:, at:at + LANES] = latents[at // LANES, mine, :].astype(jnp.bfloat16)


def in_hbm(*arrays):
    return [pltpu.with_memory_space_constraint(array, pltpu.HBM) for array in arrays]


def attend(query, cache, scales, lengths, owners):
    requests, heads, channels = query.shape
    cache_len = cache.shape[1]
    rank = channels - ROPE_DIM
    part = jax.ShapeDtypeStruct((heads // owners * requests, rank), jnp.bfloat16)
    return pl.pallas_call(
        functools.partial(attend_kernel, owners),
        out_shape=[part] * owners,
        in_specs=[pl.BlockSpec(memory_space=pl.ANY)] * 4,
        out_specs=[pl.BlockSpec(memory_space=pltpu.VMEM)] * owners,
        scratch_shapes=[
            pltpu.VMEM((rank // LANES, heads * requests, LANES), jnp.float32),
            pltpu.SMEM((requests,), jnp.int32),
            pltpu.VMEM((requests, channels, heads), jnp.bfloat16),
            pltpu.VMEM((channels,), jnp.float32),
            pltpu.VMEM((requests, channels, cache_len), jnp.bfloat16),
            pltpu.SemaphoreType.DMA((requests, cache_len // min(BLOCK, cache_len))),
            pltpu.SemaphoreType.DMA((2 + requests,)),
        ],
        compiler_params=pltpu.CompilerParams(vmem_limit_bytes=24 * 2**20),
        cost_estimate=pl.CostEstimate(
            flops=4 * requests * heads * channels * cache_len,
            bytes_accessed=2 * requests * channels * cache_len,
            transcendentals=requests * heads * cache_len,
        ),
        name="attend",
    )(*in_hbm(lengths, jnp.swapaxes(query, 1, 2), scales, jnp.swapaxes(cache, 1, 2)))


def stage_kernel(maps_hbm, after, maps, sem):
    copy = pltpu.make_async_copy(maps_hbm, maps, sem)
    copy.start()
    copy.wait()


def stage(maps, after):
    return pl.pallas_call(
        stage_kernel,
        out_shape=jax.ShapeDtypeStruct(maps.shape, maps.dtype),
        in_specs=[pl.BlockSpec(memory_space=pl.ANY)] * 2,
        out_specs=pl.BlockSpec(memory_space=pltpu.VMEM),
        scratch_shapes=[pltpu.SemaphoreType.DMA(())],
        compiler_params=pltpu.CompilerParams(vmem_limit_bytes=8 * 2**20),
        cost_estimate=pl.CostEstimate(
            flops=0, bytes_accessed=4 * maps.size, transcendentals=0
        ),
        name="stage",
    )(*in_hbm(maps), after)


def project_kernel(count, *refs):
    parts, maps, outs = refs[:count], refs[count], refs[count + 1:]
    local_heads, requests, width = outs[0].shape
    group = min(GROUP_ROWS // requests, local_heads)
    rows = group * requests
    for first in range(0, local_heads, group):
        here = slice(first * requests, first * requests + rows)
        mixed = jnp.concatenate([part[here, :] for part in parts], axis=0)
        wide = jnp.concatenate([maps[first + i] for i in range(group)], axis=1)
        values = jnp.dot(mixed, wide, preferred_element_type=jnp.float32)
        head = lax.broadcasted_iota(jnp.int32, (rows, width), 0) // requests
        for d, out in enumerate(outs):
            block = values[d * rows:(d + 1) * rows]
            own = block[:, :width]
            for i in range(1, group):
                own = jnp.where(head == i, block[:, i * width:(i + 1) * width], own)
            out[first:first + group] = own.astype(jnp.bfloat16).reshape(group, requests, width)


def project(parts, maps, requests):
    count = len(parts)
    local_heads, rank, width = maps.shape
    return pl.pallas_call(
        functools.partial(project_kernel, count),
        out_shape=[jax.ShapeDtypeStruct((local_heads, requests, width), jnp.bfloat16)] * count,
        in_specs=[pl.BlockSpec(memory_space=pltpu.VMEM)] * (count + 1),
        out_specs=[pl.BlockSpec(memory_space=pltpu.VMEM)] * count,
        compiler_params=pltpu.CompilerParams(vmem_limit_bytes=24 * 2**20),
        cost_estimate=pl.CostEstimate(
            flops=2 * count * requests * local_heads * rank * width,
            bytes_accessed=2 * local_heads * rank * width,
            transcendentals=0,
        ),
        name="project",
    )(*parts, maps)


def assemble_kernel(owners, *refs):
    parts, out, sems = refs[:owners], refs[owners], refs[owners + 1]
    me = lax.axis_index("tp")
    copies = [
        pltpu.make_async_copy(part, out.at[me ^ k], sems.at[k])
        for k, part in zip(order(owners), parts)
    ]
    for copy in copies:
        copy.start()
    for copy in copies:
        copy.wait()


def assemble(parts):
    owners = len(parts)
    return pl.pallas_call(
        functools.partial(assemble_kernel, owners),
        out_shape=pltpu.HBM((owners,) + parts[0].shape, parts[0].dtype),
        in_specs=[pl.BlockSpec(memory_space=pltpu.VMEM)] * owners,
        out_specs=pl.BlockSpec(memory_space=pltpu.HBM),
        scratch_shapes=[pltpu.SemaphoreType.DMA((owners,))],
        compiler_params=pltpu.CompilerParams(vmem_limit_bytes=2 * 2**20),
        name="assemble",
    )(*parts)


def exchange(parts):
    owners = len(parts)
    return [
        lax.ppermute(part, "tp", [(i, i ^ k) for i in range(owners)]) if k else part
        for k, part in zip(order(owners), parts)
    ]


def on_device(query, cache, scales, lengths, value_up):
    owners = lax.axis_size("tp")
    latents = attend(query, cache, scales, lengths, owners)
    maps = stage(value_up, latents[0])
    values = exchange(project(exchange(latents), maps, query.shape[0]))
    returned = assemble(values)
    _, local_heads, requests, width = returned.shape
    returned = returned.reshape(owners * local_heads, requests, width)
    return jnp.swapaxes(returned, 0, 1).reshape(requests, owners * local_heads * width)


def solution(mesh):
    in_specs = (
        P(("grp", "tp"), None, None),
        P(("grp", "tp"), None, None),
        P(),
        P(("grp", "tp")),
        P("tp", None, None),
    )
    out_specs = P(("grp", "tp"), None)
    return jax.shard_map(
        on_device, mesh=mesh, in_specs=in_specs, out_specs=out_specs, check_vma=False
    )
```

```python
import functools
import itertools
import math

import jax
import jax.numpy as jnp
from jax import lax
from jax.experimental import pallas as pl
from jax.experimental.pallas import tpu as pltpu
from jax.sharding import PartitionSpec as P

ROPE_DIM = 64
SOFTMAX_SCALE = (1.0 + 0.1 * math.log(40.0)) ** 2 / math.sqrt(192.0)
EXP2_SCALE = SOFTMAX_SCALE * math.log2(math.e)
BLOCK = 512
LANES = 128
GROUP_ROWS = 16


def order(owners):
    return [0] + list(range(owners - 1, 0, -1))


def attend_kernel(owners, lengths_hbm, query_hbm, scales_hbm, cache, *refs):
    outs, (latents, lengths, query, scales, keys, sems, small_sems) = refs[:owners], refs[owners:]
    requests, channels, heads = query.shape
    rows, rank = outs[0].shape
    cache_len = cache.shape[2]
    block = min(BLOCK, cache_len)
    blocks = cache_len // block
    me = lax.axis_index("tp")

    def fetch(r, b):
        span = pl.ds(b * block, block)
        return pltpu.make_async_copy(cache.at[r, :, span], keys.at[r, :, span], sems.at[r, b])

    def ask(r):
        return pltpu.make_async_copy(query_hbm.at[r], query.at[r], small_sems.at[2 + r])

    lengths_copy = pltpu.make_async_copy(lengths_hbm, lengths, small_sems.at[0])
    scales_copy = pltpu.make_async_copy(scales_hbm, scales, small_sems.at[1])
    lengths_copy.start()
    scales_copy.start()
    for r in range(requests):
        ask(r).start()
        fetch(r, 0).start()
    lengths_copy.wait()
    for r in range(requests):
        for b in range(1, blocks):
            @pl.when(b * block < lengths[r])
            def _():
                fetch(r, b).start()
    scales_copy.wait()
    scale_row = scales[...].reshape(1, channels)

    def scale(r):
        ask(r).wait()
        return (query[r].astype(jnp.float32).T * scale_row).astype(jnp.bfloat16)

    def score(scaled, r, b, live):
        if r not in scaled:
            scaled[r] = scale(r)
        fetch(r, b).wait()
        span = slice(b * block, (b + 1) * block)
        part = jnp.dot(scaled[r], keys[r, :, span], preferred_element_type=jnp.float32)
        if b == live - 1:
            place = b * block + lax.broadcasted_iota(jnp.int32, part.shape, 1)
            part = jnp.where(place < lengths[r], part, -jnp.inf)
        return part

    def weigh(part, r, b):
        top = jnp.max(part, axis=1, keepdims=True)
        weight = jnp.exp2((part - top) * EXP2_SCALE)
        total = jnp.sum(weight, axis=1, keepdims=True)
        mixture = lax.dot_general(
            weight.astype(jnp.bfloat16), keys[r, :rank, b * block:(b + 1) * block],
            (((1,), (1,)), ((), ())), preferred_element_type=jnp.float32,
        )
        return top, total, mixture

    def merge(one, two):
        top = jnp.maximum(one[0], two[0])
        first = jnp.exp2((one[0] - top) * EXP2_SCALE)
        second = jnp.exp2((two[0] - top) * EXP2_SCALE)
        return (top,) + tuple(x * first + y * second for x, y in zip(one[1:], two[1:]))

    def finish(r, total, mixture):
        latent = mixture * (1.0 / total) * scale_row[:, :rank]
        for at in range(0, rank, LANES):
            latents[at // LANES, pl.ds(r, heads, stride=requests), :] = latent[:, at:at + LANES]

    def several(group, live):
        scaled = {}
        units = [(r, 0, n) for r, n in zip(group, live)]
        units += [(r, b, n) for r, n in zip(group, live) for b in range(1, n)]
        part = score(scaled, *units[0])
        state = {}
        for i, (r, b, n) in enumerate(units):
            ahead = score(scaled, *units[i + 1]) if i + 1 < len(units) else None
            done = weigh(part, r, b)
            state[r] = merge(state[r], done) if b else done
            if b == n - 1:
                finish(r, *state[r][1:])
            part = ahead

    for first in range(0, requests, 2):
        group = tuple(range(first, min(first + 2, requests)))
        count = [(lengths[r] + (block - 1)) // block for r in group]
        for live in itertools.product(range(1, blocks + 1), repeat=len(group)):
            @pl.when(functools.reduce(jnp.logical_and, [c == n for c, n in zip(count, live)]))
            def _():
                several(group, live)

    for out, k in zip(outs, order(owners)):
        mine = pl.ds(pl.multiple_of((me ^ k) * rows, rows), rows)
        for at in range(0, rank, LANES):
            out[:, at:at + LANES] = latents[at // LANES, mine, :].astype(jnp.bfloat16)


def in_hbm(*arrays):
    return [pltpu.with_memory_space_constraint(array, pltpu.HBM) for array in arrays]


def attend(query, cache, scales, lengths, owners):
    requests, heads, channels = query.shape
    cache_len = cache.shape[1]
    rank = channels - ROPE_DIM
    part = jax.ShapeDtypeStruct((heads // owners * requests, rank), jnp.bfloat16)
    return pl.pallas_call(
        functools.partial(attend_kernel, owners),
        out_shape=[part] * owners,
        in_specs=[pl.BlockSpec(memory_space=pl.ANY)] * 4,
        out_specs=[pl.BlockSpec(memory_space=pltpu.VMEM)] * owners,
        scratch_shapes=[
            pltpu.VMEM((rank // LANES, heads * requests, LANES), jnp.float32),
            pltpu.SMEM((requests,), jnp.int32),
            pltpu.VMEM((requests, channels, heads), jnp.bfloat16),
            pltpu.VMEM((channels,), jnp.float32),
            pltpu.VMEM((requests, channels, cache_len), jnp.bfloat16),
            pltpu.SemaphoreType.DMA((requests, cache_len // min(BLOCK, cache_len))),
            pltpu.SemaphoreType.DMA((2 + requests,)),
        ],
        compiler_params=pltpu.CompilerParams(vmem_limit_bytes=24 * 2**20),
        cost_estimate=pl.CostEstimate(
            flops=4 * requests * heads * channels * cache_len,
            bytes_accessed=2 * requests * channels * cache_len,
            transcendentals=requests * heads * cache_len,
        ),
        name="attend",
    )(*in_hbm(lengths, jnp.swapaxes(query, 1, 2), scales, jnp.swapaxes(cache, 1, 2)))


def stage_kernel(maps_hbm, after, maps, sem):
    copy = pltpu.make_async_copy(maps_hbm, maps, sem)
    copy.start()
    copy.wait()


def stage(maps, after):
    return pl.pallas_call(
        stage_kernel,
        out_shape=jax.ShapeDtypeStruct(maps.shape, maps.dtype),
        in_specs=[pl.BlockSpec(memory_space=pl.ANY)] * 2,
        out_specs=pl.BlockSpec(memory_space=pltpu.VMEM),
        scratch_shapes=[pltpu.SemaphoreType.DMA(())],
        compiler_params=pltpu.CompilerParams(vmem_limit_bytes=8 * 2**20),
        cost_estimate=pl.CostEstimate(
            flops=0, bytes_accessed=4 * maps.size, transcendentals=0
        ),
        name="stage",
    )(*in_hbm(maps), after)


def project_kernel(count, *refs):
    parts, maps, outs = refs[:count], refs[count], refs[count + 1:]
    local_heads, requests, width = outs[0].shape
    group = min(GROUP_ROWS // requests, local_heads)
    rows = group * requests
    for first in range(0, local_heads, group):
        here = slice(first * requests, first * requests + rows)
        mixed = jnp.concatenate([part[here, :] for part in parts], axis=0)
        wide = jnp.concatenate([maps[first + i] for i in range(group)], axis=1)
        values = jnp.dot(mixed, wide, preferred_element_type=jnp.float32)
        head = lax.broadcasted_iota(jnp.int32, (rows, width), 0) // requests
        for d, out in enumerate(outs):
            block = values[d * rows:(d + 1) * rows]
            own = block[:, :width]
            for i in range(1, group):
                own = jnp.where(head == i, block[:, i * width:(i + 1) * width], own)
            out[first:first + group] = own.astype(jnp.bfloat16).reshape(group, requests, width)


def project(parts, maps, requests):
    count = len(parts)
    local_heads, rank, width = maps.shape
    return pl.pallas_call(
        functools.partial(project_kernel, count),
        out_shape=[jax.ShapeDtypeStruct((local_heads, requests, width), jnp.bfloat16)] * count,
        in_specs=[pl.BlockSpec(memory_space=pltpu.VMEM)] * (count + 1),
        out_specs=[pl.BlockSpec(memory_space=pltpu.VMEM)] * count,
        compiler_params=pltpu.CompilerParams(vmem_limit_bytes=24 * 2**20),
        cost_estimate=pl.CostEstimate(
            flops=2 * count * requests * local_heads * rank * width,
            bytes_accessed=2 * local_heads * rank * width,
            transcendentals=0,
        ),
        name="project",
    )(*parts, maps)


def assemble_kernel(owners, *refs):
    parts, out, sems = refs[:owners], refs[owners], refs[owners + 1]
    me = lax.axis_index("tp")
    copies = [
        pltpu.make_async_copy(part, out.at[me ^ k], sems.at[k])
        for k, part in zip(order(owners), parts)
    ]
    for copy in copies:
        copy.start()
    for copy in copies:
        copy.wait()


def assemble(parts):
    owners = len(parts)
    return pl.pallas_call(
        functools.partial(assemble_kernel, owners),
        out_shape=pltpu.HBM((owners,) + parts[0].shape, parts[0].dtype),
        in_specs=[pl.BlockSpec(memory_space=pltpu.VMEM)] * owners,
        out_specs=pl.BlockSpec(memory_space=pltpu.HBM),
        scratch_shapes=[pltpu.SemaphoreType.DMA((owners,))],
        compiler_params=pltpu.CompilerParams(vmem_limit_bytes=2 * 2**20),
        name="assemble",
    )(*parts)


def exchange(parts):
    owners = len(parts)
    groups = lax.axis_size("grp")

    def pairs(k):
        return [
            (g * owners + i, (g ^ 1) * owners + (i ^ k))
            for g in range(groups) for i in range(owners)
        ]

    return [
        lax.ppermute(part, ("grp", "tp"), pairs(k)) if k else part
        for k, part in zip(order(owners), parts)
    ]


def on_device(query, cache, scales, lengths, value_up):
    owners = lax.axis_size("tp")
    latents = attend(query, cache, scales, lengths, owners)
    maps = stage(value_up, latents[0])
    values = exchange(project(exchange(latents), maps, query.shape[0]))
    returned = assemble(values)
    _, local_heads, requests, width = returned.shape
    returned = returned.reshape(owners * local_heads, requests, width)
    return jnp.swapaxes(returned, 0, 1).reshape(requests, owners * local_heads * width)


def solution(mesh):
    in_specs = (
        P(("grp", "tp"), None, None),
        P(("grp", "tp"), None, None),
        P(),
        P(("grp", "tp")),
        P("tp", None, None),
    )
    out_specs = P(("grp", "tp"), None)
    return jax.shard_map(
        on_device, mesh=mesh, in_specs=in_specs, out_specs=out_specs, check_vma=False
    )
```

```python
import functools
import itertools
import math

import jax
import jax.numpy as jnp
from jax import lax
from jax.experimental import pallas as pl
from jax.experimental.pallas import tpu as pltpu
from jax.sharding import PartitionSpec as P

ROPE_DIM = 64
SOFTMAX_SCALE = (1.0 + 0.1 * math.log(40.0)) ** 2 / math.sqrt(192.0)
EXP2_SCALE = SOFTMAX_SCALE * math.log2(math.e)
BLOCK = 512
LANES = 128
PIECES = 4
GROUP_ROWS = 16


def order(owners):
    return [0] + list(range(owners - 1, 0, -1))


def attend_kernel(owners, lengths_hbm, query_hbm, scales_hbm, cache, *refs):
    outs, (latents, lengths, query, scales, keys, sems, small_sems, first_sems) = refs[:owners], refs[owners:]
    requests, channels, heads = query.shape
    rows, rank = outs[0].shape
    cache_len = cache.shape[2]
    block = min(BLOCK, cache_len)
    blocks = cache_len // block
    me = lax.axis_index("tp")

    def pieces(r, b):
        span = pl.ds(b * block, block)
        if (r, b) != (0, 0):
            return [pltpu.make_async_copy(cache.at[r, :, span], keys.at[r, :, span], sems.at[r, b])]
        size = channels // PIECES
        return [
            pltpu.make_async_copy(
                cache.at[r, pl.ds(i * size, size), span], keys.at[r, pl.ds(i * size, size), span],
                first_sems.at[i],
            )
            for i in range(PIECES)
        ]

    def fetch(r, b):
        for copy in pieces(r, b):
            copy.start()

    def arrive(r, b):
        for copy in pieces(r, b):
            copy.wait()

    def ask(r):
        return pltpu.make_async_copy(query_hbm.at[r], query.at[r], small_sems.at[2 + r])

    lengths_copy = pltpu.make_async_copy(lengths_hbm, lengths, small_sems.at[0])
    scales_copy = pltpu.make_async_copy(scales_hbm, scales, small_sems.at[1])
    lengths_copy.start()
    scales_copy.start()
    for r in range(requests):
        ask(r).start()
        fetch(r, 0)
    lengths_copy.wait()
    for r in range(requests):
        for b in range(1, blocks):
            @pl.when(b * block < lengths[r])
            def _():
                fetch(r, b)
    scales_copy.wait()
    scale_row = scales[...].reshape(1, channels)

    def scale(r):
        ask(r).wait()
        return (query[r].astype(jnp.float32).T * scale_row).astype(jnp.bfloat16)

    def score(scaled, r, b, live):
        if r not in scaled:
            scaled[r] = scale(r)
        arrive(r, b)
        span = slice(b * block, (b + 1) * block)
        part = jnp.dot(scaled[r], keys[r, :, span], preferred_element_type=jnp.float32)
        if b == live - 1:
            place = b * block + lax.broadcasted_iota(jnp.int32, part.shape, 1)
            part = jnp.where(place < lengths[r], part, -jnp.inf)
        return part

    def weigh(part, r, b):
        top = jnp.max(part, axis=1, keepdims=True)
        weight = jnp.exp2((part - top) * EXP2_SCALE)
        total = jnp.sum(weight, axis=1, keepdims=True)
        mixture = lax.dot_general(
            weight.astype(jnp.bfloat16), keys[r, :rank, b * block:(b + 1) * block],
            (((1,), (1,)), ((), ())), preferred_element_type=jnp.float32,
        )
        return top, total, mixture

    def merge(one, two):
        top = jnp.maximum(one[0], two[0])
        first = jnp.exp2((one[0] - top) * EXP2_SCALE)
        second = jnp.exp2((two[0] - top) * EXP2_SCALE)
        return (top,) + tuple(x * first + y * second for x, y in zip(one[1:], two[1:]))

    def finish(r, total, mixture):
        latent = mixture * (1.0 / total) * scale_row[:, :rank]
        for at in range(0, rank, LANES):
            latents[at // LANES, pl.ds(r, heads, stride=requests), :] = latent[:, at:at + LANES]

    def several(group, live):
        scaled = {}
        units = [(r, 0, n) for r, n in zip(group, live)]
        units += [(r, b, n) for r, n in zip(group, live) for b in range(1, n)]
        part = score(scaled, *units[0])
        state = {}
        for i, (r, b, n) in enumerate(units):
            ahead = score(scaled, *units[i + 1]) if i + 1 < len(units) else None
            done = weigh(part, r, b)
            state[r] = merge(state[r], done) if b else done
            if b == n - 1:
                finish(r, *state[r][1:])
            part = ahead

    for first in range(0, requests, 2):
        group = tuple(range(first, min(first + 2, requests)))
        count = [(lengths[r] + (block - 1)) // block for r in group]
        for live in itertools.product(range(1, blocks + 1), repeat=len(group)):
            @pl.when(functools.reduce(jnp.logical_and, [c == n for c, n in zip(count, live)]))
            def _():
                several(group, live)

    for out, k in zip(outs, order(owners)):
        mine = pl.ds(pl.multiple_of((me ^ k) * rows, rows), rows)
        for at in range(0, rank, LANES):
            out[:, at:at + LANES] = latents[at // LANES, mine, :].astype(jnp.bfloat16)


def in_hbm(*arrays):
    return [pltpu.with_memory_space_constraint(array, pltpu.HBM) for array in arrays]


def attend(query, cache, scales, lengths, owners):
    requests, heads, channels = query.shape
    cache_len = cache.shape[1]
    rank = channels - ROPE_DIM
    part = jax.ShapeDtypeStruct((heads // owners * requests, rank), jnp.bfloat16)
    return pl.pallas_call(
        functools.partial(attend_kernel, owners),
        out_shape=[part] * owners,
        in_specs=[pl.BlockSpec(memory_space=pl.ANY)] * 4,
        out_specs=[pl.BlockSpec(memory_space=pltpu.VMEM)] * owners,
        scratch_shapes=[
            pltpu.VMEM((rank // LANES, heads * requests, LANES), jnp.float32),
            pltpu.SMEM((requests,), jnp.int32),
            pltpu.VMEM((requests, channels, heads), jnp.bfloat16),
            pltpu.VMEM((channels,), jnp.float32),
            pltpu.VMEM((requests, channels, cache_len), jnp.bfloat16),
            pltpu.SemaphoreType.DMA((requests, cache_len // min(BLOCK, cache_len))),
            pltpu.SemaphoreType.DMA((2 + requests,)),
            pltpu.SemaphoreType.DMA((PIECES,)),
        ],
        compiler_params=pltpu.CompilerParams(vmem_limit_bytes=24 * 2**20),
        cost_estimate=pl.CostEstimate(
            flops=4 * requests * heads * channels * cache_len,
            bytes_accessed=2 * requests * channels * cache_len,
            transcendentals=requests * heads * cache_len,
        ),
        name="attend",
    )(*in_hbm(lengths, jnp.swapaxes(query, 1, 2), scales, jnp.swapaxes(cache, 1, 2)))


def stage_kernel(maps_hbm, after, maps, sem):
    copy = pltpu.make_async_copy(maps_hbm, maps, sem)
    copy.start()
    copy.wait()


def stage(maps, after):
    return pl.pallas_call(
        stage_kernel,
        out_shape=jax.ShapeDtypeStruct(maps.shape, maps.dtype),
        in_specs=[pl.BlockSpec(memory_space=pl.ANY)] * 2,
        out_specs=pl.BlockSpec(memory_space=pltpu.VMEM),
        scratch_shapes=[pltpu.SemaphoreType.DMA(())],
        compiler_params=pltpu.CompilerParams(vmem_limit_bytes=8 * 2**20),
        cost_estimate=pl.CostEstimate(
            flops=0, bytes_accessed=4 * maps.size, transcendentals=0
        ),
        name="stage",
    )(*in_hbm(maps), after)


def project_kernel(count, *refs):
    parts, maps, outs = refs[:count], refs[count], refs[count + 1:]
    local_heads, requests, width = outs[0].shape
    group = min(GROUP_ROWS // requests, local_heads)
    rows = group * requests
    for first in range(0, local_heads, group):
        here = slice(first * requests, first * requests + rows)
        mixed = jnp.concatenate([part[here, :] for part in parts], axis=0)
        wide = jnp.concatenate([maps[first + i] for i in range(group)], axis=1)
        values = jnp.dot(mixed, wide, preferred_element_type=jnp.float32)
        head = lax.broadcasted_iota(jnp.int32, (rows, width), 0) // requests
        for d, out in enumerate(outs):
            block = values[d * rows:(d + 1) * rows]
            own = block[:, :width]
            for i in range(1, group):
                own = jnp.where(head == i, block[:, i * width:(i + 1) * width], own)
            out[first:first + group] = own.astype(jnp.bfloat16).reshape(group, requests, width)


def project(parts, maps, requests):
    count = len(parts)
    local_heads, rank, width = maps.shape
    return pl.pallas_call(
        functools.partial(project_kernel, count),
        out_shape=[jax.ShapeDtypeStruct((local_heads, requests, width), jnp.bfloat16)] * count,
        in_specs=[pl.BlockSpec(memory_space=pltpu.VMEM)] * (count + 1),
        out_specs=[pl.BlockSpec(memory_space=pltpu.VMEM)] * count,
        compiler_params=pltpu.CompilerParams(vmem_limit_bytes=24 * 2**20),
        cost_estimate=pl.CostEstimate(
            flops=2 * count * requests * local_heads * rank * width,
            bytes_accessed=2 * local_heads * rank * width,
            transcendentals=0,
        ),
        name="project",
    )(*parts, maps)


def assemble_kernel(owners, *refs):
    parts, out, sems = refs[:owners], refs[owners], refs[owners + 1]
    me = lax.axis_index("tp")
    copies = [
        pltpu.make_async_copy(part, out.at[me ^ k], sems.at[k])
        for k, part in zip(order(owners), parts)
    ]
    for copy in copies:
        copy.start()
    for copy in copies:
        copy.wait()


def assemble(parts):
    owners = len(parts)
    return pl.pallas_call(
        functools.partial(assemble_kernel, owners),
        out_shape=pltpu.HBM((owners,) + parts[0].shape, parts[0].dtype),
        in_specs=[pl.BlockSpec(memory_space=pltpu.VMEM)] * owners,
        out_specs=pl.BlockSpec(memory_space=pltpu.HBM),
        scratch_shapes=[pltpu.SemaphoreType.DMA((owners,))],
        compiler_params=pltpu.CompilerParams(vmem_limit_bytes=2 * 2**20),
        name="assemble",
    )(*parts)


def exchange(parts):
    owners = len(parts)
    groups = lax.axis_size("grp")
    flip = 1 - groups % 2

    def pairs(k):
        return [
            (g * owners + i, (g ^ flip) * owners + (i ^ k))
            for g in range(groups) for i in range(owners)
        ]

    return [
        lax.ppermute(part, ("grp", "tp"), pairs(k)) if k else part
        for k, part in zip(order(owners), parts)
    ]


def on_device(query, cache, scales, lengths, value_up):
    owners = lax.axis_size("tp")
    latents = attend(query, cache, scales, lengths, owners)
    maps = stage(value_up, latents[0])
    values = exchange(project(exchange(latents), maps, query.shape[0]))
    returned = assemble(values)
    _, local_heads, requests, width = returned.shape
    returned = returned.reshape(owners * local_heads, requests, width)
    return jnp.swapaxes(returned, 0, 1).reshape(requests, owners * local_heads * width)


def solution(mesh):
    in_specs = (
        P(("grp", "tp"), None, None),
        P(("grp", "tp"), None, None),
        P(),
        P(("grp", "tp")),
        P("tp", None, None),
    )
    out_specs = P(("grp", "tp"), None)
    return jax.shard_map(
        on_device, mesh=mesh, in_specs=in_specs, out_specs=out_specs, check_vma=False
    )
```

```python
import functools
import itertools
import math

import jax
import jax.numpy as jnp
from jax import lax
from jax.experimental import pallas as pl
from jax.experimental.pallas import tpu as pltpu
from jax.sharding import PartitionSpec as P

ROPE_DIM = 64
SOFTMAX_SCALE = (1.0 + 0.1 * math.log(40.0)) ** 2 / math.sqrt(192.0)
EXP2_SCALE = SOFTMAX_SCALE * math.log2(math.e)
BLOCK = 512
LANES = 128
GROUP_ROWS = 16


def order(owners):
    return [0, owners - 1] + list(range(1, owners - 1))


def attend_kernel(owners, lengths_hbm, query_hbm, scales_hbm, cache, *refs):
    outs, (latents, lengths, query, scales, keys, sems, small_sems) = refs[:owners], refs[owners:]
    requests, channels, heads = query.shape
    rows, rank = outs[0].shape
    cache_len = cache.shape[2]
    block = min(BLOCK, cache_len)
    blocks = cache_len // block
    me = lax.axis_index("tp")

    def fetch(r, b):
        span = pl.ds(b * block, block)
        return pltpu.make_async_copy(cache.at[r, :, span], keys.at[r, :, span], sems.at[r, b])

    lengths_copy = pltpu.make_async_copy(lengths_hbm, lengths, small_sems.at[0])
    scales_copy = pltpu.make_async_copy(scales_hbm, scales, small_sems.at[1])
    query_copy = pltpu.make_async_copy(query_hbm, query, small_sems.at[2])
    lengths_copy.start()
    query_copy.start()
    scales_copy.start()
    for r in range(requests):
        fetch(r, 0).start()
    lengths_copy.wait()
    for r in range(requests):
        for b in range(1, blocks):
            @pl.when(b * block < lengths[r])
            def _():
                fetch(r, b).start()
    query_copy.wait()
    scales_copy.wait()
    scale_row = scales[...].reshape(1, channels)

    def scale(r):
        return (query[r].astype(jnp.float32).T * scale_row).astype(jnp.bfloat16)

    def score(scaled, r, b, live):
        if r not in scaled:
            scaled[r] = scale(r)
        fetch(r, b).wait()
        span = slice(b * block, (b + 1) * block)
        part = jnp.dot(scaled[r], keys[r, :, span], preferred_element_type=jnp.float32)
        if b == live - 1:
            place = b * block + lax.broadcasted_iota(jnp.int32, part.shape, 1)
            part = jnp.where(place < lengths[r], part, -jnp.inf)
        return part

    def weigh(part, r, b):
        top = jnp.max(part, axis=1, keepdims=True)
        weight = jnp.exp2((part - top) * EXP2_SCALE)
        total = jnp.sum(weight, axis=1, keepdims=True)
        mixture = lax.dot_general(
            weight.astype(jnp.bfloat16), keys[r, :rank, b * block:(b + 1) * block],
            (((1,), (1,)), ((), ())), preferred_element_type=jnp.float32,
        )
        return top, total, mixture

    def merge(one, two):
        top = jnp.maximum(one[0], two[0])
        first = jnp.exp2((one[0] - top) * EXP2_SCALE)
        second = jnp.exp2((two[0] - top) * EXP2_SCALE)
        return (top,) + tuple(x * first + y * second for x, y in zip(one[1:], two[1:]))

    def finish(r, total, mixture):
        latent = mixture * (1.0 / total) * scale_row[:, :rank]
        for at in range(0, rank, LANES):
            latents[at // LANES, pl.ds(r, heads, stride=requests), :] = latent[:, at:at + LANES]

    def several(group, live):
        scaled = {}
        units = [(r, 0, n) for r, n in zip(group, live)]
        units += [(r, b, n) for r, n in zip(group, live) for b in range(1, n)]
        part = score(scaled, *units[0])
        state = {}
        for i, (r, b, n) in enumerate(units):
            ahead = score(scaled, *units[i + 1]) if i + 1 < len(units) else None
            done = weigh(part, r, b)
            state[r] = merge(state[r], done) if b else done
            if b == n - 1:
                finish(r, *state[r][1:])
            part = ahead

    for first in range(0, requests, 2):
        group = tuple(range(first, min(first + 2, requests)))
        count = [(lengths[r] + (block - 1)) // block for r in group]
        for live in itertools.product(range(1, blocks + 1), repeat=len(group)):
            @pl.when(functools.reduce(jnp.logical_and, [c == n for c, n in zip(count, live)]))
            def _():
                several(group, live)

    for out, k in zip(outs, order(owners)):
        mine = pl.ds(pl.multiple_of((me ^ k) * rows, rows), rows)
        for at in range(0, rank, LANES):
            out[:, at:at + LANES] = latents[at // LANES, mine, :].astype(jnp.bfloat16)


def in_hbm(*arrays):
    return [pltpu.with_memory_space_constraint(array, pltpu.HBM) for array in arrays]


def attend(query, cache, scales, lengths, owners):
    requests, heads, channels = query.shape
    cache_len = cache.shape[1]
    rank = channels - ROPE_DIM
    part = jax.ShapeDtypeStruct((heads // owners * requests, rank), jnp.bfloat16)
    return pl.pallas_call(
        functools.partial(attend_kernel, owners),
        out_shape=[part] * owners,
        in_specs=[pl.BlockSpec(memory_space=pl.ANY)] * 4,
        out_specs=[pl.BlockSpec(memory_space=pltpu.VMEM)] * owners,
        scratch_shapes=[
            pltpu.VMEM((rank // LANES, heads * requests, LANES), jnp.float32),
            pltpu.SMEM((requests,), jnp.int32),
            pltpu.VMEM((requests, channels, heads), jnp.bfloat16),
            pltpu.VMEM((channels,), jnp.float32),
            pltpu.VMEM((requests, channels, cache_len), jnp.bfloat16),
            pltpu.SemaphoreType.DMA((requests, cache_len // min(BLOCK, cache_len))),
            pltpu.SemaphoreType.DMA((3,)),
        ],
        compiler_params=pltpu.CompilerParams(vmem_limit_bytes=24 * 2**20),
        cost_estimate=pl.CostEstimate(
            flops=4 * requests * heads * channels * cache_len,
            bytes_accessed=2 * requests * channels * cache_len,
            transcendentals=requests * heads * cache_len,
        ),
        name="attend",
    )(*in_hbm(lengths, jnp.swapaxes(query, 1, 2), scales, jnp.swapaxes(cache, 1, 2)))


def stage_kernel(maps_hbm, after, maps, sem):
    copy = pltpu.make_async_copy(maps_hbm, maps, sem)
    copy.start()
    copy.wait()


def stage(maps, after):
    return pl.pallas_call(
        stage_kernel,
        out_shape=jax.ShapeDtypeStruct(maps.shape, maps.dtype),
        in_specs=[pl.BlockSpec(memory_space=pl.ANY)] * 2,
        out_specs=pl.BlockSpec(memory_space=pltpu.VMEM),
        scratch_shapes=[pltpu.SemaphoreType.DMA(())],
        compiler_params=pltpu.CompilerParams(vmem_limit_bytes=8 * 2**20),
        cost_estimate=pl.CostEstimate(
            flops=0, bytes_accessed=4 * maps.size, transcendentals=0
        ),
        name="stage",
    )(*in_hbm(maps), after)


def project_kernel(count, *refs):
    parts, maps, outs = refs[:count], refs[count], refs[count + 1:]
    local_heads, requests, width = outs[0].shape
    group = min(GROUP_ROWS // requests, local_heads)
    rows = group * requests
    for first in range(0, local_heads, group):
        here = slice(first * requests, first * requests + rows)
        mixed = jnp.concatenate([part[here, :] for part in parts], axis=0)
        wide = jnp.concatenate([maps[first + i] for i in range(group)], axis=1)
        values = jnp.dot(mixed, wide, preferred_element_type=jnp.float32)
        head = lax.broadcasted_iota(jnp.int32, (rows, width), 0) // requests
        for d, out in enumerate(outs):
            block = values[d * rows:(d + 1) * rows]
            own = block[:, :width]
            for i in range(1, group):
                own = jnp.where(head == i, block[:, i * width:(i + 1) * width], own)
            out[first:first + group] = own.astype(jnp.bfloat16).reshape(group, requests, width)


def project(parts, maps, requests):
    count = len(parts)
    local_heads, rank, width = maps.shape
    return pl.pallas_call(
        functools.partial(project_kernel, count),
        out_shape=[jax.ShapeDtypeStruct((local_heads, requests, width), jnp.bfloat16)] * count,
        in_specs=[pl.BlockSpec(memory_space=pltpu.VMEM)] * (count + 1),
        out_specs=[pl.BlockSpec(memory_space=pltpu.VMEM)] * count,
        compiler_params=pltpu.CompilerParams(vmem_limit_bytes=24 * 2**20),
        cost_estimate=pl.CostEstimate(
            flops=2 * count * requests * local_heads * rank * width,
            bytes_accessed=2 * local_heads * rank * width,
            transcendentals=0,
        ),
        name="project",
    )(*parts, maps)


def assemble_kernel(owners, *refs):
    parts, out, sems = refs[:owners], refs[owners], refs[owners + 1]
    me = lax.axis_index("tp")
    copies = [
        pltpu.make_async_copy(part, out.at[me ^ k], sems.at[k])
        for k, part in zip(order(owners), parts)
    ]
    for copy in copies:
        copy.start()
    for copy in copies:
        copy.wait()


def assemble(parts):
    owners = len(parts)
    return pl.pallas_call(
        functools.partial(assemble_kernel, owners),
        out_shape=pltpu.HBM((owners,) + parts[0].shape, parts[0].dtype),
        in_specs=[pl.BlockSpec(memory_space=pltpu.VMEM)] * owners,
        out_specs=pl.BlockSpec(memory_space=pltpu.HBM),
        scratch_shapes=[pltpu.SemaphoreType.DMA((owners,))],
        compiler_params=pltpu.CompilerParams(vmem_limit_bytes=2 * 2**20),
        name="assemble",
    )(*parts)


def exchange(parts):
    owners = len(parts)
    groups = lax.axis_size("grp")
    flip = 1 - groups % 2

    def pairs(k):
        return [
            (g * owners + i, (g ^ flip) * owners + (i ^ k))
            for g in range(groups) for i in range(owners)
        ]

    return [
        lax.ppermute(part, ("grp", "tp"), pairs(k)) if k else part
        for k, part in zip(order(owners), parts)
    ]


def on_device(query, cache, scales, lengths, value_up):
    owners = lax.axis_size("tp")
    latents = attend(query, cache, scales, lengths, owners)
    maps = stage(value_up, latents[0])
    values = exchange(project(exchange(latents), maps, query.shape[0]))
    returned = assemble(values)
    _, local_heads, requests, width = returned.shape
    returned = returned.reshape(owners * local_heads, requests, width)
    return jnp.swapaxes(returned, 0, 1).reshape(requests, owners * local_heads * width)


def solution(mesh):
    in_specs = (
        P(("grp", "tp"), None, None),
        P(("grp", "tp"), None, None),
        P(),
        P(("grp", "tp")),
        P("tp", None, None),
    )
    out_specs = P(("grp", "tp"), None)
    return jax.shard_map(
        on_device, mesh=mesh, in_specs=in_specs, out_specs=out_specs, check_vma=False
    )
```

```python
import functools
import itertools
import math

import jax
import jax.numpy as jnp
from jax import lax
from jax.experimental import pallas as pl
from jax.experimental.pallas import tpu as pltpu
from jax.sharding import PartitionSpec as P

ROPE_DIM = 64
SOFTMAX_SCALE = (1.0 + 0.1 * math.log(40.0)) ** 2 / math.sqrt(192.0)
EXP2_SCALE = SOFTMAX_SCALE * math.log2(math.e)
BLOCK = 512
LANES = 128
GROUP_ROWS = 16


def order(owners):
    return [0, owners - 1] + list(range(1, owners - 1))


def attend_kernel(owners, lengths_hbm, query_hbm, scales_hbm, cache, *refs):
    outs, refs = refs[:owners], refs[owners:]
    latents, lengths, query, scales, keys, scaled, sems, small_sems = refs
    requests, channels, heads = query.shape
    rows, rank = outs[0].shape
    cache_len = cache.shape[2]
    block = min(BLOCK, cache_len)
    blocks = cache_len // block
    me = lax.axis_index("tp")

    def fetch(r, b):
        span = pl.ds(b * block, block)
        return pltpu.make_async_copy(cache.at[r, :, span], keys.at[r, :, span], sems.at[r, b])

    first_copy = pltpu.make_async_copy(
        cache.at[:, :, pl.ds(0, block)], keys.at[:, :, pl.ds(0, block)], small_sems.at[3]
    )
    query_copy = pltpu.make_async_copy(query_hbm, query, small_sems.at[2])
    lengths_copy = pltpu.make_async_copy(lengths_hbm, lengths, small_sems.at[0])
    scales_copy = pltpu.make_async_copy(scales_hbm, scales, small_sems.at[1])
    for copy in (query_copy, first_copy, lengths_copy, scales_copy):
        copy.start()
    lengths_copy.wait()
    for r in range(requests):
        for b in range(1, blocks):
            @pl.when(b * block < lengths[r])
            def _():
                fetch(r, b).start()
    query_copy.wait()
    scales_copy.wait()
    scale_row = scales[...].reshape(1, channels)
    for r in range(requests):
        scaled[r] = (query[r].astype(jnp.float32).T * scale_row).astype(jnp.bfloat16)
    first_copy.wait()

    def score(r, b, live):
        if b:
            fetch(r, b).wait()
        span = slice(b * block, (b + 1) * block)
        part = jnp.dot(scaled[r], keys[r, :, span], preferred_element_type=jnp.float32)
        if b == live - 1:
            place = b * block + lax.broadcasted_iota(jnp.int32, part.shape, 1)
            part = jnp.where(place < lengths[r], part, -jnp.inf)
        return part

    def weigh(part, r, b):
        top = jnp.max(part, axis=1, keepdims=True)
        weight = jnp.exp2((part - top) * EXP2_SCALE)
        total = jnp.sum(weight, axis=1, keepdims=True)
        mixture = lax.dot_general(
            weight.astype(jnp.bfloat16), keys[r, :rank, b * block:(b + 1) * block],
            (((1,), (1,)), ((), ())), preferred_element_type=jnp.float32,
        )
        return top, total, mixture

    def merge(one, two):
        top = jnp.maximum(one[0], two[0])
        first = jnp.exp2((one[0] - top) * EXP2_SCALE)
        second = jnp.exp2((two[0] - top) * EXP2_SCALE)
        return (top,) + tuple(x * first + y * second for x, y in zip(one[1:], two[1:]))

    def finish(r, total, mixture):
        latent = mixture * (1.0 / total) * scale_row[:, :rank]
        for at in range(0, rank, LANES):
            latents[at // LANES, pl.ds(r, heads, stride=requests), :] = latent[:, at:at + LANES]

    def several(group, live):
        units = [(r, 0, n) for r, n in zip(group, live)]
        units += [(r, b, n) for r, n in zip(group, live) for b in range(1, n)]
        part = score(*units[0])
        state = {}
        for i, (r, b, n) in enumerate(units):
            ahead = score(*units[i + 1]) if i + 1 < len(units) else None
            done = weigh(part, r, b)
            state[r] = merge(state[r], done) if b else done
            if b == n - 1:
                finish(r, *state[r][1:])
            part = ahead

    for first in range(0, requests, 2):
        group = tuple(range(first, min(first + 2, requests)))
        count = [(lengths[r] + (block - 1)) // block for r in group]
        for live in itertools.product(range(1, blocks + 1), repeat=len(group)):
            @pl.when(functools.reduce(jnp.logical_and, [c == n for c, n in zip(count, live)]))
            def _():
                several(group, live)

    for out, k in zip(outs, order(owners)):
        mine = pl.ds(pl.multiple_of((me ^ k) * rows, rows), rows)
        for at in range(0, rank, LANES):
            out[:, at:at + LANES] = latents[at // LANES, mine, :].astype(jnp.bfloat16)


def in_hbm(*arrays):
    return [pltpu.with_memory_space_constraint(array, pltpu.HBM) for array in arrays]


def attend(query, cache, scales, lengths, owners):
    requests, heads, channels = query.shape
    cache_len = cache.shape[1]
    rank = channels - ROPE_DIM
    part = jax.ShapeDtypeStruct((heads // owners * requests, rank), jnp.bfloat16)
    return pl.pallas_call(
        functools.partial(attend_kernel, owners),
        out_shape=[part] * owners,
        in_specs=[pl.BlockSpec(memory_space=pl.ANY)] * 4,
        out_specs=[pl.BlockSpec(memory_space=pltpu.VMEM)] * owners,
        scratch_shapes=[
            pltpu.VMEM((rank // LANES, heads * requests, LANES), jnp.float32),
            pltpu.SMEM((requests,), jnp.int32),
            pltpu.VMEM((requests, channels, heads), jnp.bfloat16),
            pltpu.VMEM((channels,), jnp.float32),
            pltpu.VMEM((requests, channels, cache_len), jnp.bfloat16),
            pltpu.VMEM((requests, heads, channels), jnp.bfloat16),
            pltpu.SemaphoreType.DMA((requests, cache_len // min(BLOCK, cache_len))),
            pltpu.SemaphoreType.DMA((4,)),
        ],
        compiler_params=pltpu.CompilerParams(vmem_limit_bytes=24 * 2**20),
        cost_estimate=pl.CostEstimate(
            flops=4 * requests * heads * channels * cache_len,
            bytes_accessed=2 * requests * channels * cache_len,
            transcendentals=requests * heads * cache_len,
        ),
        name="attend",
    )(*in_hbm(lengths, jnp.swapaxes(query, 1, 2), scales, jnp.swapaxes(cache, 1, 2)))


def stage_kernel(maps_hbm, after, maps, sem):
    copy = pltpu.make_async_copy(maps_hbm, maps, sem)
    copy.start()
    copy.wait()


def stage(maps, after):
    return pl.pallas_call(
        stage_kernel,
        out_shape=jax.ShapeDtypeStruct(maps.shape, maps.dtype),
        in_specs=[pl.BlockSpec(memory_space=pl.ANY)] * 2,
        out_specs=pl.BlockSpec(memory_space=pltpu.VMEM),
        scratch_shapes=[pltpu.SemaphoreType.DMA(())],
        compiler_params=pltpu.CompilerParams(vmem_limit_bytes=8 * 2**20),
        cost_estimate=pl.CostEstimate(
            flops=0, bytes_accessed=4 * maps.size, transcendentals=0
        ),
        name="stage",
    )(*in_hbm(maps), after)


def project_kernel(count, *refs):
    parts, maps, outs = refs[:count], refs[count], refs[count + 1:]
    local_heads, requests, width = outs[0].shape
    group = min(GROUP_ROWS // requests, local_heads)
    rows = group * requests
    for first in range(0, local_heads, group):
        here = slice(first * requests, first * requests + rows)
        mixed = jnp.concatenate([part[here, :] for part in parts], axis=0)
        wide = jnp.concatenate([maps[first + i] for i in range(group)], axis=1)
        values = jnp.dot(mixed, wide, preferred_element_type=jnp.float32)
        head = lax.broadcasted_iota(jnp.int32, (rows, width), 0) // requests
        for d, out in enumerate(outs):
            block = values[d * rows:(d + 1) * rows]
            own = block[:, :width]
            for i in range(1, group):
                own = jnp.where(head == i, block[:, i * width:(i + 1) * width], own)
            out[first:first + group] = own.astype(jnp.bfloat16).reshape(group, requests, width)


def project(parts, maps, requests):
    count = len(parts)
    local_heads, rank, width = maps.shape
    return pl.pallas_call(
        functools.partial(project_kernel, count),
        out_shape=[jax.ShapeDtypeStruct((local_heads, requests, width), jnp.bfloat16)] * count,
        in_specs=[pl.BlockSpec(memory_space=pltpu.VMEM)] * (count + 1),
        out_specs=[pl.BlockSpec(memory_space=pltpu.VMEM)] * count,
        compiler_params=pltpu.CompilerParams(vmem_limit_bytes=24 * 2**20),
        cost_estimate=pl.CostEstimate(
            flops=2 * count * requests * local_heads * rank * width,
            bytes_accessed=2 * local_heads * rank * width,
            transcendentals=0,
        ),
        name="project",
    )(*parts, maps)


def assemble_kernel(owners, *refs):
    parts, out, sems = refs[:owners], refs[owners], refs[owners + 1]
    me = lax.axis_index("tp")
    copies = [
        pltpu.make_async_copy(part, out.at[me ^ k], sems.at[k])
        for k, part in zip(order(owners), parts)
    ]
    for copy in copies:
        copy.start()
    for copy in copies:
        copy.wait()


def assemble(parts):
    owners = len(parts)
    return pl.pallas_call(
        functools.partial(assemble_kernel, owners),
        out_shape=pltpu.HBM((owners,) + parts[0].shape, parts[0].dtype),
        in_specs=[pl.BlockSpec(memory_space=pltpu.VMEM)] * owners,
        out_specs=pl.BlockSpec(memory_space=pltpu.HBM),
        scratch_shapes=[pltpu.SemaphoreType.DMA((owners,))],
        compiler_params=pltpu.CompilerParams(vmem_limit_bytes=2 * 2**20),
        name="assemble",
    )(*parts)


def exchange(parts):
    owners = len(parts)
    groups = lax.axis_size("grp")
    flip = 1 - groups % 2

    def pairs(k):
        return [
            (g * owners + i, (g ^ flip) * owners + (i ^ k))
            for g in range(groups) for i in range(owners)
        ]

    return [
        lax.ppermute(part, ("grp", "tp"), pairs(k)) if k else part
        for k, part in zip(order(owners), parts)
    ]


def on_device(query, cache, scales, lengths, value_up):
    owners = lax.axis_size("tp")
    latents = attend(query, cache, scales, lengths, owners)
    maps = stage(value_up, latents[0])
    values = exchange(project(exchange(latents), maps, query.shape[0]))
    returned = assemble(values)
    _, local_heads, requests, width = returned.shape
    returned = returned.reshape(owners * local_heads, requests, width)
    return jnp.swapaxes(returned, 0, 1).reshape(requests, owners * local_heads * width)


def solution(mesh):
    in_specs = (
        P(("grp", "tp"), None, None),
        P(("grp", "tp"), None, None),
        P(),
        P(("grp", "tp")),
        P("tp", None, None),
    )
    out_specs = P(("grp", "tp"), None)
    return jax.shard_map(
        on_device, mesh=mesh, in_specs=in_specs, out_specs=out_specs, check_vma=False
    )
```

```python
import functools
import itertools
import math

import jax
import jax.numpy as jnp
from jax import lax
from jax.experimental import pallas as pl
from jax.experimental.pallas import tpu as pltpu
from jax.sharding import PartitionSpec as P

ROPE_DIM = 64
SOFTMAX_SCALE = (1.0 + 0.1 * math.log(40.0)) ** 2 / math.sqrt(192.0)
EXP2_SCALE = SOFTMAX_SCALE * math.log2(math.e)
BLOCK = 512
LANES = 128
GROUP_ROWS = 16


def order(owners):
    return [0, owners - 1] + list(range(1, owners - 1))


def attend_kernel(owners, lengths_hbm, query_hbm, scales_hbm, cache, *refs):
    outs, (latents, lengths, query, scales, keys, sems, small_sems) = refs[:owners], refs[owners:]
    requests, channels, heads = query.shape
    rows, rank = outs[0].shape
    cache_len = cache.shape[2]
    block = min(BLOCK, cache_len)
    blocks = cache_len // block
    me = lax.axis_index("tp")

    def fetch(r, b):
        span = pl.ds(b * block, block)
        return pltpu.make_async_copy(cache.at[r, :, span], keys.at[r, :, span], sems.at[r, b])

    lengths_copy = pltpu.make_async_copy(lengths_hbm, lengths, small_sems.at[0])
    scales_copy = pltpu.make_async_copy(scales_hbm, scales, small_sems.at[1])
    query_copy = pltpu.make_async_copy(query_hbm, query, small_sems.at[2])
    query_copy.start()
    fetch(0, 0).start()
    lengths_copy.start()
    scales_copy.start()
    for r in range(1, requests):
        fetch(r, 0).start()
    lengths_copy.wait()
    for r in range(requests):
        for b in range(1, blocks):
            @pl.when(b * block < lengths[r])
            def _():
                fetch(r, b).start()
    query_copy.wait()
    scales_copy.wait()
    scale_row = scales[...].reshape(1, channels)

    def scale(r):
        return (query[r].astype(jnp.float32).T * scale_row).astype(jnp.bfloat16)

    def score(scaled, r, b, live):
        if r not in scaled:
            scaled[r] = scale(r)
        fetch(r, b).wait()
        span = slice(b * block, (b + 1) * block)
        part = jnp.dot(scaled[r], keys[r, :, span], preferred_element_type=jnp.float32)
        if b == live - 1:
            place = b * block + lax.broadcasted_iota(jnp.int32, part.shape, 1)
            part = jnp.where(place < lengths[r], part, -jnp.inf)
        return part

    def weigh(part, r, b):
        top = jnp.max(part, axis=1, keepdims=True)
        weight = jnp.exp2((part - top) * EXP2_SCALE)
        total = jnp.sum(weight, axis=1, keepdims=True)
        mixture = lax.dot_general(
            weight.astype(jnp.bfloat16), keys[r, :rank, b * block:(b + 1) * block],
            (((1,), (1,)), ((), ())), preferred_element_type=jnp.float32,
        )
        return top, total, mixture

    def merge(one, two):
        top = jnp.maximum(one[0], two[0])
        first = jnp.exp2((one[0] - top) * EXP2_SCALE)
        second = jnp.exp2((two[0] - top) * EXP2_SCALE)
        return (top,) + tuple(x * first + y * second for x, y in zip(one[1:], two[1:]))

    def finish(r, total, mixture):
        latent = mixture * (1.0 / total) * scale_row[:, :rank]
        for at in range(0, rank, LANES):
            latents[at // LANES, pl.ds(r, heads, stride=requests), :] = latent[:, at:at + LANES]

    def several(group, live):
        scaled = {}
        units = [(r, 0, n) for r, n in zip(group, live)]
        units += [(r, b, n) for r, n in zip(group, live) for b in range(1, n)]
        part = score(scaled, *units[0])
        state = {}
        for i, (r, b, n) in enumerate(units):
            ahead = score(scaled, *units[i + 1]) if i + 1 < len(units) else None
            done = weigh(part, r, b)
            state[r] = merge(state[r], done) if b else done
            if b == n - 1:
                finish(r, *state[r][1:])
            part = ahead

    for first in range(0, requests, 2):
        group = tuple(range(first, min(first + 2, requests)))
        count = [(lengths[r] + (block - 1)) // block for r in group]
        for live in itertools.product(range(1, blocks + 1), repeat=len(group)):
            @pl.when(functools.reduce(jnp.logical_and, [c == n for c, n in zip(count, live)]))
            def _():
                several(group, live)

    for out, k in zip(outs, order(owners)):
        mine = pl.ds(pl.multiple_of((me ^ k) * rows, rows), rows)
        for at in range(0, rank, LANES):
            out[:, at:at + LANES] = latents[at // LANES, mine, :].astype(jnp.bfloat16)


def in_hbm(*arrays):
    return [pltpu.with_memory_space_constraint(array, pltpu.HBM) for array in arrays]


def attend(query, cache, scales, lengths, owners):
    requests, heads, channels = query.shape
    cache_len = cache.shape[1]
    rank = channels - ROPE_DIM
    part = jax.ShapeDtypeStruct((heads // owners * requests, rank), jnp.bfloat16)
    return pl.pallas_call(
        functools.partial(attend_kernel, owners),
        out_shape=[part] * owners,
        in_specs=[pl.BlockSpec(memory_space=pl.ANY)] * 4,
        out_specs=[pl.BlockSpec(memory_space=pltpu.VMEM)] * owners,
        scratch_shapes=[
            pltpu.VMEM((rank // LANES, heads * requests, LANES), jnp.float32),
            pltpu.SMEM((requests,), jnp.int32),
            pltpu.VMEM((requests, channels, heads), jnp.bfloat16),
            pltpu.VMEM((channels,), jnp.float32),
            pltpu.VMEM((requests, channels, cache_len), jnp.bfloat16),
            pltpu.SemaphoreType.DMA((requests, cache_len // min(BLOCK, cache_len))),
            pltpu.SemaphoreType.DMA((3,)),
        ],
        compiler_params=pltpu.CompilerParams(vmem_limit_bytes=24 * 2**20),
        cost_estimate=pl.CostEstimate(
            flops=4 * requests * heads * channels * cache_len,
            bytes_accessed=2 * requests * channels * cache_len,
            transcendentals=requests * heads * cache_len,
        ),
        name="attend",
    )(*in_hbm(lengths, jnp.swapaxes(query, 1, 2), scales, jnp.swapaxes(cache, 1, 2)))


def stage_kernel(maps_hbm, after, maps, sem):
    copy = pltpu.make_async_copy(maps_hbm, maps, sem)
    copy.start()
    copy.wait()


def stage(maps, after):
    return pl.pallas_call(
        stage_kernel,
        out_shape=jax.ShapeDtypeStruct(maps.shape, maps.dtype),
        in_specs=[pl.BlockSpec(memory_space=pl.ANY)] * 2,
        out_specs=pl.BlockSpec(memory_space=pltpu.VMEM),
        scratch_shapes=[pltpu.SemaphoreType.DMA(())],
        compiler_params=pltpu.CompilerParams(vmem_limit_bytes=8 * 2**20),
        cost_estimate=pl.CostEstimate(
            flops=0, bytes_accessed=4 * maps.size, transcendentals=0
        ),
        name="stage",
    )(*in_hbm(maps), after)


def project_kernel(count, *refs):
    parts, maps, outs = refs[:count], refs[count], refs[count + 1:]
    local_heads, requests, width = outs[0].shape
    group = min(GROUP_ROWS // requests, local_heads)
    rows = group * requests
    for first in range(0, local_heads, group):
        here = slice(first * requests, first * requests + rows)
        mixed = jnp.concatenate([part[here, :] for part in parts], axis=0)
        wide = jnp.concatenate([maps[first + i] for i in range(group)], axis=1)
        values = jnp.dot(mixed, wide, preferred_element_type=jnp.float32)
        head = lax.broadcasted_iota(jnp.int32, (rows, width), 0) // requests
        for d, out in enumerate(outs):
            block = values[d * rows:(d + 1) * rows]
            own = block[:, :width]
            for i in range(1, group):
                own = jnp.where(head == i, block[:, i * width:(i + 1) * width], own)
            out[first:first + group] = own.astype(jnp.bfloat16).reshape(group, requests, width)


def project(parts, maps, requests):
    count = len(parts)
    local_heads, rank, width = maps.shape
    return pl.pallas_call(
        functools.partial(project_kernel, count),
        out_shape=[jax.ShapeDtypeStruct((local_heads, requests, width), jnp.bfloat16)] * count,
        in_specs=[pl.BlockSpec(memory_space=pltpu.VMEM)] * (count + 1),
        out_specs=[pl.BlockSpec(memory_space=pltpu.VMEM)] * count,
        compiler_params=pltpu.CompilerParams(vmem_limit_bytes=24 * 2**20),
        cost_estimate=pl.CostEstimate(
            flops=2 * count * requests * local_heads * rank * width,
            bytes_accessed=2 * local_heads * rank * width,
            transcendentals=0,
        ),
        name="project",
    )(*parts, maps)


def assemble_kernel(owners, *refs):
    parts, out, sems = refs[:owners], refs[owners], refs[owners + 1]
    me = lax.axis_index("tp")
    copies = [
        pltpu.make_async_copy(part, out.at[me ^ k], sems.at[k])
        for k, part in zip(order(owners), parts)
    ]
    for copy in copies:
        copy.start()
    for copy in copies:
        copy.wait()


def assemble(parts):
    owners = len(parts)
    return pl.pallas_call(
        functools.partial(assemble_kernel, owners),
        out_shape=pltpu.HBM((owners,) + parts[0].shape, parts[0].dtype),
        in_specs=[pl.BlockSpec(memory_space=pltpu.VMEM)] * owners,
        out_specs=pl.BlockSpec(memory_space=pltpu.HBM),
        scratch_shapes=[pltpu.SemaphoreType.DMA((owners,))],
        compiler_params=pltpu.CompilerParams(vmem_limit_bytes=2 * 2**20),
        name="assemble",
    )(*parts)


def exchange(parts):
    owners = len(parts)
    groups = lax.axis_size("grp")
    flip = 1 - groups % 2

    def pairs(k):
        return [
            (g * owners + i, (g ^ flip) * owners + (i ^ k))
            for g in range(groups) for i in range(owners)
        ]

    return [
        lax.ppermute(part, ("grp", "tp"), pairs(k)) if k else part
        for k, part in zip(order(owners), parts)
    ]


def on_device(query, cache, scales, lengths, value_up):
    owners = lax.axis_size("tp")
    latents = attend(query, cache, scales, lengths, owners)
    maps = stage(value_up, latents[0])
    values = exchange(project(exchange(latents), maps, query.shape[0]))
    returned = assemble(values)
    _, local_heads, requests, width = returned.shape
    returned = returned.reshape(owners * local_heads, requests, width)
    return jnp.swapaxes(returned, 0, 1).reshape(requests, owners * local_heads * width)


def solution(mesh):
    in_specs = (
        P(("grp", "tp"), None, None),
        P(("grp", "tp"), None, None),
        P(),
        P(("grp", "tp")),
        P("tp", None, None),
    )
    out_specs = P(("grp", "tp"), None)
    return jax.shard_map(
        on_device, mesh=mesh, in_specs=in_specs, out_specs=out_specs, check_vma=False
    )
```

```python
import functools
import itertools
import math

import jax
import jax.numpy as jnp
from jax import lax
from jax.experimental import pallas as pl
from jax.experimental.pallas import tpu as pltpu
from jax.sharding import PartitionSpec as P

ROPE_DIM = 64
SOFTMAX_SCALE = (1.0 + 0.1 * math.log(40.0)) ** 2 / math.sqrt(192.0)
EXP2_SCALE = SOFTMAX_SCALE * math.log2(math.e)
BLOCK = 512
LANES = 128
GROUP_ROWS = 16


def order(owners):
    return [0, owners - 1] + list(range(1, owners - 1))


def attend_kernel(owners, lengths_hbm, query_hbm, scales_hbm, cache, *refs):
    outs, (latents, lengths, query, scales, keys, sems, small_sems) = refs[:owners], refs[owners:]
    requests, channels, heads = query.shape
    rows, rank = outs[0].shape
    cache_len = cache.shape[2]
    block = min(BLOCK, cache_len)
    blocks = cache_len // block
    me = lax.axis_index("tp")

    def fetch(r, b):
        span = pl.ds(b * block, block)
        return pltpu.make_async_copy(cache.at[r, :, span], keys.at[r, :, span], sems.at[r, b])

    lengths_copy = pltpu.make_async_copy(lengths_hbm, lengths, small_sems.at[0])
    scales_copy = pltpu.make_async_copy(scales_hbm, scales, small_sems.at[1])
    query_copy = pltpu.make_async_copy(query_hbm, query, small_sems.at[2])
    lengths_copy.start()
    query_copy.start()
    scales_copy.start()
    for r in range(requests):
        fetch(r, 0).start()
    lengths_copy.wait()
    for r in range(requests):
        for b in range(1, blocks):
            @pl.when(b * block < lengths[r])
            def _():
                fetch(r, b).start()
    query_copy.wait()
    scales_copy.wait()
    scale_row = scales[...].reshape(1, channels)

    def scale(r):
        return (query[r].astype(jnp.float32).T * scale_row).astype(jnp.bfloat16)

    def score(scaled, r, b, live):
        if r not in scaled:
            scaled[r] = scale(r)
        fetch(r, b).wait()
        span = slice(b * block, (b + 1) * block)
        part = jnp.dot(scaled[r], keys[r, :, span], preferred_element_type=jnp.float32)
        if b == live - 1:
            place = b * block + lax.broadcasted_iota(jnp.int32, part.shape, 1)
            part = jnp.where(place < lengths[r], part, -jnp.inf)
        return part

    def weigh(part, r, b):
        top = jnp.max(part, axis=1, keepdims=True)
        weight = jnp.exp2((part - top) * EXP2_SCALE)
        total = jnp.sum(weight, axis=1, keepdims=True)
        mixture = lax.dot_general(
            weight.astype(jnp.bfloat16), keys[r, :rank, b * block:(b + 1) * block],
            (((1,), (1,)), ((), ())), preferred_element_type=jnp.float32,
        )
        return top, total, mixture

    def merge(one, two):
        top = jnp.maximum(one[0], two[0])
        first = jnp.exp2((one[0] - top) * EXP2_SCALE)
        second = jnp.exp2((two[0] - top) * EXP2_SCALE)
        return (top,) + tuple(x * first + y * second for x, y in zip(one[1:], two[1:]))

    def finish(r, total, mixture):
        latent = mixture * (1.0 / total) * scale_row[:, :rank]
        for at in range(0, rank, LANES):
            latents[at // LANES, pl.ds(r, heads, stride=requests), :] = latent[:, at:at + LANES]

    def several(group, live):
        scaled = {}
        units = [(r, 0, n) for r, n in zip(group, live)]
        units += [(r, b, n) for r, n in zip(group, live) for b in range(1, n)]
        part = score(scaled, *units[0])
        state = {}
        for i, (r, b, n) in enumerate(units):
            ahead = score(scaled, *units[i + 1]) if i + 1 < len(units) else None
            done = weigh(part, r, b)
            state[r] = merge(state[r], done) if b else done
            if b == n - 1:
                finish(r, *state[r][1:])
            part = ahead

    for first in range(0, requests, 2):
        group = tuple(range(first, min(first + 2, requests)))
        count = [(lengths[r] + (block - 1)) // block for r in group]
        for live in itertools.product(range(1, blocks + 1), repeat=len(group)):
            @pl.when(functools.reduce(jnp.logical_and, [c == n for c, n in zip(count, live)]))
            def _():
                several(group, live)

    for out, k in zip(outs, order(owners)):
        mine = pl.ds(pl.multiple_of((me ^ k) * rows, rows), rows)
        for at in range(0, rank, LANES):
            out[:, at:at + LANES] = latents[at // LANES, mine, :].astype(jnp.bfloat16)


def in_hbm(*arrays):
    return [pltpu.with_memory_space_constraint(array, pltpu.HBM) for array in arrays]


def attend(query, cache, scales, lengths, owners):
    requests, heads, channels = query.shape
    cache_len = cache.shape[1]
    rank = channels - ROPE_DIM
    part = jax.ShapeDtypeStruct((heads // owners * requests, rank), jnp.bfloat16)
    return pl.pallas_call(
        functools.partial(attend_kernel, owners),
        out_shape=[part] * owners,
        in_specs=[pl.BlockSpec(memory_space=pl.ANY)] * 4,
        out_specs=[pl.BlockSpec(memory_space=pltpu.VMEM)] * owners,
        scratch_shapes=[
            pltpu.VMEM((rank // LANES, heads * requests, LANES), jnp.float32),
            pltpu.SMEM((requests,), jnp.int32),
            pltpu.VMEM((requests, channels, heads), jnp.bfloat16),
            pltpu.VMEM((channels,), jnp.float32),
            pltpu.VMEM((requests, channels, cache_len), jnp.bfloat16),
            pltpu.SemaphoreType.DMA((requests, cache_len // min(BLOCK, cache_len))),
            pltpu.SemaphoreType.DMA((3,)),
        ],
        compiler_params=pltpu.CompilerParams(vmem_limit_bytes=24 * 2**20),
        cost_estimate=pl.CostEstimate(
            flops=4 * requests * heads * channels * cache_len,
            bytes_accessed=2 * requests * channels * cache_len,
            transcendentals=requests * heads * cache_len,
        ),
        name="attend",
    )(*in_hbm(lengths, jnp.swapaxes(query, 1, 2), scales, jnp.swapaxes(cache, 1, 2)))


def stage_kernel(maps_hbm, after, maps, sem):
    copy = pltpu.make_async_copy(maps_hbm, maps, sem)
    copy.start()
    copy.wait()


def stage(maps, after):
    return pl.pallas_call(
        stage_kernel,
        out_shape=jax.ShapeDtypeStruct(maps.shape, maps.dtype),
        in_specs=[pl.BlockSpec(memory_space=pl.ANY)] * 2,
        out_specs=pl.BlockSpec(memory_space=pltpu.VMEM),
        scratch_shapes=[pltpu.SemaphoreType.DMA(())],
        compiler_params=pltpu.CompilerParams(vmem_limit_bytes=8 * 2**20),
        cost_estimate=pl.CostEstimate(
            flops=0, bytes_accessed=4 * maps.size, transcendentals=0
        ),
        name="stage",
    )(*in_hbm(maps), after)


def project_kernel(count, *refs):
    parts, maps, outs = refs[:count], refs[count], refs[count + 1:]
    local_heads, width = maps.shape[0], maps.shape[2]
    requests = outs[0].shape[0] // local_heads
    group = min(GROUP_ROWS // requests, local_heads)
    rows = group * requests
    for first in range(0, local_heads, group):
        here = slice(first * requests, first * requests + rows)
        mixed = jnp.concatenate([part[here, :] for part in parts], axis=0)
        wide = jnp.concatenate([maps[first + i] for i in range(group)], axis=1)
        values = jnp.dot(mixed, wide, preferred_element_type=jnp.float32)
        head = lax.broadcasted_iota(jnp.int32, (rows, width), 0) // requests
        for d, out in enumerate(outs):
            block = values[d * rows:(d + 1) * rows]
            own = block[:, :width]
            for i in range(1, group):
                own = jnp.where(head == i, block[:, i * width:(i + 1) * width], own)
            out[here, :] = own.astype(jnp.bfloat16)


def project(parts, maps, requests):
    count = len(parts)
    local_heads, rank, width = maps.shape
    return pl.pallas_call(
        functools.partial(project_kernel, count),
        out_shape=[jax.ShapeDtypeStruct((local_heads * requests, width), jnp.bfloat16)] * count,
        in_specs=[pl.BlockSpec(memory_space=pltpu.VMEM)] * (count + 1),
        out_specs=[pl.BlockSpec(memory_space=pltpu.VMEM)] * count,
        compiler_params=pltpu.CompilerParams(vmem_limit_bytes=24 * 2**20),
        cost_estimate=pl.CostEstimate(
            flops=2 * count * requests * local_heads * rank * width,
            bytes_accessed=2 * local_heads * rank * width,
            transcendentals=0,
        ),
        name="project",
    )(*parts, maps)


def assemble_kernel(owners, *refs):
    parts, (out, blocks, sem) = refs[:owners], refs[owners:]
    me = lax.axis_index("tp")
    for k, part in zip(order(owners), parts):
        blocks[me ^ k] = part[...].reshape(blocks.shape[1:])
    copy = pltpu.make_async_copy(blocks, out, sem)
    copy.start()
    copy.wait()


def assemble(parts, requests):
    owners = len(parts)
    rows, width = parts[0].shape
    shape = (owners, rows // requests, requests, width)
    return pl.pallas_call(
        functools.partial(assemble_kernel, owners),
        out_shape=pltpu.HBM(shape, parts[0].dtype),
        in_specs=[pl.BlockSpec(memory_space=pltpu.VMEM)] * owners,
        out_specs=pl.BlockSpec(memory_space=pltpu.HBM),
        scratch_shapes=[pltpu.VMEM(shape, parts[0].dtype), pltpu.SemaphoreType.DMA(())],
        compiler_params=pltpu.CompilerParams(vmem_limit_bytes=2 * 2**20),
        name="assemble",
    )(*parts)


def exchange(parts):
    owners = len(parts)
    groups = lax.axis_size("grp")
    flip = 1 - groups % 2

    def pairs(k):
        return [
            (g * owners + i, (g ^ flip) * owners + (i ^ k))
            for g in range(groups) for i in range(owners)
        ]

    return [
        lax.ppermute(part, ("grp", "tp"), pairs(k)) if k else part
        for k, part in zip(order(owners), parts)
    ]


def on_device(query, cache, scales, lengths, value_up):
    owners = lax.axis_size("tp")
    latents = attend(query, cache, scales, lengths, owners)
    maps = stage(value_up, latents[0])
    values = exchange(project(exchange(latents), maps, query.shape[0]))
    returned = assemble(values, query.shape[0])
    _, local_heads, requests, width = returned.shape
    returned = returned.reshape(owners * local_heads, requests, width)
    return jnp.swapaxes(returned, 0, 1).reshape(requests, owners * local_heads * width)


def solution(mesh):
    in_specs = (
        P(("grp", "tp"), None, None),
        P(("grp", "tp"), None, None),
        P(),
        P(("grp", "tp")),
        P("tp", None, None),
    )
    out_specs = P(("grp", "tp"), None)
    return jax.shard_map(
        on_device, mesh=mesh, in_specs=in_specs, out_specs=out_specs, check_vma=False
    )
```

```python
import functools
import itertools
import math

import jax
import jax.numpy as jnp
from jax import lax
from jax.experimental import pallas as pl
from jax.experimental.pallas import tpu as pltpu
from jax.sharding import PartitionSpec as P

ROPE_DIM = 64
SOFTMAX_SCALE = (1.0 + 0.1 * math.log(40.0)) ** 2 / math.sqrt(192.0)
EXP2_SCALE = SOFTMAX_SCALE * math.log2(math.e)
BLOCK = 512
LANES = 128
GROUP_ROWS = 16


def order(owners):
    return [0, owners - 1] + list(range(1, owners - 1))


def attend_kernel(owners, lengths_hbm, query_hbm, scales_hbm, cache, *refs):
    outs, (latents, lengths, query, scales, keys, sems, small_sems) = refs[:owners], refs[owners:]
    requests, channels, heads = query.shape
    rows, rank = outs[0].shape
    cache_len = cache.shape[2]
    block = min(BLOCK, cache_len)
    blocks = cache_len // block
    me = lax.axis_index("tp")

    def fetch(r, b):
        span = pl.ds(b * block, block)
        return pltpu.make_async_copy(cache.at[r, :, span], keys.at[r, :, span], sems.at[r, b])

    lengths_copy = pltpu.make_async_copy(lengths_hbm, lengths, small_sems.at[0])
    scales_copy = pltpu.make_async_copy(scales_hbm, scales, small_sems.at[1])
    query_copy = pltpu.make_async_copy(query_hbm, query, small_sems.at[2])
    lengths_copy.start()
    query_copy.start()
    scales_copy.start()
    for r in range(requests):
        fetch(r, 0).start()
    lengths_copy.wait()
    def fetch_from(r, b):
        if b < blocks:
            @pl.when(b * block < lengths[r])
            def _():
                fetch(r, b).start()
                fetch_from(r, b + 1)

    for r in range(requests):
        fetch_from(r, 1)
    query_copy.wait()
    scales_copy.wait()
    scale_row = scales[...].reshape(1, channels)

    def scale(r):
        return (query[r].astype(jnp.float32).T * scale_row).astype(jnp.bfloat16)

    def score(scaled, r, b, live):
        if r not in scaled:
            scaled[r] = scale(r)
        fetch(r, b).wait()
        span = slice(b * block, (b + 1) * block)
        part = jnp.dot(scaled[r], keys[r, :, span], preferred_element_type=jnp.float32)
        if b == live - 1:
            place = b * block + lax.broadcasted_iota(jnp.int32, part.shape, 1)
            part = jnp.where(place < lengths[r], part, -jnp.inf)
        return part

    def weigh(part, r, b):
        top = jnp.max(part, axis=1, keepdims=True)
        weight = jnp.exp2((part - top) * EXP2_SCALE)
        total = jnp.sum(weight, axis=1, keepdims=True)
        mixture = lax.dot_general(
            weight.astype(jnp.bfloat16), keys[r, :rank, b * block:(b + 1) * block],
            (((1,), (1,)), ((), ())), preferred_element_type=jnp.float32,
        )
        return top, total, mixture

    def merge(one, two):
        top = jnp.maximum(one[0], two[0])
        first = jnp.exp2((one[0] - top) * EXP2_SCALE)
        second = jnp.exp2((two[0] - top) * EXP2_SCALE)
        return (top,) + tuple(x * first + y * second for x, y in zip(one[1:], two[1:]))

    def finish(r, total, mixture):
        latent = mixture * (1.0 / total) * scale_row[:, :rank]
        for at in range(0, rank, LANES):
            latents[at // LANES, pl.ds(r, heads, stride=requests), :] = latent[:, at:at + LANES]

    def several(group, live):
        scaled = {}
        units = [(r, 0, n) for r, n in zip(group, live)]
        units += [(r, b, n) for r, n in zip(group, live) for b in range(1, n)]
        part = score(scaled, *units[0])
        state = {}
        for i, (r, b, n) in enumerate(units):
            ahead = score(scaled, *units[i + 1]) if i + 1 < len(units) else None
            done = weigh(part, r, b)
            state[r] = merge(state[r], done) if b else done
            if b == n - 1:
                finish(r, *state[r][1:])
            part = ahead

    for first in range(0, requests, 2):
        group = tuple(range(first, min(first + 2, requests)))
        count = [(lengths[r] + (block - 1)) // block for r in group]
        for live in itertools.product(range(1, blocks + 1), repeat=len(group)):
            @pl.when(functools.reduce(jnp.logical_and, [c == n for c, n in zip(count, live)]))
            def _():
                several(group, live)

    for out, k in zip(outs, order(owners)):
        mine = pl.ds(pl.multiple_of((me ^ k) * rows, rows), rows)
        for at in range(0, rank, LANES):
            out[:, at:at + LANES] = latents[at // LANES, mine, :].astype(jnp.bfloat16)


def in_hbm(*arrays):
    return [pltpu.with_memory_space_constraint(array, pltpu.HBM) for array in arrays]


def attend(query, cache, scales, lengths, owners):
    requests, heads, channels = query.shape
    cache_len = cache.shape[1]
    rank = channels - ROPE_DIM
    part = jax.ShapeDtypeStruct((heads // owners * requests, rank), jnp.bfloat16)
    return pl.pallas_call(
        functools.partial(attend_kernel, owners),
        out_shape=[part] * owners,
        in_specs=[pl.BlockSpec(memory_space=pl.ANY)] * 4,
        out_specs=[pl.BlockSpec(memory_space=pltpu.VMEM)] * owners,
        scratch_shapes=[
            pltpu.VMEM((rank // LANES, heads * requests, LANES), jnp.float32),
            pltpu.SMEM((requests,), jnp.int32),
            pltpu.VMEM((requests, channels, heads), jnp.bfloat16),
            pltpu.VMEM((channels,), jnp.float32),
            pltpu.VMEM((requests, channels, cache_len), jnp.bfloat16),
            pltpu.SemaphoreType.DMA((requests, cache_len // min(BLOCK, cache_len))),
            pltpu.SemaphoreType.DMA((3,)),
        ],
        compiler_params=pltpu.CompilerParams(vmem_limit_bytes=24 * 2**20),
        cost_estimate=pl.CostEstimate(
            flops=4 * requests * heads * channels * cache_len,
            bytes_accessed=2 * requests * channels * cache_len,
            transcendentals=requests * heads * cache_len,
        ),
        name="attend",
    )(*in_hbm(lengths, jnp.swapaxes(query, 1, 2), scales, jnp.swapaxes(cache, 1, 2)))


def stage_kernel(maps_hbm, after, maps, sem):
    copy = pltpu.make_async_copy(maps_hbm, maps, sem)
    copy.start()
    copy.wait()


def stage(maps, after):
    return pl.pallas_call(
        stage_kernel,
        out_shape=jax.ShapeDtypeStruct(maps.shape, maps.dtype),
        in_specs=[pl.BlockSpec(memory_space=pl.ANY)] * 2,
        out_specs=pl.BlockSpec(memory_space=pltpu.VMEM),
        scratch_shapes=[pltpu.SemaphoreType.DMA(())],
        compiler_params=pltpu.CompilerParams(vmem_limit_bytes=8 * 2**20),
        cost_estimate=pl.CostEstimate(
            flops=0, bytes_accessed=4 * maps.size, transcendentals=0
        ),
        name="stage",
    )(*in_hbm(maps), after)


def project_kernel(count, *refs):
    parts, maps, outs = refs[:count], refs[count], refs[count + 1:]
    local_heads, requests, width = outs[0].shape
    group = min(GROUP_ROWS // requests, local_heads)
    rows = group * requests
    for first in range(0, local_heads, group):
        here = slice(first * requests, first * requests + rows)
        mixed = jnp.concatenate([part[here, :] for part in parts], axis=0)
        wide = jnp.concatenate([maps[first + i] for i in range(group)], axis=1)
        values = jnp.dot(mixed, wide, preferred_element_type=jnp.float32)
        head = lax.broadcasted_iota(jnp.int32, (rows, width), 0) // requests
        for d, out in enumerate(outs):
            block = values[d * rows:(d + 1) * rows]
            own = block[:, :width]
            for i in range(1, group):
                own = jnp.where(head == i, block[:, i * width:(i + 1) * width], own)
            out[first:first + group] = own.astype(jnp.bfloat16).reshape(group, requests, width)


def project(parts, maps, requests):
    count = len(parts)
    local_heads, rank, width = maps.shape
    return pl.pallas_call(
        functools.partial(project_kernel, count),
        out_shape=[jax.ShapeDtypeStruct((local_heads, requests, width), jnp.bfloat16)] * count,
        in_specs=[pl.BlockSpec(memory_space=pltpu.VMEM)] * (count + 1),
        out_specs=[pl.BlockSpec(memory_space=pltpu.VMEM)] * count,
        compiler_params=pltpu.CompilerParams(vmem_limit_bytes=24 * 2**20),
        cost_estimate=pl.CostEstimate(
            flops=2 * count * requests * local_heads * rank * width,
            bytes_accessed=2 * local_heads * rank * width,
            transcendentals=0,
        ),
        name="project",
    )(*parts, maps)


def assemble_kernel(owners, *refs):
    parts, out, sems = refs[:owners], refs[owners], refs[owners + 1]
    me = lax.axis_index("tp")
    copies = [
        pltpu.make_async_copy(part, out.at[me ^ k], sems.at[k])
        for k, part in zip(order(owners), parts)
    ]
    for copy in copies:
        copy.start()
    for copy in copies:
        copy.wait()


def assemble(parts):
    owners = len(parts)
    return pl.pallas_call(
        functools.partial(assemble_kernel, owners),
        out_shape=pltpu.HBM((owners,) + parts[0].shape, parts[0].dtype),
        in_specs=[pl.BlockSpec(memory_space=pltpu.VMEM)] * owners,
        out_specs=pl.BlockSpec(memory_space=pltpu.HBM),
        scratch_shapes=[pltpu.SemaphoreType.DMA((owners,))],
        compiler_params=pltpu.CompilerParams(vmem_limit_bytes=2 * 2**20),
        name="assemble",
    )(*parts)


def exchange(parts):
    owners = len(parts)
    groups = lax.axis_size("grp")
    flip = 1 - groups % 2

    def pairs(k):
        return [
            (g * owners + i, (g ^ flip) * owners + (i ^ k))
            for g in range(groups) for i in range(owners)
        ]

    return [
        lax.ppermute(part, ("grp", "tp"), pairs(k)) if k else part
        for k, part in zip(order(owners), parts)
    ]


def on_device(query, cache, scales, lengths, value_up):
    owners = lax.axis_size("tp")
    latents = attend(query, cache, scales, lengths, owners)
    maps = stage(value_up, latents[0])
    values = exchange(project(exchange(latents), maps, query.shape[0]))
    returned = assemble(values)
    _, local_heads, requests, width = returned.shape
    returned = returned.reshape(owners * local_heads, requests, width)
    return jnp.swapaxes(returned, 0, 1).reshape(requests, owners * local_heads * width)


def solution(mesh):
    in_specs = (
        P(("grp", "tp"), None, None),
        P(("grp", "tp"), None, None),
        P(),
        P(("grp", "tp")),
        P("tp", None, None),
    )
    out_specs = P(("grp", "tp"), None)
    return jax.shard_map(
        on_device, mesh=mesh, in_specs=in_specs, out_specs=out_specs, check_vma=False
    )
```

```python
import functools
import itertools
import math

import jax
import jax.numpy as jnp
from jax import lax
from jax.experimental import pallas as pl
from jax.experimental.pallas import tpu as pltpu
from jax.sharding import PartitionSpec as P

ROPE_DIM = 64
SOFTMAX_SCALE = (1.0 + 0.1 * math.log(40.0)) ** 2 / math.sqrt(192.0)
EXP2_SCALE = SOFTMAX_SCALE * math.log2(math.e)
BLOCK = 512
LANES = 128
GROUP_ROWS = 16


def order(owners):
    return [0, owners - 1] + list(range(1, owners - 1))


def attend_kernel(owners, lengths_hbm, query_hbm, scales_hbm, cache, *refs):
    outs, (latents, lengths, query, scales, keys, sems, small_sems) = refs[:owners], refs[owners:]
    requests, channels, heads = query.shape
    rows, rank = outs[0].shape
    cache_len = cache.shape[2]
    block = min(BLOCK, cache_len)
    blocks = cache_len // block
    me = lax.axis_index("tp")

    def fetch(r, b):
        span = pl.ds(b * block, block)
        return pltpu.make_async_copy(cache.at[r, :, span], keys.at[r, :, span], sems.at[r, b])

    lengths_copy = pltpu.make_async_copy(lengths_hbm, lengths, small_sems.at[0])
    scales_copy = pltpu.make_async_copy(scales_hbm, scales, small_sems.at[1])
    query_copy = pltpu.make_async_copy(query_hbm, query, small_sems.at[2])
    lengths_copy.start()
    query_copy.start()
    scales_copy.start()
    for r in range(requests):
        fetch(r, 0).start()
    lengths_copy.wait()
    for r in range(requests):
        for b in range(1, blocks):
            @pl.when(b * block < lengths[r])
            def _():
                fetch(r, b).start()
    query_copy.wait()
    scales_copy.wait()
    scale_row = scales[...].reshape(1, channels)

    def scale(r):
        return (query[r].astype(jnp.float32).T * scale_row).astype(jnp.bfloat16)

    def score(scaled, r, b, live):
        if r not in scaled:
            scaled[r] = scale(r)
        fetch(r, b).wait()
        span = slice(b * block, (b + 1) * block)
        part = jnp.dot(scaled[r], keys[r, :, span], preferred_element_type=jnp.float32)
        if b == live - 1:
            place = b * block + lax.broadcasted_iota(jnp.int32, part.shape, 1)
            part = jnp.where(place < lengths[r], part, -jnp.inf)
        return part

    def weigh(part, r, b, before):
        top = jnp.max(part, axis=1, keepdims=True)
        if before is not None:
            top = jnp.maximum(top, before[0])
        weight = jnp.exp2((part - top) * EXP2_SCALE)
        total = jnp.sum(weight, axis=1, keepdims=True)
        mixture = lax.dot_general(
            weight.astype(jnp.bfloat16), keys[r, :rank, b * block:(b + 1) * block],
            (((1,), (1,)), ((), ())), preferred_element_type=jnp.float32,
        )
        if before is not None:
            fade = jnp.exp2((before[0] - top) * EXP2_SCALE)
            total, mixture = before[1] * fade + total, before[2] * fade + mixture
        return top, total, mixture

    def finish(r, total, mixture):
        latent = mixture * (1.0 / total) * scale_row[:, :rank]
        for at in range(0, rank, LANES):
            latents[at // LANES, pl.ds(r, heads, stride=requests), :] = latent[:, at:at + LANES]

    def several(group, live):
        scaled = {}
        units = [(r, 0, n) for r, n in zip(group, live)]
        units += [(r, b, n) for r, n in zip(group, live) for b in range(1, n)]
        part = score(scaled, *units[0])
        state = {}
        for i, (r, b, n) in enumerate(units):
            ahead = score(scaled, *units[i + 1]) if i + 1 < len(units) else None
            state[r] = weigh(part, r, b, state.get(r))
            if b == n - 1:
                finish(r, *state[r][1:])
            part = ahead

    for first in range(0, requests, 2):
        group = tuple(range(first, min(first + 2, requests)))
        count = [(lengths[r] + (block - 1)) // block for r in group]
        for live in itertools.product(range(1, blocks + 1), repeat=len(group)):
            @pl.when(functools.reduce(jnp.logical_and, [c == n for c, n in zip(count, live)]))
            def _():
                several(group, live)

    for out, k in zip(outs, order(owners)):
        mine = pl.ds(pl.multiple_of((me ^ k) * rows, rows), rows)
        for at in range(0, rank, LANES):
            out[:, at:at + LANES] = latents[at // LANES, mine, :].astype(jnp.bfloat16)


def in_hbm(*arrays):
    return [pltpu.with_memory_space_constraint(array, pltpu.HBM) for array in arrays]


def attend(query, cache, scales, lengths, owners):
    requests, heads, channels = query.shape
    cache_len = cache.shape[1]
    rank = channels - ROPE_DIM
    part = jax.ShapeDtypeStruct((heads // owners * requests, rank), jnp.bfloat16)
    return pl.pallas_call(
        functools.partial(attend_kernel, owners),
        out_shape=[part] * owners,
        in_specs=[pl.BlockSpec(memory_space=pl.ANY)] * 4,
        out_specs=[pl.BlockSpec(memory_space=pltpu.VMEM)] * owners,
        scratch_shapes=[
            pltpu.VMEM((rank // LANES, heads * requests, LANES), jnp.float32),
            pltpu.SMEM((requests,), jnp.int32),
            pltpu.VMEM((requests, channels, heads), jnp.bfloat16),
            pltpu.VMEM((channels,), jnp.float32),
            pltpu.VMEM((requests, channels, cache_len), jnp.bfloat16),
            pltpu.SemaphoreType.DMA((requests, cache_len // min(BLOCK, cache_len))),
            pltpu.SemaphoreType.DMA((3,)),
        ],
        compiler_params=pltpu.CompilerParams(vmem_limit_bytes=24 * 2**20),
        cost_estimate=pl.CostEstimate(
            flops=4 * requests * heads * channels * cache_len,
            bytes_accessed=2 * requests * channels * cache_len,
            transcendentals=requests * heads * cache_len,
        ),
        name="attend",
    )(*in_hbm(lengths, jnp.swapaxes(query, 1, 2), scales, jnp.swapaxes(cache, 1, 2)))


def stage_kernel(maps_hbm, after, maps, sem):
    copy = pltpu.make_async_copy(maps_hbm, maps, sem)
    copy.start()
    copy.wait()


def stage(maps, after):
    return pl.pallas_call(
        stage_kernel,
        out_shape=jax.ShapeDtypeStruct(maps.shape, maps.dtype),
        in_specs=[pl.BlockSpec(memory_space=pl.ANY)] * 2,
        out_specs=pl.BlockSpec(memory_space=pltpu.VMEM),
        scratch_shapes=[pltpu.SemaphoreType.DMA(())],
        compiler_params=pltpu.CompilerParams(vmem_limit_bytes=8 * 2**20),
        cost_estimate=pl.CostEstimate(
            flops=0, bytes_accessed=4 * maps.size, transcendentals=0
        ),
        name="stage",
    )(*in_hbm(maps), after)


def project_kernel(count, *refs):
    parts, maps, outs = refs[:count], refs[count], refs[count + 1:]
    local_heads, requests, width = outs[0].shape
    group = min(GROUP_ROWS // requests, local_heads)
    rows = group * requests
    for first in range(0, local_heads, group):
        here = slice(first * requests, first * requests + rows)
        mixed = jnp.concatenate([part[here, :] for part in parts], axis=0)
        wide = jnp.concatenate([maps[first + i] for i in range(group)], axis=1)
        values = jnp.dot(mixed, wide, preferred_element_type=jnp.float32)
        head = lax.broadcasted_iota(jnp.int32, (rows, width), 0) // requests
        for d, out in enumerate(outs):
            block = values[d * rows:(d + 1) * rows]
            own = block[:, :width]
            for i in range(1, group):
                own = jnp.where(head == i, block[:, i * width:(i + 1) * width], own)
            out[first:first + group] = own.astype(jnp.bfloat16).reshape(group, requests, width)


def project(parts, maps, requests):
    count = len(parts)
    local_heads, rank, width = maps.shape
    return pl.pallas_call(
        functools.partial(project_kernel, count),
        out_shape=[jax.ShapeDtypeStruct((local_heads, requests, width), jnp.bfloat16)] * count,
        in_specs=[pl.BlockSpec(memory_space=pltpu.VMEM)] * (count + 1),
        out_specs=[pl.BlockSpec(memory_space=pltpu.VMEM)] * count,
        compiler_params=pltpu.CompilerParams(vmem_limit_bytes=24 * 2**20),
        cost_estimate=pl.CostEstimate(
            flops=2 * count * requests * local_heads * rank * width,
            bytes_accessed=2 * local_heads * rank * width,
            transcendentals=0,
        ),
        name="project",
    )(*parts, maps)


def assemble_kernel(owners, *refs):
    parts, out, sems = refs[:owners], refs[owners], refs[owners + 1]
    me = lax.axis_index("tp")
    copies = [
        pltpu.make_async_copy(part, out.at[me ^ k], sems.at[k])
        for k, part in zip(order(owners), parts)
    ]
    for copy in copies:
        copy.start()
    for copy in copies:
        copy.wait()


def assemble(parts):
    owners = len(parts)
    return pl.pallas_call(
        functools.partial(assemble_kernel, owners),
        out_shape=pltpu.HBM((owners,) + parts[0].shape, parts[0].dtype),
        in_specs=[pl.BlockSpec(memory_space=pltpu.VMEM)] * owners,
        out_specs=pl.BlockSpec(memory_space=pltpu.HBM),
        scratch_shapes=[pltpu.SemaphoreType.DMA((owners,))],
        compiler_params=pltpu.CompilerParams(vmem_limit_bytes=2 * 2**20),
        name="assemble",
    )(*parts)


def exchange(parts):
    owners = len(parts)
    groups = lax.axis_size("grp")
    flip = 1 - groups % 2

    def pairs(k):
        return [
            (g * owners + i, (g ^ flip) * owners + (i ^ k))
            for g in range(groups) for i in range(owners)
        ]

    return [
        lax.ppermute(part, ("grp", "tp"), pairs(k)) if k else part
        for k, part in zip(order(owners), parts)
    ]


def on_device(query, cache, scales, lengths, value_up):
    owners = lax.axis_size("tp")
    latents = attend(query, cache, scales, lengths, owners)
    maps = stage(value_up, latents[0])
    values = exchange(project(exchange(latents), maps, query.shape[0]))
    returned = assemble(values)
    _, local_heads, requests, width = returned.shape
    returned = returned.reshape(owners * local_heads, requests, width)
    return jnp.swapaxes(returned, 0, 1).reshape(requests, owners * local_heads * width)


def solution(mesh):
    in_specs = (
        P(("grp", "tp"), None, None),
        P(("grp", "tp"), None, None),
        P(),
        P(("grp", "tp")),
        P("tp", None, None),
    )
    out_specs = P(("grp", "tp"), None)
    return jax.shard_map(
        on_device, mesh=mesh, in_specs=in_specs, out_specs=out_specs, check_vma=False
    )
```
